32 devices in a mesh: dp: 16 (over z, y, core), tensor: 2 (over x).
Axes of the slice: x: 2, y: 2, z: 4, core: 2. Of those that a mesh axis runs over, the one named last changes fastest.
Arguments:
- hidden_in: bfloat16 [16384, 1024], P(('dp', 'tensor')), may hold values from -6 to 6
- memory: bfloat16 [16384, 1024], P(('dp', 'tensor')), may hold values from -6 to 6
- in_proj: bfloat16 [2, 3, 1024, 1024], P(None, None, 'tensor'), may hold values from -0.1875 to 0.1875
- in_bias: float32 [2, 2, 1024], P(None, None, 'tensor'), may hold values from -1.8 to 1.8
- out_proj: bfloat16 [2, 1024, 1024], P(None, 'tensor'), may hold values from -1.5 to 1.5
- ffn_up: bfloat16 [4096, 1024], P('tensor'), may hold values from -0.1875 to 0.1875
- ffn_up_bias: float32 [4096], P('tensor'), may hold values from -1.8 to 1.8
- ffn_down: bfloat16 [4096, 1024], P('tensor'), may hold values from -0.09375 to 0.09375
- out_bias: float32 [3, 1024], replicated, may hold values from -1.8 to 1.8
- norm_gain: float32 [3, 1024], replicated, may hold values from 0.5 to 1.5
- norm_bias: float32 [3, 1024], replicated, may hold values from -1.8 to 1.8
- out_grad: bfloat16 [16384, 1024], P(('dp', 'tensor')), may hold values from -6 to 6
- target_len: int32 [16], replicated, may hold values from 1 to 1024, 10240 in all
- source_len: int32 [16], replicated, may hold values from 1 to 1024, 10240 in all
- assignment: int32 [16], P('dp'), may hold values from 0 to 15, each once
Outputs:
- hidden_out: bfloat16 [16384, 1024], P(('dp', 'tensor'))
- hidden_grad: float32 [16384, 1024], P(('dp', 'tensor'))
- memory_grad: float32 [16384, 1024], P(('dp', 'tensor'))
- in_proj_grad: float32 [2, 3, 1024, 1024], P(None, None, 'tensor', 'dp')
- out_proj_grad: float32 [2, 1024, 1024], P(None, 'tensor', 'dp')
- ffn_up_grad: float32 [4096, 1024], P('tensor', 'dp')
- ffn_down_grad: float32 [4096, 1024], P('tensor', 'dp')
- in_bias_grad: float32 [2, 2, 1024], replicated
- ffn_up_bias_grad: float32 [4096], replicated
- out_bias_grad: float32 [3, 1024], replicated
- norm_gain_grad: float32 [3, 1024], replicated
- norm_bias_grad: float32 [3, 1024], replicated
The draws below stay inside these ranges and needn't reach their ends.
Inputs may be any that keep to these rules, and one draw needn't show every extreme that they name: `target_len`: each row's target length; the longest is 1024. `source_len`: each row's memory length; the longest is 1024. `assignment`: a permutation of the 16 rows.
All inputs are finite; a program needn't handle non-finite values.
Results may differ from the reference program's by a relative error of at most 0.018.
Values may be sent and summed in bfloat16 or wider, within the bound.
No kernel may reach another device: no remote copies, remote signals or barrier semaphores. Data moves between devices by JAX's collectives and lax.ppermute only.
A program may use at most 320 MiB of HBM per device.

```python
import math
import jax
import jax.numpy as jnp
import numpy as np
from jax import lax

D = 1024
HEADS = 16
HEAD_DIM = 64
FF = 4096
LEN = 1024
SRC = 1024
ROWS = 16
TOKENS = 16384
MEM_TOKENS = 16384


def with_spikes(entries, own_key, source, target, blocks, factor):
    owner, partner = [(jnp.arange(entries.shape[position]) // (entries.shape[position] // blocks)).reshape([-1 if axis == position else 1 for axis in range(entries.ndim)]) for position in (source, target)]
    chosen = jax.random.permutation(own_key, blocks)[partner]
    strong = (owner == chosen) | (owner == (partner + blocks // 2) % blocks)
    return jnp.where(strong, factor * entries, entries)


def level_of(key, dims, split, low, top_value):
    gain, own = 1.0, jax.random.fold_in(key, 6)
    for axis_at, parts in split:
        draws = jnp.exp(jax.random.uniform(jax.random.fold_in(own, axis_at), (parts,), jnp.float32, low / len(split), top_value / len(split)))
        gain = gain * jnp.repeat(draws, dims[axis_at] // parts).reshape([-1 if axis == axis_at else 1 for axis in range(len(dims))])
    return gain


def split_up(count, total, bound, skew):
    weights = [(1 << 20) // math.isqrt(standing ** skew) + 1 for standing in range(2, count + 1)]
    rest, counts = total - bound - (count - 1), [1] * (count - 1)
    while rest > 0:
        free = [i for i in range(count - 1) if counts[i] < bound]
        whole, left = sum([weights[i] for i in free]), rest
        for i in free:
            more = min(bound - counts[i], max(1, left * weights[i] // whole), rest)
            counts[i] = counts[i] + more
            rest = rest - more
    return np.array([bound] + counts)


def uneven_parts(key, number_of, total, reach, lean):
    if number_of == 2:
        one = jax.random.randint(key, (), max(1, total - reach), min(reach, total - 1) + 1)
        return jnp.stack([one, total - one])
    tallies = jnp.asarray(split_up(number_of, total, reach, lean), jnp.int32)
    pairs = (number_of - 1) // 2
    giver, receiver = tallies[1:1 + 2 * pairs:2], tallies[2:2 + 2 * pairs:2]
    slack = jnp.minimum(giver - 1, reach - receiver)
    shifted = jax.random.randint(jax.random.fold_in(key, 1), (pairs,), 0, 1 << 20) % (slack + 1)
    tallies = tallies.at[1:1 + 2 * pairs:2].set(giver - shifted).at[2:2 + 2 * pairs:2].set(receiver + shifted)
    return tallies[jax.random.permutation(jax.random.fold_in(key, 2), number_of)]


def normal_values(stream_key, extent, scale, bound, pieces=(), kind=jnp.bfloat16):
    array = jax.random.normal(stream_key, extent, jnp.float32) * scale
    if len(pieces) > 0:
        array = level_of(stream_key, extent, pieces, -0.22, 0.18) * array
    return jnp.clip(array, min=-bound, max=bound).astype(kind)


def bell_draw_with(stream_key, dims, spread, most, pieces, heavy, kind=jnp.bfloat16):
    drawn = spread * jax.random.normal(stream_key, dims, jnp.float32)
    if pieces:
        drawn = drawn * level_of(stream_key, dims, pieces, -0.22, 0.18)
    return jnp.clip(with_spikes(drawn, jax.random.fold_in(stream_key, 3), *heavy), -most, most).astype(kind)


def setup_inputs(seed: int = 0) -> dict:
    splits = jax.random.split(jax.random.key(seed), 16)
    hidden_in = normal_values(splits[0], (TOKENS, D), 1.0, 6.0, ((0, 32),))
    memory = normal_values(splits[1], (MEM_TOKENS, D), 1.0, 6.0, ((0, 32),))
    in_proj = normal_values(splits[2], (2, 3, D, D), D ** -0.5, 0.1875, ((2, 2),))
    in_bias = normal_values(splits[3], (2, 2, D), 0.3, 1.8, ((2, 2),), jnp.float32)
    out_proj = normal_values(splits[4], (2, D, D), (max(D // 64, 1)) ** -0.5, 1.5, ((1, 2),))
    ffn_up = normal_values(splits[5], (FF, D), D ** -0.5, 0.1875, ((0, 2),))
    ffn_up_bias = normal_values(splits[6], (FF,), 0.3, 1.8, ((0, 2),), jnp.float32)
    ffn_down = normal_values(splits[7], (FF, D), FF ** -0.5, 0.09375, ((0, 2),))
    out_bias = normal_values(splits[8], (3, D), 0.3, 1.8, (), jnp.float32)
    norm_gain = jnp.clip(1.0 + 0.1 * jax.random.normal(splits[9], (3, D), jnp.float32), 0.5, 1.5)
    norm_bias = normal_values(splits[10], (3, D), 0.3, 1.8, (), jnp.float32)
    out_grad = bell_draw_with(splits[11], (TOKENS, D), 1.0, 6.0, ((0, 32),), (0, 1, 32, 2.75))
    target_len = uneven_parts(splits[12], ROWS, ROWS * LEN * 5 // 8, LEN, 2).astype(jnp.int32)
    source_len = uneven_parts(splits[13], ROWS, ROWS * SRC * 5 // 8, SRC, 2).astype(jnp.int32)
    assignment = jax.random.permutation(splits[14], ROWS).astype(jnp.int32)
    return dict(hidden_in=hidden_in, memory=memory, in_proj=in_proj, in_bias=in_bias, out_proj=out_proj, ffn_up=ffn_up, ffn_up_bias=ffn_up_bias, ffn_down=ffn_down, out_bias=out_bias, norm_gain=norm_gain, norm_bias=norm_bias, out_grad=out_grad, target_len=target_len, source_len=source_len, assignment=assignment)


@jax.custom_vjp
def low(v):
    return lax.optimization_barrier(v.astype(jnp.bfloat16)).astype(jnp.float32)

@jax.custom_vjp
def low_back(v):
    return v

def low_keep(v):
    return (low(v), None)

def low_pass(kept, grad):
    return (grad,)

def back_keep(v):
    return (v, None)

def back_low(kept, grad):
    return (low(grad),)
low.defvjp(low_keep, low_pass)
low_back.defvjp(back_keep, back_low)

def norm_rows(values, gain_row, shift_row):
    centred = values - lax.optimization_barrier(jnp.mean(values, axis=-1, keepdims=True))
    inverse = lax.rsqrt(lax.optimization_barrier(jnp.mean(centred * centred, axis=-1, keepdims=True)) + jnp.asarray(1e-05, values.dtype))
    return centred * inverse * gain_row + shift_row

def project(matrix, weight):
    return jnp.einsum('nd,fd->nf', matrix, weight, precision=lax.Precision.HIGHEST)

def apply_right(matrix, weight):
    return jnp.dot(matrix, weight, precision=lax.Precision.HIGHEST)

def attend_one(query, keys, values, allowed):
    score_scale = jnp.asarray(1.0 / math.sqrt(HEAD_DIM), query.dtype)
    raw_scores = jnp.einsum('qhe,khe->hqk', query, keys, precision=lax.Precision.HIGHEST)
    scores = low_back(raw_scores * score_scale)
    masked = jnp.where(allowed[None], scores, jnp.asarray(-1e+30, scores.dtype))
    row_max = lax.optimization_barrier(jnp.max(masked, axis=-1, keepdims=True))
    exp_scores = jnp.exp(masked - row_max)
    row_total = lax.optimization_barrier(jnp.sum(exp_scores, axis=-1, keepdims=True))
    attn_probs = exp_scores / row_total
    return jnp.einsum('hqk,khe->qhe', low(attn_probs), values, precision=lax.Precision.HIGHEST)

def attend_rows(query, keys, values, lengths, causal):
    row_count = lengths.shape[0]
    query_rows = query.reshape(row_count, -1, HEADS, HEAD_DIM)
    key_rows = keys.reshape(row_count, -1, HEADS, HEAD_DIM)
    value_rows = values.reshape(row_count, -1, HEADS, HEAD_DIM)

    def one_row(packed):
        query_part, key_part, value_part, length = packed
        key_pos = jnp.arange(key_part.shape[0], dtype=jnp.int32)[None, :]
        allowed = jnp.broadcast_to(key_pos < length.astype(jnp.int32), (query_part.shape[0], key_part.shape[0]))
        if causal:
            query_pos = jnp.arange(query_part.shape[0], dtype=jnp.int32)[:, None]
            allowed = allowed & (key_pos <= query_pos)
        return attend_one(query_part, key_part, value_part, allowed)
    mixed = lax.map(jax.checkpoint(one_row), (query_rows, key_rows, value_rows, lengths.astype(jnp.int32)))
    return mixed.reshape(query.shape[0], HEADS * HEAD_DIM)

def decoder_layer(parameters, hidden, memory, target_lengths, source_lengths):
    in_proj, in_bias, out_proj, ffn_up, ffn_up_bias, ffn_down, out_bias, norm_gain, norm_bias = parameters
    normed_one = low(norm_rows(hidden, norm_gain[0], norm_bias[0]))
    query_one = low_back(low(project(normed_one, in_proj[0, 0]) + in_bias[0, 0]))
    key_one = low_back(low(project(normed_one, in_proj[0, 1])))
    value_one = low_back(low(project(normed_one, in_proj[0, 2]) + in_bias[0, 1]))
    mixed_one = low_back(low(attend_rows(query_one, key_one, value_one, target_lengths, True)))
    stream_one = hidden + low_back(apply_right(mixed_one, out_proj[0])) + out_bias[0]
    normed_two = low(norm_rows(stream_one, norm_gain[1], norm_bias[1]))
    query_two = low_back(low(project(normed_two, in_proj[1, 0]) + in_bias[1, 0]))
    key_two = low_back(low(project(memory, in_proj[1, 1])))
    value_two = low_back(low(project(memory, in_proj[1, 2]) + in_bias[1, 1]))
    mixed_two = low_back(low(attend_rows(query_two, key_two, value_two, source_lengths, False)))
    stream_two = stream_one + low_back(apply_right(mixed_two, out_proj[1])) + out_bias[1]
    normed_three = low(norm_rows(stream_two, norm_gain[2], norm_bias[2]))
    pre_active = low_back(project(normed_three, ffn_up) + ffn_up_bias)
    active = low_back(low(jax.nn.gelu(pre_active, approximate=False)))
    return stream_two + low_back(apply_right(active, ffn_down)) + out_bias[2]

def reference(hidden_in, memory, in_proj, in_bias, out_proj, ffn_up, ffn_up_bias, ffn_down, out_bias, norm_gain, norm_bias, out_grad, target_len, source_len, assignment):
    parameters = tuple((weight.astype(jnp.float32) for weight in (in_proj, in_bias, out_proj, ffn_up, ffn_up_bias, ffn_down, out_bias, norm_gain, norm_bias)))
    slot_index = assignment.astype(jnp.int32)
    total_rows = assignment.shape[0]
    row_ids = jnp.arange(total_rows, dtype=jnp.int32)
    owner = slot_index[:, None] == row_ids[None, :]
    slot_target = lax.optimization_barrier(jnp.sum(jnp.where(owner, target_len.astype(jnp.int32)[None, :], jnp.int32(0)), axis=1)).astype(jnp.int32)
    slot_source = lax.optimization_barrier(jnp.sum(jnp.where(owner, source_len.astype(jnp.int32)[None, :], jnp.int32(0)), axis=1)).astype(jnp.int32)
    group_rows = math.gcd(total_rows, max(1, 4096 // LEN))
    group_count = total_rows // group_rows
    float_type = parameters[0].dtype
    hidden_groups = hidden_in.astype(jnp.float32).reshape(group_count, group_rows * LEN, D)
    memory_groups = memory.astype(jnp.float32).reshape(group_count, group_rows * SRC, D)
    cotangents = out_grad.astype(jnp.float32).reshape(group_count, group_rows * LEN, D)
    target_groups = slot_target.reshape(group_count, group_rows).astype(jnp.int32)
    source_groups = slot_source.reshape(group_count, group_rows).astype(jnp.int32)

    def scan_step(running, packed):
        hidden_part, memory_part, cotangent, target_part, source_part = packed

        def apply_layer(params_now, hidden_now, memory_now):
            return decoder_layer(params_now, hidden_now, memory_now, target_part, source_part)
        result, pullback = jax.vjp(apply_layer, parameters, hidden_part, memory_part)
        grad_params, grad_hidden, grad_memory = pullback(cotangent.astype(result.dtype))
        running = tuple((total + part.astype(total.dtype) for total, part in zip(running, grad_params)))
        return (running, (result.astype(float_type), grad_hidden.astype(float_type), grad_memory.astype(float_type)))
    zero_grads = tuple((jnp.zeros(weight.shape, float_type) for weight in parameters))
    param_grads, (outputs, hidden_grads, memory_grads) = lax.scan(scan_step, zero_grads, (hidden_groups, memory_groups, cotangents, target_groups, source_groups))
    return (outputs.reshape(-1, D).astype(jnp.bfloat16), hidden_grads.reshape(-1, D), memory_grads.reshape(-1, D), param_grads[0], param_grads[2], param_grads[3], param_grads[5], param_grads[1], param_grads[4], param_grads[6], param_grads[7], param_grads[8])
```

```python
import functools

import jax
import jax.numpy as jnp
from jax import lax
from jax.experimental import pallas as pl
from jax.experimental.pallas import tpu as pltpu
from jax.sharding import PartitionSpec as P

HEAD_DIM = 64
F32 = jnp.float32
BF = jnp.bfloat16
NT = (((1,), (1,)), ((), ()))
TN = (((0,), (0,)), ((), ()))
NN = (((1,), (0,)), ((), ()))

epsilon = 1e-05
masked_score = -1e30
root_half = 0.7071067811865476
normal_peak = 0.3989422804014327
score_scale = HEAD_DIM ** (-0.5)


def mm(left, right, dims=NN):
    return lax.dot_general(left, right, dims, preferred_element_type=F32)


def three_parts(values):
    top = values.astype(BF).astype(F32)
    rest = values - top
    middle = rest.astype(BF).astype(F32)
    return top, middle, rest - middle


def attend_kernel(causal, step, len_ref, q_ref, k_ref, v_ref, o_ref, sum_ref):
    length = len_ref[0]
    rows, keys = q_ref.shape[0], k_ref.shape[0]
    lane = lax.broadcasted_iota(jnp.int32, (1, 128), 1)
    key_pos = lax.broadcasted_iota(jnp.int32, (keys, 1), 0)
    bias = jnp.where(key_pos < length, 0.0, masked_score)
    q = q_ref[...].astype(F32) * score_scale
    k = k_ref[...].astype(F32)
    v = v_ref[...].astype(F32)
    sides = []
    for head in range(2):
        own = (lane < 64) if head == 0 else (lane >= 64)
        first = lane == (64 if head == 0 else 0)
        q_wide = jnp.where(own, q, jnp.where(first, 1.0, 0.0)).astype(BF)
        k_wide = jnp.where(own, k, jnp.where(first, bias, 0.0)).astype(BF)
        v_wide = jnp.where(own, v, 1.0).astype(BF)
        sides.append((q_wide, k_wide, v_wide))
    for block in range(rows // step):
        here = slice(block * step, (block + 1) * step)
        reach = (block + 1) * step if causal else keys
        parts = []
        for head in range(2):
            q_wide, k_wide, v_wide = sides[head]
            scores = mm(q_wide[here], k_wide[:reach], NT)
            if causal:
                below = lax.broadcasted_iota(jnp.int32, (step, step), 1) <= lax.broadcasted_iota(
                    jnp.int32, (step, step), 0
                )
                edge = jnp.where(below, scores[:, reach - step :], masked_score)
                if block == 0:
                    scores = edge
                else:
                    scores = jnp.concatenate([scores[:, : reach - step], edge], axis=1)
            top = jnp.max(scores, axis=1, keepdims=True)
            weights = jnp.exp(scores - top).astype(BF)
            mixed = mm(weights, v_wide[:reach])
            total = mixed[:, 64:65] if head == 0 else mixed[:, 0:1]
            parts.append((mixed / total, top + jnp.log(total)))
        o_ref[here, :] = jnp.where(lane < 64, parts[0][0], parts[1][0]).astype(BF)
        sum_ref[here, :] = jnp.where(lane < 64, parts[0][1], parts[1][1])


def attend_back_kernel(
    causal, step, len_ref, q_ref, k_ref, v_ref, g_ref, o_ref, sum_ref,
    dq_ref, dk_ref, dv_ref, acc_ref,
):
    length = len_ref[0]
    rows, keys = q_ref.shape[0], k_ref.shape[0]
    lane = lax.broadcasted_iota(jnp.int32, (1, 128), 1)
    key_pos = lax.broadcasted_iota(jnp.int32, (keys, 1), 0)
    bias = jnp.where(key_pos < length, 0.0, masked_score)
    q = q_ref[...].astype(F32) * score_scale
    k = k_ref[...].astype(F32)
    v = v_ref[...].astype(F32)
    g = g_ref[...].astype(F32)
    overlap = g * o_ref[...].astype(F32)
    log_sums = sum_ref[...]
    sides = []
    for head in range(2):
        own = (lane < 64) if head == 0 else (lane >= 64)
        base = 64 if head == 0 else 0
        at = [lane == base + i for i in range(4)]
        minus = jnp.where(at[1] | at[2] | at[3], -1.0, 0.0)
        delta = jnp.sum(jnp.where(own, overlap, 0.0), axis=1, keepdims=True)
        log_sum = log_sums[:, 0:1] if head == 0 else log_sums[:, 64:65]
        s0, s1, s2 = three_parts(log_sum)
        d0, d1, d2 = three_parts(delta)
        extra_q = jnp.where(
            at[0], 1.0, jnp.where(at[1], s0, jnp.where(at[2], s1, jnp.where(at[3], s2, 0.0)))
        )
        extra_g = jnp.where(at[1], d0, jnp.where(at[2], d1, jnp.where(at[3], d2, 0.0)))
        q_wide = jnp.where(own, q, extra_q).astype(BF)
        k_wide = jnp.where(own, k, jnp.where(at[0], bias, minus)).astype(BF)
        g_wide = jnp.where(own, g, extra_g).astype(BF)
        v_wide = jnp.where(own, v, minus).astype(BF)
        sides.append((q_wide, k_wide, g_wide, v_wide))
    for block in range(keys // step):
        here = slice(block * step, (block + 1) * step)
        low = block * step if causal else 0
        dks = []
        dvs = []
        for head in range(2):
            q_wide, k_wide, g_wide, v_wide = sides[head]
            scores = mm(k_wide[here], q_wide[low:], NT)
            if causal:
                below = lax.broadcasted_iota(jnp.int32, (step, step), 0) <= lax.broadcasted_iota(
                    jnp.int32, (step, step), 1
                )
                edge = jnp.where(below, scores[:, :step], masked_score)
                if low + step == rows:
                    scores = edge
                else:
                    scores = jnp.concatenate([edge, scores[:, step:]], axis=1)
            probs = jnp.exp(scores)
            grads = (probs * mm(v_wide[here], g_wide[low:], NT)).astype(BF)
            dvs.append(mm(probs.astype(BF), g_wide[low:]))
            dks.append(mm(grads, q_wide[low:]))
            dq = mm(grads, k_wide[here], TN)
            if block == 0:
                acc_ref[head] = dq
            else:
                acc_ref[head, low:, :] += dq
        dv_ref[here, :] = jnp.where(lane < 64, dvs[0], dvs[1]).astype(BF)
        dk_ref[here, :] = jnp.where(lane < 64, dks[0], dks[1]).astype(BF)
    dq_ref[...] = (jnp.where(lane < 64, acc_ref[0], acc_ref[1]) * score_scale).astype(BF)


def pair_spec(rows):
    return pl.BlockSpec((rows, 128), lambda i: (0, i))


def attend(q, k, v, length, causal):
    rows, width = q.shape
    keys = k.shape[0]
    return pl.pallas_call(
        functools.partial(attend_kernel, causal, 256),
        grid=(width // 128,),
        in_specs=[
            pl.BlockSpec(memory_space=pltpu.SMEM),
            pair_spec(rows),
            pair_spec(keys),
            pair_spec(keys),
        ],
        out_specs=[pair_spec(rows), pair_spec(rows)],
        out_shape=[
            jax.ShapeDtypeStruct((rows, width), BF),
            jax.ShapeDtypeStruct((rows, width), F32),
        ],
        compiler_params=pltpu.CompilerParams(vmem_limit_bytes=40 << 20),
        cost_estimate=pl.CostEstimate(
            flops=16 * rows * keys * width,
            bytes_accessed=8 * rows * width,
            transcendentals=rows * keys * width // 64,
        ),
    )(length, q, k, v)


def attend_back(q, k, v, grad, out, sums, length, causal):
    rows, width = q.shape
    keys = k.shape[0]
    return pl.pallas_call(
        functools.partial(attend_back_kernel, causal, 256),
        grid=(width // 128,),
        in_specs=[
            pl.BlockSpec(memory_space=pltpu.SMEM),
            pair_spec(rows),
            pair_spec(keys),
            pair_spec(keys),
            pair_spec(rows),
            pair_spec(rows),
            pair_spec(rows),
        ],
        out_specs=[pair_spec(rows), pair_spec(keys), pair_spec(keys)],
        out_shape=[
            jax.ShapeDtypeStruct((rows, width), BF),
            jax.ShapeDtypeStruct((keys, width), BF),
            jax.ShapeDtypeStruct((keys, width), BF),
        ],
        scratch_shapes=[pltpu.VMEM((2, rows, 128), F32)],
        compiler_params=pltpu.CompilerParams(vmem_limit_bytes=40 << 20),
        cost_estimate=pl.CostEstimate(
            flops=40 * rows * keys * width,
            bytes_accessed=16 * rows * width,
            transcendentals=rows * keys * width // 64,
        ),
    )(length, q, k, v, grad, out, sums)


def normalize(values, gain_row, shift_row):
    centred = values - jnp.mean(values, axis=-1, keepdims=True)
    inverse = lax.rsqrt(jnp.mean(centred * centred, axis=-1, keepdims=True) + epsilon)
    unit_rows = centred * inverse
    return ((unit_rows * gain_row + shift_row).astype(BF), unit_rows, inverse)


def normalize_back(gradient, unit_rows, inverse, gain_row):
    scaled = gradient * gain_row
    return inverse * (
        scaled
        - jnp.mean(scaled, axis=-1, keepdims=True)
        - unit_rows * jnp.mean(scaled * unit_rows, axis=-1, keepdims=True)
    )


def gelu_parts(values):
    below = 0.5 * (1.0 + lax.erf(values * root_half))
    slope = below + values * jnp.exp(-0.5 * values * values) * normal_peak
    return (values * below).astype(BF), slope


def take(array, index, axis=0):
    return lax.dynamic_index_in_dim(array, index, axis, keepdims=False)


def make_shards(mesh):
    dp_size = mesh.shape["dp"]
    bits = dp_size.bit_length() - 1

    def shards(
        hidden_in, memory, in_proj, in_bias, out_proj, ffn_up, ffn_up_bias, ffn_down, out_bias,
        norm_gain, norm_bias, out_grad, target_len, source_len, assignment,
    ):
        dp = lax.axis_index("dp")
        side = lax.axis_index("tensor")
        core = dp & 1
        bit = [(dp >> i) & 1 for i in range(bits)]

        def over(array, i):
            return lax.ppermute(array, "dp", [(d, d ^ (1 << i)) for d in range(dp_size)])

        def across(array):
            return lax.ppermute(array, "tensor", [(0, 1), (1, 0)])

        def slot_swap(array):
            pairs = []
            for j in range(dp_size // 2):
                pairs += [(4 * j + 1, 4 * j + 2), (4 * j + 2, 4 * j + 1)]
            got = lax.ppermute(array, ("dp", "tensor"), pairs)
            return got

        def to_row(array):
            got = slot_swap(array)
            return jnp.where(core == side, array, got)

        def from_row(array):
            got = slot_swap(array.astype(BF))
            return jnp.where(core == side, array, got.astype(array.dtype))

        def whole_row(half):
            other = over(half, 0)
            return jnp.concatenate(
                [jnp.where(core == 0, half, other), jnp.where(core == 0, other, half)], axis=0
            )

        def core_sum(part):
            return part + over(part.astype(BF), 0).astype(F32)

        def half_of(array, index):
            return take(array.reshape(2, array.shape[0] // 2, -1), index)

        def core_scatter(part):
            other = over(half_of(part, 1 - core).astype(BF), 0)
            return half_of(part, core) + other.astype(F32)

        own_row = jnp.broadcast_to(assignment.reshape(1, 1).astype(F32), (8, 128))
        held = jnp.where(core == side, own_row, over(own_row, 0))[0, 0].astype(jnp.int32)
        row_ids = lax.iota(jnp.int32, target_len.shape[0])
        target_length = jnp.sum(jnp.where(row_ids == held, target_len, 0)).reshape(1)
        source_length = jnp.sum(jnp.where(row_ids == held, source_len, 0)).reshape(1)

        hidden_half = to_row(hidden_in)
        hidden_row = whole_row(hidden_half)

        def quarter(array, axis):
            shape = array.shape
            split = shape[:axis] + (2, shape[axis] // 2) + shape[axis + 1 :]
            return take(array.reshape(split), core, axis)

        def fetch(part, axis):
            shape = part.shape
            split = shape[:axis] + (4, shape[axis] // 4) + shape[axis + 1 :]
            pieces = part.reshape(split)
            place = bit[1] + 2 * bit[2]
            first = across(take(pieces, place, axis))
            by_y = over(first, 1)
            by_z = over(first, 2)
            cut = first.shape[-1] // 2
            last = jnp.concatenate(
                [over(by_y[..., :cut], 2), over(by_z[..., cut:], 1)], axis=-1
            )
            out = jnp.zeros(split, part.dtype)
            for piece, spot in ((first, place), (by_y, place ^ 1), (by_z, place ^ 2), (last, place ^ 3)):
                out = lax.dynamic_update_slice_in_dim(out, jnp.expand_dims(piece, axis), spot, axis)
            return out.reshape(shape)

        def both(part, axis):
            return jnp.concatenate([part, fetch(part, axis)], axis=axis)

        bias_part = jnp.concatenate(
            [quarter(in_bias, 2).reshape(-1), quarter(ffn_up_bias, 0)], axis=0
        )
        far_bias = across(bias_part)
        head_part = in_bias.shape[2] // 2
        in_bias_own = jnp.concatenate(
            [
                bias_part[: 4 * head_part].reshape(2, 2, head_part),
                far_bias[: 4 * head_part].reshape(2, 2, head_part),
            ],
            axis=2,
        )
        up_bias_own = jnp.concatenate([bias_part[4 * head_part :], far_bias[4 * head_part :]])

        in_quarter = quarter(in_proj, 2)
        w_self = both(in_quarter[0], 1)
        memory_row = whole_row(to_row(memory))
        w_cross = both(in_quarter[1], 1)
        w_out = both(quarter(out_proj, 1), 1)
        w_up = both(quarter(ffn_up, 0), 0)
        w_down = both(quarter(ffn_down, 0), 0)
        grad_half = to_row(out_grad)
        grad_row = whole_row(grad_half)

        stream_zero = hidden_row.astype(F32)
        rows_one, unit_one, inverse_one = normalize(stream_zero, norm_gain[0], norm_bias[0])
        query_one = (mm(rows_one, w_self[0], NT) + in_bias_own[0, 0]).astype(BF)
        key_one = mm(rows_one, w_self[1], NT).astype(BF)
        value_one = (mm(rows_one, w_self[2], NT) + in_bias_own[0, 1]).astype(BF)
        mixed_one, sums_one = attend(query_one, key_one, value_one, target_length, True)
        stream_one = stream_zero + core_sum(mm(mixed_one, w_out[0])) + out_bias[0]

        rows_two, unit_two, inverse_two = normalize(stream_one, norm_gain[1], norm_bias[1])
        key_two = mm(memory_row, w_cross[1], NT).astype(BF)
        value_two = (mm(memory_row, w_cross[2], NT) + in_bias_own[1, 1]).astype(BF)
        query_two = (mm(rows_two, w_cross[0], NT) + in_bias_own[1, 0]).astype(BF)
        mixed_two, sums_two = attend(query_two, key_two, value_two, source_length, False)
        stream_two = stream_one + core_sum(mm(mixed_two, w_out[1])) + out_bias[1]

        rows_three, unit_three, inverse_three = normalize(stream_two, norm_gain[2], norm_bias[2])
        active, slope = gelu_parts(mm(rows_three, w_up, NT) + up_bias_own)
        hidden_out = from_row(
            (half_of(stream_two, core) + core_scatter(mm(active, w_down)) + out_bias[2]).astype(BF)
        )

        def reduce_grad(rows_mat, cols_mat):
            count, kinds, _, width = cols_mat.shape
            there = cols_mat[:, :, 1].reshape(count, kinds * width)
            here = cols_mat[:, :, 0].reshape(count, kinds * width)
            arrived = across(mm(rows_mat, there, TN).astype(BF))
            kept = mm(rows_mat, here, TN) + arrived.astype(F32)
            kept = kept.reshape((2,) * bits + (-1, kinds * width))
            done = []
            for i in range(1, bits):
                axis = bits - 1 - i - sum(1 for j in done if j > i)
                arrived = over(take(kept, 1 - bit[i], axis).astype(BF), i)
                kept = take(kept, bit[i], axis) + arrived.astype(F32)
                done.append(i)
            arrived = over(take(kept, 1 - core), 0)
            kept = take(kept, core)
            first = jnp.where(core == 0, kept, arrived).reshape(-1, kinds, width)
            second = jnp.where(core == 0, arrived, kept).reshape(-1, kinds, width)
            total = jnp.concatenate([first, second], axis=2)
            return jnp.transpose(total, (1, 2, 0))

        def parted(array):
            return array.reshape(array.shape[0], 1, 2, -1)

        down_share = reduce_grad(grad_row, parted(active))[0]
        grad_active = mm(grad_row, w_down, NT).astype(BF)
        grad_pre = (grad_active.astype(F32) * slope).astype(BF)
        up_share = reduce_grad(rows_three, parted(grad_pre))[0]
        back_three = core_sum(mm(grad_pre, w_up))
        grad_two = grad_row.astype(F32) + normalize_back(
            back_three, unit_three, inverse_three, norm_gain[2]
        )

        down_two = grad_two.astype(BF)
        out_share_two = reduce_grad(down_two, parted(mixed_two))
        grad_mixed_two = mm(down_two, w_out[1], NT).astype(BF)
        dq_two, dk_two, dv_two = attend_back(
            query_two, key_two, value_two, grad_mixed_two, mixed_two, sums_two, source_length, False
        )
        q_share_two = reduce_grad(rows_two, parted(dq_two))
        kv_share_two = reduce_grad(memory_row, jnp.stack([dk_two, dv_two], axis=1).reshape(dk_two.shape[0], 2, 2, -1))
        memory_grad = from_row(core_scatter(mm(dk_two, w_cross[1]) + mm(dv_two, w_cross[2])))
        back_two = core_sum(mm(dq_two, w_cross[0]))
        grad_one = grad_two + normalize_back(back_two, unit_two, inverse_two, norm_gain[1])

        down_one = grad_one.astype(BF)
        out_share_one = reduce_grad(down_one, parted(mixed_one))
        grad_mixed_one = mm(down_one, w_out[0], NT).astype(BF)
        dq_one, dk_one, dv_one = attend_back(
            query_one, key_one, value_one, grad_mixed_one, mixed_one, sums_one, target_length, True
        )
        in_share_one = reduce_grad(
            rows_one, jnp.stack([dq_one, dk_one, dv_one], axis=1).reshape(dq_one.shape[0], 3, 2, -1)
        )
        back_one = core_scatter(
            mm(dq_one, w_self[0]) + mm(dk_one, w_self[1]) + mm(dv_one, w_self[2])
        )
        unit_one_half = half_of(unit_one, core)
        grad_one_half = half_of(grad_one, core)
        hidden_grad = from_row(
            grad_one_half
            + normalize_back(back_one, unit_one_half, half_of(inverse_one, core), norm_gain[0])
        )

        in_proj_grad = jnp.stack([in_share_one, jnp.concatenate([q_share_two, kv_share_two])])
        out_proj_grad = jnp.concatenate([out_share_one, out_share_two])

        def placed(array, size):
            width = array.shape[-1] // 2
            out = jnp.zeros(array.shape[:-1] + (size // width, width), F32)
            axis = out.ndim - 2
            for part, half in ((array[..., :width], side), (array[..., width:], 1 - side)):
                out = lax.dynamic_update_slice_in_dim(
                    out, jnp.expand_dims(part, axis), half * 2 + core, axis
                )
            return out.reshape(array.shape[:-1] + (size,))

        def col_sum(array):
            return jnp.sum(array.astype(F32), axis=0)

        in_bias_part = placed(
            jnp.stack(
                [
                    jnp.stack([col_sum(dq_one), col_sum(dv_one)]),
                    jnp.stack([col_sum(dq_two), col_sum(dv_two)]),
                ]
            ),
            4 * head_part,
        )
        up_bias_part = placed(col_sum(grad_pre), 2 * ffn_up_bias.shape[0])
        back_three_half = half_of(back_three, core)
        back_two_half = half_of(back_two, core)
        model_part = jnp.stack(
            [
                col_sum(grad_one_half),
                col_sum(half_of(grad_two, core)),
                col_sum(grad_half),
                col_sum(back_one * unit_one_half),
                col_sum(back_two_half * half_of(unit_two, core)),
                col_sum(back_three_half * half_of(unit_three, core)),
                col_sum(back_one),
                col_sum(back_two_half),
                col_sum(back_three_half),
            ]
        )
        width = model_part.shape[1]
        sums = jnp.concatenate(
            [in_bias_part.reshape(-1, width), up_bias_part.reshape(-1, width), model_part]
        )
        for i in range(bits):
            sums = sums + over(sums, i)
        sums = sums + across(sums)
        in_bias_grad = sums[:4].reshape(2, 2, width)
        up_rows = up_bias_part.size // width
        ffn_up_bias_grad = sums[4 : 4 + up_rows].reshape(-1)
        out_bias_grad = sums[4 + up_rows : 7 + up_rows]
        norm_gain_grad = sums[7 + up_rows : 10 + up_rows]
        norm_bias_grad = sums[10 + up_rows : 13 + up_rows]
        return (
            hidden_out,
            hidden_grad,
            memory_grad,
            in_proj_grad,
            out_proj_grad,
            up_share,
            down_share,
            in_bias_grad,
            ffn_up_bias_grad,
            out_bias_grad,
            norm_gain_grad,
            norm_bias_grad,
        )

    return shards


def solution(mesh):
    return jax.shard_map(
        make_shards(mesh),
        mesh=mesh,
        in_specs=(
            P(("dp", "tensor"), None),
            P(("dp", "tensor"), None),
            P(None, None, "tensor", None),
            P(None, None, "tensor"),
            P(None, "tensor", None),
            P("tensor", None),
            P("tensor"),
            P("tensor", None),
            P(),
            P(),
            P(),
            P(("dp", "tensor"), None),
            P(),
            P(),
            P("dp"),
        ),
        out_specs=(
            P(("dp", "tensor"), None),
            P(("dp", "tensor"), None),
            P(("dp", "tensor"), None),
            P(None, None, "tensor", "dp"),
            P(None, "tensor", "dp"),
            P("tensor", "dp"),
            P("tensor", "dp"),
            P(),
            P(),
            P(),
            P(),
            P(),
        ),
        check_vma=False,
    )
```

```python
import functools

import jax
import jax.numpy as jnp
from jax import lax
from jax.experimental import pallas as pl
from jax.experimental.pallas import tpu as pltpu
from jax.sharding import PartitionSpec as P

HEAD_DIM = 64
F32 = jnp.float32
BF = jnp.bfloat16
NT = (((1,), (1,)), ((), ()))
TN = (((0,), (0,)), ((), ()))
NN = (((1,), (0,)), ((), ()))

epsilon = 1e-05
masked_score = -1e30
root_half = 0.7071067811865476
normal_peak = 0.3989422804014327
score_scale = HEAD_DIM ** (-0.5)


def mm(left, right, dims=NN):
    return lax.dot_general(left, right, dims, preferred_element_type=F32)


def three_parts(values):
    top = values.astype(BF).astype(F32)
    rest = values - top
    middle = rest.astype(BF).astype(F32)
    return top, middle, rest - middle


def attend_kernel(causal, step, joint, len_ref, *refs):
    if joint:
        a_ref, o_ref, sum_ref = refs
        q, k, v = a_ref[:, :128], a_ref[:, 128:256], a_ref[:, 256:]
    else:
        q_ref, kv_ref, o_ref, sum_ref = refs
        q, k, v = q_ref[...], kv_ref[:, :128], kv_ref[:, 128:]
    length = len_ref[0]
    rows, keys = q.shape[0], k.shape[0]
    lane = lax.broadcasted_iota(jnp.int32, (1, 128), 1)
    key_pos = lax.broadcasted_iota(jnp.int32, (keys, 1), 0)
    bias = jnp.where(key_pos < length, 0.0, masked_score)
    q = q.astype(F32) * score_scale
    k = k.astype(F32)
    v = v.astype(F32)
    sides = []
    for head in range(2):
        own = (lane < 64) if head == 0 else (lane >= 64)
        first = lane == (64 if head == 0 else 0)
        q_wide = jnp.where(own, q, jnp.where(first, 1.0, 0.0)).astype(BF)
        k_wide = jnp.where(own, k, jnp.where(first, bias, 0.0)).astype(BF)
        v_wide = jnp.where(own, v, 1.0).astype(BF)
        sides.append((q_wide, k_wide, v_wide))
    for block in range(rows // step):
        here = slice(block * step, (block + 1) * step)
        reach = (block + 1) * step if causal else keys
        parts = []
        for head in range(2):
            q_wide, k_wide, v_wide = sides[head]
            scores = mm(q_wide[here], k_wide[:reach], NT)
            if causal:
                below = lax.broadcasted_iota(jnp.int32, (step, step), 1) <= lax.broadcasted_iota(
                    jnp.int32, (step, step), 0
                )
                edge = jnp.where(below, scores[:, reach - step :], masked_score)
                if block == 0:
                    scores = edge
                else:
                    scores = jnp.concatenate([scores[:, : reach - step], edge], axis=1)
            top = jnp.max(scores, axis=1, keepdims=True)
            weights = jnp.exp(scores - top).astype(BF)
            mixed = mm(weights, v_wide[:reach])
            total = mixed[:, 64:65] if head == 0 else mixed[:, 0:1]
            parts.append((mixed / total, top + jnp.log(total)))
        o_ref[here, :] = jnp.where(lane < 64, parts[0][0], parts[1][0]).astype(BF)
        sum_ref[here, :] = jnp.where(lane < 64, parts[0][1], parts[1][1])


def attend_back_kernel(causal, step, joint, len_ref, *refs):
    if joint:
        a_ref, g_ref, o_ref, sum_ref, da_ref, col_ref, acc_ref = refs
        q, k, v = a_ref[:, :128], a_ref[:, 128:256], a_ref[:, 256:]
        dq_ref, dk_ref, dv_ref = da_ref, da_ref, da_ref
        starts = (0, 128, 256)
    else:
        q_ref, kv_ref, g_ref, o_ref, sum_ref, dq_ref, dkv_ref, col_ref, acc_ref = refs
        q, k, v = q_ref[...], kv_ref[:, :128], kv_ref[:, 128:]
        dk_ref, dv_ref = dkv_ref, dkv_ref
        starts = (0, 0, 128)
    length = len_ref[0]
    rows, keys = q.shape[0], k.shape[0]
    lane = lax.broadcasted_iota(jnp.int32, (1, 128), 1)
    key_pos = lax.broadcasted_iota(jnp.int32, (keys, 1), 0)
    bias = jnp.where(key_pos < length, 0.0, masked_score)
    q = q.astype(F32) * score_scale
    k = k.astype(F32)
    v = v.astype(F32)
    g = g_ref[...].astype(F32)
    overlap = g * o_ref[...].astype(F32)
    log_sums = sum_ref[...]
    sides = []
    for head in range(2):
        own = (lane < 64) if head == 0 else (lane >= 64)
        base = 64 if head == 0 else 0
        at = [lane == base + i for i in range(4)]
        minus = jnp.where(at[1] | at[2] | at[3], -1.0, 0.0)
        delta = jnp.sum(jnp.where(own, overlap, 0.0), axis=1, keepdims=True)
        log_sum = log_sums[:, 0:1] if head == 0 else log_sums[:, 64:65]
        s0, s1, s2 = three_parts(log_sum)
        d0, d1, d2 = three_parts(delta)
        extra_q = jnp.where(
            at[0], 1.0, jnp.where(at[1], s0, jnp.where(at[2], s1, jnp.where(at[3], s2, 0.0)))
        )
        extra_g = jnp.where(at[1], d0, jnp.where(at[2], d1, jnp.where(at[3], d2, 0.0)))
        q_wide = jnp.where(own, q, extra_q).astype(BF)
        k_wide = jnp.where(own, k, jnp.where(at[0], bias, minus)).astype(BF)
        g_wide = jnp.where(own, g, extra_g).astype(BF)
        v_wide = jnp.where(own, v, minus).astype(BF)
        sides.append((q_wide, k_wide, g_wide, v_wide))
    dv_sum = jnp.zeros((1, 128), F32)
    for block in range(keys // step):
        here = slice(block * step, (block + 1) * step)
        low = block * step if causal else 0
        dks = []
        dvs = []
        for head in range(2):
            q_wide, k_wide, g_wide, v_wide = sides[head]
            scores = mm(k_wide[here], q_wide[low:], NT)
            if causal:
                below = lax.broadcasted_iota(jnp.int32, (step, step), 0) <= lax.broadcasted_iota(
                    jnp.int32, (step, step), 1
                )
                edge = jnp.where(below, scores[:, :step], masked_score)
                if low + step == rows:
                    scores = edge
                else:
                    scores = jnp.concatenate([edge, scores[:, step:]], axis=1)
            probs = jnp.exp(scores)
            grads = (probs * mm(v_wide[here], g_wide[low:], NT)).astype(BF)
            dvs.append(mm(probs.astype(BF), g_wide[low:]))
            dks.append(mm(grads, q_wide[low:]))
            dq = mm(grads, k_wide[here], TN)
            if block == 0:
                acc_ref[head] = dq
            else:
                acc_ref[head, low:, :] += dq
        dv = jnp.where(lane < 64, dvs[0], dvs[1]).astype(BF)
        dv_sum = dv_sum + jnp.sum(dv.astype(F32), axis=0, keepdims=True)
        dv_ref[here, starts[2] : starts[2] + 128] = dv
        dk_ref[here, starts[1] : starts[1] + 128] = jnp.where(lane < 64, dks[0], dks[1]).astype(BF)
    dq = (jnp.where(lane < 64, acc_ref[0], acc_ref[1]) * score_scale).astype(BF)
    dq_ref[:, starts[0] : starts[0] + 128] = dq
    dq_sum = jnp.sum(dq.astype(F32), axis=0, keepdims=True)
    col_ref[...] = jnp.broadcast_to(jnp.concatenate([dq_sum, dv_sum], axis=1), (8, 256))


def columns(rows, width):
    return pl.BlockSpec((rows, width), lambda i: (0, i))


def attend(arrays, length, causal):
    joint = len(arrays) == 1
    rows = arrays[0].shape[0]
    pairs = arrays[0].shape[1] // (384 if joint else 128)
    keys = arrays[-1].shape[0]
    return pl.pallas_call(
        functools.partial(attend_kernel, causal, 256, joint),
        grid=(pairs,),
        in_specs=[pl.BlockSpec(memory_space=pltpu.SMEM)]
        + [columns(a.shape[0], a.shape[1] // pairs) for a in arrays],
        out_specs=[columns(rows, 128), columns(rows, 128)],
        out_shape=[
            jax.ShapeDtypeStruct((rows, 128 * pairs), BF),
            jax.ShapeDtypeStruct((rows, 128 * pairs), F32),
        ],
        compiler_params=pltpu.CompilerParams(vmem_limit_bytes=24 << 20),
        cost_estimate=pl.CostEstimate(flops=1, bytes_accessed=1, transcendentals=0),
    )(length, *arrays)


def attend_back(arrays, grad, out, sums, length, causal):
    joint = len(arrays) == 1
    rows = arrays[0].shape[0]
    pairs = arrays[0].shape[1] // (384 if joint else 128)
    keys = arrays[-1].shape[0]
    return pl.pallas_call(
        functools.partial(attend_back_kernel, causal, 256, joint),
        grid=(pairs,),
        in_specs=[pl.BlockSpec(memory_space=pltpu.SMEM)]
        + [columns(a.shape[0], a.shape[1] // pairs) for a in arrays]
        + [columns(rows, 128)] * 3,
        out_specs=[columns(a.shape[0], a.shape[1] // pairs) for a in arrays] + [columns(8, 256)],
        out_shape=[jax.ShapeDtypeStruct(a.shape, BF) for a in arrays]
        + [jax.ShapeDtypeStruct((8, 256 * pairs), F32)],
        scratch_shapes=[pltpu.VMEM((2, rows, 128), F32)],
        compiler_params=pltpu.CompilerParams(vmem_limit_bytes=24 << 20),
        cost_estimate=pl.CostEstimate(flops=1, bytes_accessed=1, transcendentals=0),
    )(length, *arrays, grad, out, sums)


def unit_of(values):
    centred = values - jnp.mean(values, axis=-1, keepdims=True)
    inverse = lax.rsqrt(jnp.mean(centred * centred, axis=-1, keepdims=True) + epsilon)
    return centred * inverse, inverse


def piece_sum(own_refs, far_refs, out_ref):
    block = out_ref.shape[0]
    per_piece = own_refs[0].shape[0] // block
    for number, (own_ref, far_ref) in enumerate(zip(own_refs, far_refs)):
        for part in range(per_piece):

            @pl.when(pl.program_id(0) == number * per_piece + part)
            def _():
                here = slice(part * block, (part + 1) * block)
                out_ref[...] = own_ref[here, :].astype(F32) + far_ref[here, :].astype(F32)


def norm_kernel(pieces, *refs):
    gain_ref, shift_ref, stream_ref = refs[:3]
    stream = stream_ref[...].astype(F32)
    if pieces:
        own_refs, far_refs = refs[3 : 3 + pieces], refs[3 + pieces : 3 + 2 * pieces]
        bias_ref, kept_ref, out_ref, sum_ref = refs[3 + 2 * pieces :]
        piece_sum(own_refs, far_refs, sum_ref)
        stream = stream + sum_ref[...] + bias_ref[...]
        kept_ref[...] = stream
    else:
        out_ref = refs[3]
    unit, _ = unit_of(stream)
    out_ref[...] = (unit * gain_ref[...] + shift_ref[...]).astype(BF)


def whole(array):
    return pl.BlockSpec(array.shape, lambda *i: (0, 0))


def norm(gain, shift, stream, own=(), far=(), bias=None):
    rows, width = stream.shape
    block = 256
    spec = pl.BlockSpec((block, width), lambda i: (i, 0))
    operands = [gain, shift, stream, *own, *far] + ([] if bias is None else [bias])
    return pl.pallas_call(
        functools.partial(norm_kernel, len(own)),
        grid=(rows // block,),
        in_specs=[whole(gain), whole(shift), spec] + [whole(a) for a in operands[3:]],
        out_specs=[spec] * (2 if own else 1),
        out_shape=([jax.ShapeDtypeStruct((rows, width), F32)] if own else [])
        + [jax.ShapeDtypeStruct((rows, width), BF)],
        scratch_shapes=[pltpu.VMEM((block, width), F32)] if own else [],
        compiler_params=pltpu.CompilerParams(vmem_limit_bytes=24 << 20),
        cost_estimate=pl.CostEstimate(flops=1, bytes_accessed=1, transcendentals=0),
    )(*operands)


def norm_back_kernel(pieces, per_half, core_ref, gain_ref, *refs):
    step = pl.program_id(0)
    own_refs, far_refs = refs[:pieces], refs[pieces : 2 * pieces]
    stream_ref, down_ref, full_ref, low_ref, sum_ref, grad_ref = refs[2 * pieces :]
    piece_sum(own_refs, far_refs, grad_ref)
    grad = grad_ref[...]
    unit, inverse = unit_of(stream_ref[...].astype(F32))
    scaled = grad * gain_ref[...]
    total = down_ref[...].astype(F32) + inverse * (
        scaled
        - jnp.mean(scaled, axis=-1, keepdims=True)
        - unit * jnp.mean(scaled * unit, axis=-1, keepdims=True)
    )
    full_ref[...] = total
    low_ref[...] = total.astype(BF)

    @pl.when(step == 0)
    def _():
        sum_ref[...] = jnp.zeros_like(sum_ref)

    def add():
        sum_ref[0:1, :] += jnp.sum(total, axis=0, keepdims=True)
        sum_ref[1:2, :] += jnp.sum(grad * unit, axis=0, keepdims=True)
        sum_ref[2:3, :] += jnp.sum(grad, axis=0, keepdims=True)

    if per_half is None:
        add()
    else:
        pl.when((step // per_half) == core_ref[0])(add)


def norm_back(core, gain, own, far, stream, down, whole_slot):
    rows, width = stream.shape
    block = 256
    spec = pl.BlockSpec((block, width), lambda i, ref: (i, 0))
    if whole_slot:
        down_spec = spec
    else:
        down_spec = pl.BlockSpec((block, width), lambda i, ref: (i + ref[0] * (rows // block), 0))
    return pl.pallas_call(
        functools.partial(
            norm_back_kernel, len(own), rows // (2 * block) if whole_slot else None
        ),
        grid_spec=pltpu.PrefetchScalarGridSpec(
            num_scalar_prefetch=1,
            grid=(rows // block,),
            in_specs=[whole(a) for a in (gain, *own, *far)] + [spec, down_spec],
            out_specs=[spec, spec, pl.BlockSpec((8, width), lambda i, ref: (0, 0))],
            scratch_shapes=[pltpu.VMEM((block, width), F32)],
        ),
        out_shape=[
            jax.ShapeDtypeStruct((rows, width), F32),
            jax.ShapeDtypeStruct((rows, width), BF),
            jax.ShapeDtypeStruct((8, width), F32),
        ],
        compiler_params=pltpu.CompilerParams(vmem_limit_bytes=24 << 20),
        cost_estimate=pl.CostEstimate(flops=1, bytes_accessed=1, transcendentals=0),
    )(core, gain, *own, *far, stream, down)


def ffn_kernel(a_ref, g_ref, up_ref, down_ref, bias_ref, active_ref, grad_ref, sum_ref):
    rows = a_ref.shape[0]
    total = jnp.zeros((1, up_ref.shape[0]), F32)
    for start in range(0, rows, 256):
        here = slice(start, start + 256)
        values = mm(a_ref[here, :], up_ref[...], NT) + bias_ref[...]
        below = 0.5 * (1.0 + lax.erf(values * root_half))
        slope = below + values * jnp.exp(-0.5 * values * values) * normal_peak
        active_ref[here, :] = (values * below).astype(BF)
        grad = mm(g_ref[here, :], down_ref[...], NT).astype(BF).astype(F32)
        grad = (grad * slope).astype(BF)
        grad_ref[here, :] = grad
        total = total + jnp.sum(grad.astype(F32), axis=0, keepdims=True)
    sum_ref[...] = jnp.broadcast_to(total, sum_ref.shape)


def ffn(rows_mat, grad_mat, up, down, bias):
    rows, width = rows_mat.shape
    hidden = up.shape[0]
    block = 256
    whole = pl.BlockSpec((rows, width), lambda i: (0, 0))
    weight = pl.BlockSpec((block, width), lambda i: (i, 0))
    return pl.pallas_call(
        ffn_kernel,
        grid=(hidden // block,),
        in_specs=[whole, whole, weight, weight, columns(1, block)],
        out_specs=[columns(rows, block), columns(rows, block), columns(8, block)],
        out_shape=[
            jax.ShapeDtypeStruct((rows, hidden), BF),
            jax.ShapeDtypeStruct((rows, hidden), BF),
            jax.ShapeDtypeStruct((8, hidden), F32),
        ],
        compiler_params=pltpu.CompilerParams(vmem_limit_bytes=24 << 20),
        cost_estimate=pl.CostEstimate(flops=1, bytes_accessed=1, transcendentals=0),
    )(rows_mat, grad_mat, up, down, bias)


def product_kernel(count, dims, scalar_ref, *refs):
    total = mm(refs[0][...], refs[1][...], dims)
    for number in range(1, count):
        total = total + mm(refs[2 * number][...], refs[2 * number + 1][...], dims)
    for ref in refs[2 * count : -1]:
        total = total + ref[...]
    refs[-1][...] = total.astype(BF)


def product(terms, dims=NN, bias=None, half=None):
    block = 256
    select = jnp.zeros((1,), jnp.int32) if half is None else half.reshape(1)
    rows = terms[0][0].shape[1 if dims == TN else 0] // (1 if half is None else 2)
    cols = terms[0][1].shape[0 if dims == NT else 1]
    operands = []
    specs = []
    for left, right in terms:
        operands += [left, right]
        if dims == TN:
            specs.append(pl.BlockSpec((left.shape[0], block), lambda i, ref: (0, i)))
            specs.append(pl.BlockSpec(right.shape, lambda i, ref: (0, 0)))
        else:
            specs.append(pl.BlockSpec((rows, left.shape[1]), lambda i, ref: (ref[0], 0)))
            if dims == NT:
                specs.append(pl.BlockSpec((block, right.shape[1]), lambda i, ref: (i, 0)))
            else:
                specs.append(pl.BlockSpec((right.shape[0], block), lambda i, ref: (0, i)))
    if bias is not None:
        operands.append(bias)
        specs.append(pl.BlockSpec((1, block), lambda i, ref: (0, i)))
    if dims == TN:
        grid, out_spec = rows // block, pl.BlockSpec((block, cols), lambda i, ref: (i, 0))
    else:
        grid, out_spec = cols // block, pl.BlockSpec((rows, block), lambda i, ref: (0, i))
    return pl.pallas_call(
        functools.partial(product_kernel, len(terms), dims),
        grid_spec=pltpu.PrefetchScalarGridSpec(
            num_scalar_prefetch=1, grid=(grid,), in_specs=specs, out_specs=out_spec
        ),
        out_shape=jax.ShapeDtypeStruct((rows, cols), BF),
        compiler_params=pltpu.CompilerParams(vmem_limit_bytes=24 << 20),
        cost_estimate=pl.CostEstimate(flops=1, bytes_accessed=1, transcendentals=0),
    )(select, *operands)


def split_kernel(counts, low, bit_ref, *refs):
    send_ref, keep_ref = refs[-2:]
    first = bit_ref[0] == 0
    at = 0
    offset = 0
    for count in counts:
        total = refs[at][...].astype(F32)
        for ref in refs[at + 1 : at + count]:
            total = total + ref[...].astype(F32)
        at += count
        upper, under = total[:low], total[low:]
        width = total.shape[1]
        keep_ref[:, offset : offset + width] = jnp.where(first, upper, under).astype(keep_ref.dtype)
        send_ref[:, offset : offset + width] = jnp.where(first, under, upper).astype(send_ref.dtype)
        offset += width


def split_step(parts, bit, low, send_type=BF):
    operands = []
    specs = []
    widths = []
    for part in parts:
        for item in part:
            array, block, width = item if isinstance(item, tuple) else (item, 0, item.shape[1])
            operands.append(array)
            specs.append(pl.BlockSpec((2 * low, width), lambda i, block=block: (i, block)))
        widths.append(width)
    rows = operands[0].shape[0]
    wide = sum(widths)
    out_spec = pl.BlockSpec((low, wide), lambda i: (i, 0))
    return pl.pallas_call(
        functools.partial(split_kernel, [len(p) for p in parts], low),
        grid=(rows // (2 * low),),
        in_specs=[pl.BlockSpec(memory_space=pltpu.SMEM)] + specs,
        out_specs=[out_spec, out_spec],
        out_shape=[
            jax.ShapeDtypeStruct((rows // 2, wide), send_type),
            jax.ShapeDtypeStruct((rows // 2, wide), F32),
        ],
        compiler_params=pltpu.CompilerParams(vmem_limit_bytes=24 << 20),
        cost_estimate=pl.CostEstimate(flops=1, bytes_accessed=1, transcendentals=0),
    )(bit.reshape(1), *operands)


def copy_kernel(count, moves, scalar_ref, *refs):
    semaphore = refs[-1]
    copies = []
    for number, (source, start, rows, out, out_start) in enumerate(moves):
        ends = []
        for ref, (lead, row) in ((refs[source], start), (refs[count + out], out_start)):
            if callable(row):
                row = pl.multiple_of(row(scalar_ref[0], scalar_ref[1]), 64)
            ends.append(ref.at[(*lead, pl.ds(row, rows))])
        copies.append(pltpu.make_async_copy(*ends, semaphore.at[number]))
    for copy in copies:
        copy.start()
    for copy in copies:
        copy.wait()


def copy_rows(scalars, sources, shapes, moves, grant=24):
    return pl.pallas_call(
        functools.partial(copy_kernel, len(sources), moves),
        in_specs=[pl.BlockSpec(memory_space=pltpu.SMEM)]
        + [pl.BlockSpec(memory_space=pltpu.HBM)] * len(sources),
        out_specs=[pl.BlockSpec(memory_space=pltpu.VMEM)] * len(shapes),
        out_shape=[jax.ShapeDtypeStruct(shape, BF) for shape in shapes],
        scratch_shapes=[pltpu.SemaphoreType.DMA((len(moves),))],
        compiler_params=pltpu.CompilerParams(vmem_limit_bytes=grant << 20),
        cost_estimate=pl.CostEstimate(flops=1, bytes_accessed=1, transcendentals=0),
    )(scalars, *sources)


def take(array, index, axis=0):
    return lax.dynamic_index_in_dim(array, index, axis, keepdims=False)


def tie(values, *others):
    return lax.optimization_barrier((values, others))[0]


def make_shards(mesh):
    dp_size = mesh.shape["dp"]
    bits = dp_size.bit_length() - 1

    def shards(
        hidden_in, memory, in_proj, in_bias, out_proj, ffn_up, ffn_up_bias, ffn_down, out_bias,
        norm_gain, norm_bias, out_grad, target_len, source_len, assignment,
    ):
        dp = lax.axis_index("dp")
        side = lax.axis_index("tensor")
        core = dp & 1
        core_one = core.reshape(1)
        bit = [(dp >> i) & 1 for i in range(bits)]
        model = norm_gain.shape[1]

        def over(array, i):
            return lax.ppermute(array, "dp", [(d, d ^ (1 << i)) for d in range(dp_size)])

        def across(array):
            return lax.ppermute(array, "tensor", [(0, 1), (1, 0)])

        def slot_swap(array):
            pairs = []
            for j in range(dp_size // 2):
                pairs += [(4 * j + 1, 4 * j + 2), (4 * j + 2, 4 * j + 1)]
            return jnp.where(core == side, array, lax.ppermute(array, ("dp", "tensor"), pairs))

        def whole_row(half):
            other = over(half, 0)
            return jnp.concatenate(
                [jnp.where(core == 0, half, other), jnp.where(core == 0, other, half)], axis=0
            )

        def half_of(array, index):
            return take(array.reshape(2, array.shape[0] // 2, -1), index)

        own_row = jnp.broadcast_to(assignment.reshape(1, 1).astype(F32), (8, 128))
        held = jnp.where(core == side, own_row, over(own_row, 0))[0, 0].astype(jnp.int32)
        row_ids = lax.iota(jnp.int32, target_len.shape[0])
        target_length = jnp.sum(jnp.where(row_ids == held, target_len, 0)).reshape(1)
        source_length = jnp.sum(jnp.where(row_ids == held, source_len, 0)).reshape(1)

        place = bit[1] + 2 * bit[2]
        where = jnp.stack([core, place])
        heads_q = in_proj.shape[2] // 2
        heads_p = heads_q // 4
        pairs = heads_q // 128
        ffn_q = ffn_up.shape[0] // 2
        ffn_p = ffn_q // 4

        def spot(quarter, size):
            return lambda c, p: c * quarter + p * size

        def pieces(sources, picks, quarter, size):
            moves = [
                (source, (lead, spot(quarter, size)), size, 0, ((kind,), 0))
                for kind, (source, lead) in enumerate(picks)
            ]
            return copy_rows(where, sources, [(len(picks), size, model)], moves, 60)[0]

        def hand_on(far):
            return far, over(far, 1), over(far, 2)

        def hand_last(got):
            cut = got[0].shape[0] // 2
            return got + (over(got[1][:cut], 2), over(got[2][cut:], 1))

        def there_moves(got, kind, out, size, dest):
            cut = got[0].shape[0] // 2
            moves = []
            for number in range(4):
                if number < 3:
                    source, lead = number, (kind,)
                elif kind < cut:
                    source, lead = 3, (kind,)
                else:
                    source, lead = 4, (kind - cut,)
                moves.append(
                    (source, (lead, 0), size, out, ((), lambda c, p, n=number: dest(p ^ n)))
                )
            return moves

        def pair_row(kinds, kind):
            return lambda head: ((head // 2) * kinds + kind) * 128 + (head % 2) * 64

        def near_pairs(layer, kinds, out):
            return [
                (0, ((layer, kind), lambda c, p, r=pair: c * heads_q + r * 128), 128, out,
                 ((), (pair * len(kinds) + number) * 128))
                for pair in range(pairs)
                for number, kind in enumerate(kinds)
            ]

        own_c = lambda c, p: c * heads_q
        near_c = lambda c, p: c * ffn_q

        first_piece = pieces(
            [in_proj, out_proj], [(0, (0, 0)), (0, (0, 1)), (0, (0, 2)), (1, (0,))], heads_q, heads_p
        )
        self_far = across(first_piece)
        in_late, out_late, up_late, down_late = tie((in_proj, out_proj, ffn_up, ffn_down), first_piece)
        second_piece = pieces(
            [in_late, out_late], [(0, (1, 0)), (0, (1, 1)), (0, (1, 2)), (1, (1,))], heads_q, heads_p
        )
        third_piece = pieces(
            list(tie((up_late, down_late), second_piece)), [(0, ()), (1, ())], ffn_q, ffn_p
        )
        wide = (3 * heads_q, model)
        slim = (heads_q, model)
        near_self, near_out_one = copy_rows(
            where,
            list(tie((in_late, out_late), third_piece)),
            [wide, slim],
            near_pairs(0, [0, 1, 2], 0) + [(1, ((0,), own_c), heads_q, 1, ((), 0))],
            60,
        )
        near_query, near_memory, near_out_two = copy_rows(
            where,
            list(tie((in_late, out_late), near_self)),
            [slim, (2 * heads_q, model), slim],
            [(0, ((1, 0), own_c), heads_q, 0, ((), 0))]
            + near_pairs(1, [1, 2], 1)
            + [(1, ((1,), own_c), heads_q, 2, ((), 0))],
            60,
        )
        near_up, near_down = copy_rows(
            where,
            list(tie((up_late, down_late), near_query)),
            [(ffn_q, model)] * 2,
            [(i, ((), near_c), ffn_q, i, ((), 0)) for i in range(2)],
            60,
        )

        def quarter(array, axis):
            size = array.shape[axis] // 2
            return lax.dynamic_slice_in_dim(array, core * size, size, axis)

        self_far = tie(self_far, near_up, near_memory)
        self_got = hand_on(self_far)
        hidden_half = slot_swap(tie(hidden_in, self_far))
        memory_half = slot_swap(tie(memory, hidden_half))
        cross_far = across(tie(second_piece, hidden_half))
        hidden_row = whole_row(tie(hidden_half, self_got))
        self_got = hand_last(self_got)

        bias_near = jnp.concatenate([quarter(in_bias, 2).reshape(-1), quarter(ffn_up_bias, 0)])
        bias_far = across(bias_near)
        head_part = in_bias.shape[2] // 2
        bias_sides = [b[: 4 * head_part].reshape(2, 2, pairs, 128) for b in (bias_near, bias_far)]
        up_bias = [b[4 * head_part :].reshape(1, -1) for b in (bias_near, bias_far)]
        zero = jnp.zeros((pairs, 128), F32)
        self_bias = [jnp.stack([b[0, 0], zero, b[0, 1]], axis=1).reshape(1, -1) for b in bias_sides]
        query_bias = [b[1, 0].reshape(1, -1) for b in bias_sides]
        memory_bias = [jnp.stack([zero, b[1, 1]], axis=1).reshape(1, -1) for b in bias_sides]

        gains = [norm_gain[i : i + 1] for i in range(3)]
        shifts = [norm_bias[i : i + 1] for i in range(3)]

        def both_sides(lefts, rights, rows=None):
            if rows is not None:
                lefts = [lax.dynamic_slice_in_dim(a, *rows) for a in lefts]
            return (mm(lefts[0], rights[0]) + mm(lefts[1], rights[1])).astype(BF)

        def in_pieces(lefts, rights, start=0, count=2):
            return [both_sides(lefts, rights, (start + 512 * i, 512)) for i in range(count)]

        def exchange(pieces):
            return [over(piece, 0) for piece in pieces]

        (rows_one,) = norm(gains[0], shifts[0], hidden_row)

        def self_side(weight, bias):
            joint = product([(rows_one, weight)], NT, bias)
            return ([joint], *attend([joint], target_length, True))

        one = [self_side(near_self, self_bias[0])]
        memory_half = tie(memory_half, one[0][1])
        memory_row = whole_row(memory_half)
        far_self, far_out_one = copy_rows(
            where,
            list(tie(self_got, one[0][1])),
            [wide, slim],
            [m for k in range(3) for m in there_moves(self_got, k, 0, heads_p, pair_row(3, k))]
            + there_moves(self_got, 3, 1, heads_p, lambda head: head * heads_p),
        )
        w_self = [near_self, far_self]
        cross_far = tie(cross_far, one[0][1])
        cross_got = hand_on(cross_far)
        ffn_far = across(tie(third_piece, cross_far))
        one.append(self_side(tie(far_self, cross_far), self_bias[1]))
        part = in_pieces(tie([s[1] for s in one], cross_got), [near_out_one, far_out_one])
        stream_one, rows_two = norm(
            gains[1], shifts[1], hidden_row, part, exchange(part), out_bias[0:1]
        )

        def cross_side(weight, bias, kv_weight, kv_bias):
            kv = product([(memory_row, kv_weight)], NT, kv_bias)
            query = product([(rows_two, weight)], NT, bias)
            return ([query, kv], *attend([query, kv], source_length, False))

        cross_got = hand_last(cross_got)
        rows_two = tie(rows_two, ffn_far)
        ffn_got = hand_on(ffn_far)
        grad_half = slot_swap(tie(out_grad, ffn_far))
        two = [cross_side(near_query, query_bias[0], near_memory, memory_bias[0])]
        far_query, far_memory, far_out_two = copy_rows(
            where,
            list(tie(cross_got, two[0][1])),
            [slim, (2 * heads_q, model), slim],
            there_moves(cross_got, 0, 0, heads_p, lambda head: head * heads_p)
            + [m for k in range(2) for m in there_moves(cross_got, k + 1, 1, heads_p, pair_row(2, k))]
            + there_moves(cross_got, 3, 2, heads_p, lambda head: head * heads_p),
        )
        far_query = tie(far_query, ffn_got)
        ffn_got = hand_last(ffn_got)
        two.append(cross_side(far_query, query_bias[1], far_memory, memory_bias[1]))
        grad_row = whole_row(tie(grad_half, two[1][1]))
        w_query = [near_query, far_query]
        w_memory = [near_memory, far_memory]
        w_out = [[near_out_one, near_out_two], [far_out_one, far_out_two]]
        part = in_pieces([s[1] for s in two], [near_out_two, far_out_two])
        stream_two, rows_three = norm(
            gains[2], shifts[2], stream_one, part, exchange(part), out_bias[1:2]
        )

        sides = [ffn(rows_three, grad_row, near_up, near_down, up_bias[0])]
        near_grads = [
            mm(grad_row, sides[0][0], TN).astype(BF), mm(rows_three, sides[0][1], TN).astype(BF)
        ]
        far_up, far_down = copy_rows(
            where,
            list(tie(ffn_got, near_grads)),
            [(ffn_q, model)] * 2,
            [m for k in range(2) for m in there_moves(ffn_got, k, k, ffn_p, lambda n: n * ffn_p)],
        )
        sides.append(ffn(rows_three, grad_row, far_up, far_down, up_bias[1]))
        w_up = [near_up, far_up]
        w_down = [near_down, far_down]
        active = [s[0] for s in sides]
        grad_pre = [s[1] for s in sides]

        unit = model // dp_size

        class Sum:
            def __init__(self, parts, left):
                self.parts, self.left, self.sent = parts, left, None

            def step(self, i, send_type=BF):
                low = unit << sum(1 for j in self.left if j < i)
                send, keep = split_step(self.parts, bit[i], low, send_type)
                self.left = [j for j in self.left if j != i]
                self.sent = send
                self.parts = [[keep, over(send, i)]]
                return self

            def after(self, *others):
                items = [item for part in self.parts for item in part]
                arrays = tie([i[0] if isinstance(i, tuple) else i for i in items], *others)
                whole = iter(
                    (a, *i[1:]) if isinstance(i, tuple) else a for a, i in zip(arrays, items)
                )
                self.parts = [[next(whole) for _ in part] for part in self.parts]
                return self

        every = list(range(bits))

        def turn(total):
            keep, arrived = total.parts[0]
            half = keep.shape[1] // 2
            send = (keep[:, half:] + arrived[:, half:].astype(F32)).astype(BF)
            total.parts = [[(keep, 0, half), (arrived, 0, half), across(send)]]
            total.sent = send
            return total

        def joined(*totals):
            return Sum([part for total in totals for part in total.parts], totals[0].left)

        down_there = mm(grad_row, active[1], TN).astype(BF)
        up_parts = [[near_grads[1]], [mm(rows_three, grad_pre[1], TN).astype(BF)]]
        part = in_pieces(tie(grad_pre, down_there, up_parts), w_up)
        down_there = across(down_there)
        up_sum = Sum(up_parts, every).step(2)
        part_far = exchange(part)
        half_rows = model // 2
        here_rows = (core * half_rows, half_rows)
        there_rows = ((1 - core) * half_rows, half_rows)
        hidden_send = both_sides(active, w_down, there_rows)
        hidden_own = both_sides(active, w_down, here_rows)
        grad_two, down_two, sums_three = norm_back(
            core_one, gains[2], part, part_far, stream_two, grad_row, True
        )

        def back_side(down, weight, kept, length, causal):
            arrays, mixed, sums = kept
            grad_mixed = mm(down, weight, NT).astype(BF)
            return attend_back(arrays, grad_mixed, mixed, sums, length, causal)

        two_back = [None, None]
        two_back[1] = back_side(down_two, w_out[1][1], two[1], source_length, False)
        down_there = tie(down_there, two_back[1][0])
        down_sum = Sum([[near_grads[0], down_there]], every).step(1)
        up_sum = turn(up_sum.after(two_back[1][0]))
        kv_there = mm(memory_row, two_back[1][1], TN).astype(BF)
        two_back[0] = back_side(tie(down_two, kv_there, down_sum.sent, up_sum.sent), w_out[0][1], two[0], source_length, False)
        kv_there = across(kv_there)
        part = in_pieces([s[0] for s in two_back], w_query)
        part_far = exchange(part)
        q_sum = Sum(
            [
                [mm(mat, array, TN).astype(BF)]
                for i in range(2)
                for mat, array in ((down_two, two[i][1]), (rows_two, two_back[i][0]))
            ],
            every,
        ).step(2)
        memory_send = both_sides([s[1] for s in two_back], w_memory, there_rows)
        memory_own = both_sides([s[1] for s in two_back], w_memory, here_rows)
        grad_one, down_one, sums_two = norm_back(
            core_one, gains[1], part, part_far, stream_one, grad_two, True
        )
        memory_grad = memory_own.astype(F32) + over(memory_send, 0).astype(F32)
        hidden_out = half_of(stream_two, core) + hidden_own.astype(F32)
        hidden_out = (hidden_out + over(hidden_send, 0).astype(F32) + out_bias[2]).astype(BF)
        moved = jnp.stack([memory_grad.astype(BF), hidden_out])

        down_sum = down_sum.after(down_one).step(2)
        up_sum = up_sum.after(down_one).step(1)
        out_sum = Sum([[mm(down_one, one[i][1], TN).astype(BF)] for i in range(2)], every).step(1)
        one_back = [None, None]
        one_back[1] = back_side(tie(down_one, moved, out_sum.sent, down_sum.sent, up_sum.sent), w_out[1][0], one[1], target_length, True)
        self_there = mm(rows_one, one_back[1][0], TN).astype(BF)
        third = self_there.shape[1] // 3
        first_there = self_there[:, : 2 * third]
        kv_there = tie(kv_there, one_back[1][0])
        kv_sum = Sum([[mm(memory_row, two_back[0][1], TN).astype(BF), kv_there]], every).step(1)
        first_sum = joined(down_sum, up_sum).after(one_back[1][0]).step(3)
        q_sum = turn(q_sum.after(one_back[1][0]))
        out_sum = turn(out_sum.after(one_back[1][0]))
        sent = [first_there] + [t.sent for t in (kv_sum, first_sum, q_sum, out_sum)]
        one_back[0] = back_side(tie(down_one, sent), w_out[0][0], one[0], target_length, True)
        first_there = across(first_there)
        self_here = mm(rows_one, one_back[0][0], TN).astype(BF)

        last_sum = Sum([[(array, 2, third)] for array in (self_here, self_there)], every).step(1)
        kv_sum = kv_sum.after(one_back[0][0]).step(2)
        q_sum = q_sum.after(one_back[0][0]).step(1)

        sent = [t.sent for t in (last_sum, kv_sum, q_sum)]
        last_back = tie([s[0] for s in one_back], sent)
        part_far = exchange(in_pieces(last_back, w_self, (1 - core) * half_rows, 1))
        part = in_pieces(last_back, w_self, core * half_rows, 1)
        self_sum = Sum([[(self_here, 0, 2 * third), first_there]], every).after(part).step(1)
        last_sum = turn(last_sum.after(part))
        part_far = tie(part_far, self_sum.sent, last_sum.sent)
        _, hidden_low, sums_one = norm_back(
            core_one, gains[0], part, part_far, hidden_half, grad_one, False
        )
        moved = slot_swap(moved)
        hidden_grad = slot_swap(hidden_low).astype(F32)
        memory_grad = moved[0].astype(F32)
        hidden_out = moved[1]

        def finish(total, first):
            for i in range(first, bits):
                total.step(i)
            total.step(0, F32)
            mine, other = total.parts[0]
            return jnp.stack(
                [jnp.where(core == 0, mine, other), jnp.where(core == 0, other, mine)]
            )

        def laid_out(total, low, groups, kinds, width):
            part = total[:, :, low : low + groups * kinds * width]
            part = part.reshape(2, part.shape[1], groups, kinds, width)
            return jnp.transpose(part, (3, 0, 2, 4, 1)).reshape(kinds, 2 * groups * width, -1)

        near_cols = active[0].shape[1]
        self_sum = joined(self_sum, last_sum, out_sum).after(hidden_low).step(2)
        cross_sum = joined(kv_sum, q_sum).after(hidden_low).step(3)
        total = finish(first_sum.after(hidden_low), 4)
        down_share = laid_out(total, 0, 1, 1, near_cols)[0]
        up_share = laid_out(total, near_cols, 1, 1, near_cols)[0]
        total = finish(self_sum, 3)
        self_in = laid_out(total, 0, pairs, 3, 128)
        self_out = laid_out(total, 3 * head_part, 1, 1, head_part)
        total = finish(cross_sum, 4)
        cross_kv = laid_out(total, 0, pairs, 2, 128)
        cross_out = laid_out(total, 2 * head_part, 1, 1, head_part)
        cross_q = laid_out(total, 3 * head_part, 1, 1, head_part)
        in_proj_grad = jnp.stack([self_in, jnp.concatenate([cross_q, cross_kv])])
        out_proj_grad = jnp.concatenate([self_out, cross_out])

        def spread(near, far):
            width = near.shape[-1]
            out = jnp.zeros(near.shape[:-1] + (4, width), F32)
            axis = out.ndim - 2
            for part, half in ((near, side), (far, 1 - side)):
                out = lax.dynamic_update_slice_in_dim(
                    out, jnp.expand_dims(part, axis), half * 2 + core, axis
                )
            return out.reshape(near.shape[:-1] + (4 * width,))

        def bias_sums(columns):
            return jnp.swapaxes(columns[0].reshape(pairs, 2, 128), 0, 1).reshape(2, -1)

        in_bias_part = spread(
            *(
                jnp.stack([bias_sums(one_back[i][-1]), bias_sums(two_back[i][-1])])
                for i in range(2)
            )
        )
        up_bias_part = spread(sides[0][2][0], sides[1][2][0])
        dy_sum = jnp.sum(grad_half.astype(F32), axis=0)
        model_part = jnp.stack(
            [
                sums_two[0],
                sums_three[0],
                dy_sum,
                sums_one[1],
                sums_two[1],
                sums_three[1],
                sums_one[2],
                sums_two[2],
                sums_three[2],
            ]
        )
        sums = jnp.concatenate(
            [in_bias_part.reshape(-1, model), up_bias_part.reshape(-1, model), model_part]
        )
        sums = sums + across(sums)
        for i in range(bits):
            sums = sums + over(sums, i)
        in_bias_grad = sums[:4].reshape(2, 2, model)
        up_rows = up_bias_part.size // model
        ffn_up_bias_grad = sums[4 : 4 + up_rows].reshape(-1)
        out_bias_grad = sums[4 + up_rows : 7 + up_rows]
        norm_gain_grad = sums[7 + up_rows : 10 + up_rows]
        norm_bias_grad = sums[10 + up_rows : 13 + up_rows]
        return (
            hidden_out,
            hidden_grad,
            memory_grad,
            in_proj_grad,
            out_proj_grad,
            up_share,
            down_share,
            in_bias_grad,
            ffn_up_bias_grad,
            out_bias_grad,
            norm_gain_grad,
            norm_bias_grad,
        )

    return shards


def solution(mesh):
    return jax.shard_map(
        make_shards(mesh),
        mesh=mesh,
        in_specs=(
            P(("dp", "tensor"), None),
            P(("dp", "tensor"), None),
            P(None, None, "tensor", None),
            P(None, None, "tensor"),
            P(None, "tensor", None),
            P("tensor", None),
            P("tensor"),
            P("tensor", None),
            P(),
            P(),
            P(),
            P(("dp", "tensor"), None),
            P(),
            P(),
            P("dp"),
        ),
        out_specs=(
            P(("dp", "tensor"), None),
            P(("dp", "tensor"), None),
            P(("dp", "tensor"), None),
            P(None, None, "tensor", "dp"),
            P(None, "tensor", "dp"),
            P("tensor", "dp"),
            P("tensor", "dp"),
            P(),
            P(),
            P(),
            P(),
            P(),
        ),
        check_vma=False,
    )
```

```python
import functools

import jax
import jax.numpy as jnp
from jax import lax
from jax.experimental import pallas as pl
from jax.experimental.pallas import tpu as pltpu
from jax.sharding import PartitionSpec as P

HEAD_DIM = 64
F32 = jnp.float32
BF = jnp.bfloat16
NT = (((1,), (1,)), ((), ()))
TN = (((0,), (0,)), ((), ()))
NN = (((1,), (0,)), ((), ()))

epsilon = 1e-05
masked_score = -1e30
root_half = 0.7071067811865476
normal_peak = 0.3989422804014327
score_scale = HEAD_DIM ** (-0.5)


def mm(left, right, dims=NN):
    return lax.dot_general(left, right, dims, preferred_element_type=F32)


def three_parts(values):
    top = values.astype(BF).astype(F32)
    rest = values - top
    middle = rest.astype(BF).astype(F32)
    return top, middle, rest - middle


def attend_kernel(causal, step, joint, len_ref, *refs):
    for pair in range(refs[-1].shape[1] // 128):
        attend_pair(causal, step, joint, pair, len_ref, *refs)


def attend_pair(causal, step, joint, pair, len_ref, *refs):
    if joint:
        a_ref, o_ref, sum_ref = refs
        q, k, v = (a_ref[:, pair * 384 + i * 128 : pair * 384 + (i + 1) * 128] for i in range(3))
    else:
        q_ref, kv_ref, o_ref, sum_ref = refs
        q = q_ref[:, pair * 128 : (pair + 1) * 128]
        k, v = (kv_ref[:, pair * 256 + i * 128 : pair * 256 + (i + 1) * 128] for i in range(2))
    mine = slice(pair * 128, (pair + 1) * 128)
    length = len_ref[0]
    rows, keys = q.shape[0], k.shape[0]
    lane = lax.broadcasted_iota(jnp.int32, (1, 128), 1)
    key_pos = lax.broadcasted_iota(jnp.int32, (keys, 1), 0)
    bias = jnp.where(key_pos < length, 0.0, masked_score)
    q = q.astype(F32) * score_scale
    k = k.astype(F32)
    v = v.astype(F32)
    sides = []
    for head in range(2):
        own = (lane < 64) if head == 0 else (lane >= 64)
        first = lane == (64 if head == 0 else 0)
        q_wide = jnp.where(own, q, jnp.where(first, 1.0, 0.0)).astype(BF)
        k_wide = jnp.where(own, k, jnp.where(first, bias, 0.0)).astype(BF)
        v_wide = jnp.where(own, v, 1.0).astype(BF)
        sides.append((q_wide, k_wide, v_wide))
    tasks = [(block, head) for block in range(rows // step) for head in range(2)]

    def scores_of(block, head):
        reach = (block + 1) * step if causal else keys
        q_wide, k_wide, _ = sides[head]
        scores = mm(q_wide[block * step : (block + 1) * step], k_wide[:reach], NT)
        if causal:
            below = lax.broadcasted_iota(jnp.int32, (step, step), 1) <= lax.broadcasted_iota(
                jnp.int32, (step, step), 0
            )
            edge = jnp.where(below, scores[:, reach - step :], masked_score)
            if block == 0:
                scores = edge
            else:
                scores = jnp.concatenate([scores[:, : reach - step], edge], axis=1)
        return scores

    ahead = scores_of(*tasks[0])
    parts = []
    for number, (block, head) in enumerate(tasks):
        scores = ahead
        if number + 1 < len(tasks):
            ahead = scores_of(*tasks[number + 1])
        here = slice(block * step, (block + 1) * step)
        reach = scores.shape[1]
        top = jnp.max(scores, axis=1, keepdims=True)
        weights = jnp.exp(scores - top).astype(BF)
        mixed = mm(weights, sides[head][2][:reach])
        total = mixed[:, 64:65] if head == 0 else mixed[:, 0:1]
        parts.append((mixed / total, top + jnp.log(total)))
        if head == 1:
            o_ref[here, mine] = jnp.where(lane < 64, parts[0][0], parts[1][0]).astype(BF)
            sum_ref[here, mine] = jnp.where(lane < 64, parts[0][1], parts[1][1])
            parts = []


def attend_back_kernel(causal, step, joint, len_ref, *refs):
    for pair in range(refs[-2].shape[1] // 256):
        attend_back_pair(causal, step, joint, pair, len_ref, *refs)


def attend_back_pair(causal, step, joint, pair, len_ref, *refs):
    if joint:
        a_ref, g_ref, o_ref, sum_ref, da_ref, col_ref, acc_ref = refs
        q, k, v = (a_ref[:, pair * 384 + i * 128 : pair * 384 + (i + 1) * 128] for i in range(3))
        dq_ref, dk_ref, dv_ref = da_ref, da_ref, da_ref
        starts = [pair * 384 + i * 128 for i in range(3)]
    else:
        q_ref, kv_ref, g_ref, o_ref, sum_ref, dq_ref, dkv_ref, col_ref, acc_ref = refs
        q = q_ref[:, pair * 128 : (pair + 1) * 128]
        k, v = (kv_ref[:, pair * 256 + i * 128 : pair * 256 + (i + 1) * 128] for i in range(2))
        dk_ref, dv_ref = dkv_ref, dkv_ref
        starts = (pair * 128, pair * 256, pair * 256 + 128)
    mine = slice(pair * 128, (pair + 1) * 128)
    length = len_ref[0]
    rows, keys = q.shape[0], k.shape[0]
    lane = lax.broadcasted_iota(jnp.int32, (1, 128), 1)
    key_pos = lax.broadcasted_iota(jnp.int32, (keys, 1), 0)
    bias = jnp.where(key_pos < length, 0.0, masked_score)
    q = q.astype(F32) * score_scale
    k = k.astype(F32)
    v = v.astype(F32)
    g = g_ref[:, mine].astype(F32)
    overlap = g * o_ref[:, mine].astype(F32)
    log_sums = sum_ref[:, mine]
    sides = []
    for head in range(2):
        own = (lane < 64) if head == 0 else (lane >= 64)
        base = 64 if head == 0 else 0
        at = [lane == base + i for i in range(4)]
        minus = jnp.where(at[1] | at[2] | at[3], -1.0, 0.0)
        delta = jnp.sum(jnp.where(own, overlap, 0.0), axis=1, keepdims=True)
        log_sum = log_sums[:, 0:1] if head == 0 else log_sums[:, 64:65]
        s0, s1, s2 = three_parts(log_sum)
        d0, d1, d2 = three_parts(delta)
        extra_q = jnp.where(
            at[0], 1.0, jnp.where(at[1], s0, jnp.where(at[2], s1, jnp.where(at[3], s2, 0.0)))
        )
        extra_g = jnp.where(at[1], d0, jnp.where(at[2], d1, jnp.where(at[3], d2, 0.0)))
        q_wide = jnp.where(own, q, extra_q).astype(BF)
        k_wide = jnp.where(own, k, jnp.where(at[0], bias, minus)).astype(BF)
        g_wide = jnp.where(own, g, extra_g).astype(BF)
        v_wide = jnp.where(own, v, minus).astype(BF)
        sides.append((q_wide, k_wide, g_wide, v_wide))
    tasks = [(block, head) for block in range(keys // step) for head in range(2)]

    def products_of(block, head):
        here = slice(block * step, (block + 1) * step)
        low = block * step if causal else 0
        q_wide, k_wide, g_wide, v_wide = sides[head]
        scores = mm(k_wide[here], q_wide[low:], NT)
        if causal:
            below = lax.broadcasted_iota(jnp.int32, (step, step), 0) <= lax.broadcasted_iota(
                jnp.int32, (step, step), 1
            )
            edge = jnp.where(below, scores[:, :step], masked_score)
            if low + step == rows:
                scores = edge
            else:
                scores = jnp.concatenate([edge, scores[:, step:]], axis=1)
        return scores, mm(v_wide[here], g_wide[low:], NT)

    ahead = products_of(*tasks[0])
    dv_sum = jnp.zeros((1, 128), F32)
    dks = []
    dvs = []
    for number, (block, head) in enumerate(tasks):
        scores, change = ahead
        if number + 1 < len(tasks):
            ahead = products_of(*tasks[number + 1])
        here = slice(block * step, (block + 1) * step)
        low = block * step if causal else 0
        q_wide, k_wide, g_wide, v_wide = sides[head]
        probs = jnp.exp(scores)
        grads = (probs * change).astype(BF)
        dvs.append(mm(probs.astype(BF), g_wide[low:]))
        dks.append(mm(grads, q_wide[low:]))
        dq = mm(k_wide[here], grads, TN)
        if block == 0:
            acc_ref[head] = dq
        else:
            acc_ref[head, :, low:] += dq
        if head == 1:
            dv = jnp.where(lane < 64, dvs[0], dvs[1]).astype(BF)
            dv_sum = dv_sum + jnp.sum(dv.astype(F32), axis=0, keepdims=True)
            dv_ref[here, starts[2] : starts[2] + 128] = dv
            dk_ref[here, starts[1] : starts[1] + 128] = jnp.where(lane < 64, dks[0], dks[1]).astype(BF)
            dks = []
            dvs = []
    side_row = lax.broadcasted_iota(jnp.int32, (128, 1), 0)
    dq = (jnp.where(side_row < 64, acc_ref[0], acc_ref[1]) * score_scale).T.astype(BF)
    dq_ref[:, starts[0] : starts[0] + 128] = dq
    dq_sum = jnp.sum(dq.astype(F32), axis=0, keepdims=True)
    both = jnp.concatenate([dq_sum, dv_sum], axis=1)
    col_ref[:, pair * 256 : (pair + 1) * 256] = jnp.broadcast_to(both, (8, 256))


CHEAP = pl.CostEstimate(flops=1, bytes_accessed=1, transcendentals=0)


def call(kernel, outs, operands, scalars=(), scratch=()):
    vmem = pl.BlockSpec(memory_space=pltpu.VMEM)
    return pl.pallas_call(
        kernel,
        in_specs=[pl.BlockSpec(memory_space=pltpu.SMEM)] * len(scalars) + [vmem] * len(operands),
        out_specs=[vmem] * len(outs),
        out_shape=[jax.ShapeDtypeStruct(*out) for out in outs],
        scratch_shapes=list(scratch),
        compiler_params=pltpu.CompilerParams(vmem_limit_bytes=24 << 20),
        cost_estimate=CHEAP,
    )(*scalars, *operands)


def attend(arrays, length, causal):
    joint = len(arrays) == 1
    rows = arrays[0].shape[0]
    width = arrays[0].shape[1] // (3 if joint else 1)
    return call(
        functools.partial(attend_kernel, causal, min(512, rows), joint),
        [((rows, width), BF), ((rows, width), F32)],
        arrays,
        [length],
    )


def attend_back(arrays, grad, out, sums, length, causal):
    joint = len(arrays) == 1
    rows, width = out.shape
    return call(
        functools.partial(attend_back_kernel, causal, min(256 if causal else 512, rows), joint),
        [(a.shape, BF) for a in arrays] + [((8, 2 * width), F32)],
        [*arrays, grad, out, sums],
        [length],
        [pltpu.VMEM((2, 128, rows), F32)],
    )


def unit_of(values):
    centred = values - jnp.mean(values, axis=-1, keepdims=True)
    inverse = lax.rsqrt(jnp.mean(centred * centred, axis=-1, keepdims=True) + epsilon)
    return centred * inverse, inverse


def row_blocks(rows):
    block = min(256, rows)
    return [slice(start, start + block) for start in range(0, rows, block)]


def piece_sum(own_refs, far_refs, here):
    size = own_refs[0].shape[0]
    number, start = here.start // size, here.start % size
    part = slice(start, start + here.stop - here.start)
    return own_refs[number][part, :].astype(F32) + far_refs[number][part, :].astype(F32)


def norm_kernel(pieces, *refs):
    gain_ref, shift_ref, stream_ref = refs[:3]
    out_ref = refs[-1]
    for here in row_blocks(stream_ref.shape[0]):
        stream = stream_ref[here, :].astype(F32)
        if pieces:
            stream = stream + piece_sum(refs[3 : 3 + pieces], refs[3 + pieces : 3 + 2 * pieces], here)
            stream = stream + refs[3 + 2 * pieces][...]
            refs[-2][here, :] = stream
        unit, _ = unit_of(stream)
        out_ref[here, :] = (unit * gain_ref[...] + shift_ref[...]).astype(BF)


def norm(gain, shift, stream, own=(), far=(), bias=None):
    outs = ([(stream.shape, F32)] if own else []) + [(stream.shape, BF)]
    operands = [gain, shift, stream, *own, *far] + ([] if bias is None else [bias])
    return call(functools.partial(norm_kernel, len(own)), outs, operands)


def norm_back_kernel(pieces, whole_slot, core_ref, gain_ref, *refs):
    own_refs, far_refs = refs[:pieces], refs[pieces : 2 * pieces]
    stream_ref, down_ref, full_ref, low_ref, sum_ref = refs[2 * pieces :]
    rows = stream_ref.shape[0]
    blocks = row_blocks(rows)
    sum_ref[...] = jnp.zeros_like(sum_ref)
    for number, here in enumerate(blocks):
        grad = piece_sum(own_refs, far_refs, here)
        unit, inverse = unit_of(stream_ref[here, :].astype(F32))
        scaled = grad * gain_ref[...]
        if whole_slot:
            down = down_ref[here, :]
        else:
            size = here.stop - here.start
            down = down_ref[pl.ds(pl.multiple_of(core_ref[0] * rows + here.start, size), size), :]
        total = down.astype(F32) + inverse * (
            scaled
            - jnp.mean(scaled, axis=-1, keepdims=True)
            - unit * jnp.mean(scaled * unit, axis=-1, keepdims=True)
        )
        full_ref[here, :] = total
        low_ref[here, :] = total.astype(BF)

        def add(total=total, grad=grad, unit=unit):
            sum_ref[0:1, :] += jnp.sum(total, axis=0, keepdims=True)
            sum_ref[1:2, :] += jnp.sum(grad * unit, axis=0, keepdims=True)
            sum_ref[2:3, :] += jnp.sum(grad, axis=0, keepdims=True)

        if whole_slot:
            pl.when((2 * number) // len(blocks) == core_ref[0])(add)
        else:
            add()


def norm_back(core, gain, own, far, stream, down, whole_slot):
    return call(
        functools.partial(norm_back_kernel, len(own), whole_slot),
        [(stream.shape, F32), (stream.shape, BF), ((8, stream.shape[1]), F32)],
        [gain, *own, *far, stream, down],
        [core],
    )


def ffn_kernel(a_ref, g_ref, up_ref, down_ref, bias_ref, active_ref, grad_ref, sum_ref):
    hidden = up_ref.shape[0]

    def block_of(number, carry):
        units = pl.ds(pl.multiple_of(number * 256, 256), 256)
        total = jnp.zeros((1, 256), F32)
        for here in row_blocks(a_ref.shape[0]):
            values = mm(a_ref[here, :], up_ref[units, :], NT) + bias_ref[:, units]
            below = 0.5 * (1.0 + lax.erf(values * root_half))
            slope = below + values * jnp.exp(-0.5 * values * values) * normal_peak
            active_ref[here, units] = (values * below).astype(BF)
            grad = mm(g_ref[here, :], down_ref[units, :], NT).astype(BF).astype(F32)
            grad = (grad * slope).astype(BF)
            grad_ref[here, units] = grad
            total = total + jnp.sum(grad.astype(F32), axis=0, keepdims=True)
        sum_ref[:, units] = jnp.broadcast_to(total, (8, 256))
        return carry

    lax.fori_loop(0, hidden // 256, block_of, 0)


def ffn(rows_mat, grad_mat, up, down, bias):
    rows, hidden = rows_mat.shape[0], up.shape[0]
    return call(
        ffn_kernel,
        [((rows, hidden), BF), ((rows, hidden), BF), ((8, hidden), F32)],
        [rows_mat, grad_mat, up, down, bias],
    )


def product_kernel(count, dims, biased, first_ref, *refs):
    out_ref = refs[-1]
    rows, cols = out_ref.shape
    block = min(256, rows if dims == TN else cols)
    for start in range(0, rows if dims == TN else cols, block):
        here = slice(start, start + block)
        total = None
        for left_ref, right_ref in zip(refs[: 2 * count : 2], refs[1 : 2 * count : 2]):
            if dims == TN:
                left, right = left_ref[:, here], right_ref[...]
            else:
                left = left_ref[pl.ds(pl.multiple_of(first_ref[0], 256), rows), :]
                right = right_ref[here, :] if dims == NT else right_ref[:, here]
            term = mm(left, right, dims)
            total = term if total is None else total + term
        if biased:
            total = total + refs[2 * count][:, here]
        if dims == TN:
            out_ref[here, :] = total.astype(BF)
        else:
            out_ref[:, here] = total.astype(BF)


def product(terms, dims=NN, bias=None, span=None):
    left, right = terms[0]
    if span is None:
        span = (0, left.shape[1 if dims == TN else 0])
    cols = right.shape[0 if dims == NT else 1]
    operands = [array for term in terms for array in term] + ([] if bias is None else [bias])
    return call(
        functools.partial(product_kernel, len(terms), dims, bias is not None),
        [((span[1], cols), BF)],
        operands,
        [jnp.asarray(span[0], jnp.int32).reshape(1)],
    )[0]


def split_kernel(parts, low, bit_ref, *refs):
    send_ref, keep_ref = refs[-2:]
    first = bit_ref[0] == 0
    offset = 0
    at = 0
    for part in parts:
        width = part[0][1]
        here = slice(offset, offset + width)
        for block in range(keep_ref.shape[0] // low):
            rows = slice(2 * low * block, 2 * low * (block + 1))
            total = None
            for ref, (start, _) in zip(refs[at : at + len(part)], part):
                values = ref[rows, start : start + width].astype(F32)
                total = values if total is None else total + values
            upper, under = total[:low], total[low:]
            out = slice(low * block, low * (block + 1))
            keep_ref[out, here] = jnp.where(first, upper, under).astype(keep_ref.dtype)
            send_ref[out, here] = jnp.where(first, under, upper).astype(send_ref.dtype)
        at += len(part)
        offset += width


def split_step(parts, bit, low, send_type=BF):
    operands = []
    layout = []
    for part in parts:
        spans = []
        for item in part:
            array, block, width = item if isinstance(item, tuple) else (item, 0, item.shape[1])
            operands.append(array)
            spans.append((block * width, width))
        layout.append(spans)
    rows = operands[0].shape[0] // 2
    wide = sum(spans[0][1] for spans in layout)
    return call(
        functools.partial(split_kernel, layout, low),
        [((rows, wide), send_type), ((rows, wide), F32)],
        operands,
        [bit.reshape(1)],
    )


def copy_kernel(count, moves, scalar_ref, *refs):
    semaphore = refs[-1]
    copies = []
    for number, (source, start, rows, out, out_start) in enumerate(moves):
        ends = []
        for ref, (lead, row) in ((refs[source], start), (refs[count + out], out_start)):
            if callable(row):
                row = pl.multiple_of(row(scalar_ref[0], scalar_ref[1]), 64)
            ends.append(ref.at[(*lead, pl.ds(row, rows))])
        copies.append(pltpu.make_async_copy(*ends, semaphore.at[number]))
    for copy in copies:
        copy.start()
    for copy in copies:
        copy.wait()


def copy_rows(scalars, sources, shapes, moves, grant=24):
    return pl.pallas_call(
        functools.partial(copy_kernel, len(sources), moves),
        in_specs=[pl.BlockSpec(memory_space=pltpu.SMEM)]
        + [pl.BlockSpec(memory_space=pltpu.HBM)] * len(sources),
        out_specs=[pl.BlockSpec(memory_space=pltpu.VMEM)] * len(shapes),
        out_shape=[jax.ShapeDtypeStruct(shape, BF) for shape in shapes],
        scratch_shapes=[pltpu.SemaphoreType.DMA((len(moves),))],
        compiler_params=pltpu.CompilerParams(vmem_limit_bytes=grant << 20),
        cost_estimate=pl.CostEstimate(flops=1, bytes_accessed=1, transcendentals=0),
    )(scalars, *sources)


def add_kernel(start, one_ref, two_ref, out_ref):
    here = slice(start, start + out_ref.shape[1])
    out_ref[...] = (one_ref[:, here].astype(F32) + two_ref[:, here].astype(F32)).astype(BF)


def add_columns(one, two, start, width):
    out = ((one.shape[0], width), BF)
    return call(functools.partial(add_kernel, start), [out], [one, two])[0]


def lay_out_kernel(core_ref, self_ref, self_far_ref, cross_ref, cross_far_ref, in_ref, out_ref):
    pairs = self_ref.shape[1] // 384
    quarter = pairs * 128
    for part in range(2):
        mine = core_ref[0] == part
        total = jnp.where(mine, self_ref[...], self_far_ref[...])
        for pair in range(pairs):
            rows = slice(part * quarter + pair * 128, part * quarter + (pair + 1) * 128)
            for kind in range(3):
                start = (pair * 3 + kind) * 128
                in_ref[0, kind, rows, :] = total[:, start : start + 128].T
        total = jnp.where(mine, cross_ref[...], cross_far_ref[...])
        for pair in range(pairs):
            rows = slice(part * quarter + pair * 128, part * quarter + (pair + 1) * 128)
            for kind in range(2):
                start = (pair * 2 + kind) * 128
                in_ref[1, kind + 1, rows, :] = total[:, start : start + 128].T
            start = 2 * quarter + pair * 128
            out_ref[1, rows, :] = total[:, start : start + 128].T
            start += quarter
            in_ref[1, 0, rows, :] = total[:, start : start + 128].T
            start += quarter
            out_ref[0, rows, :] = total[:, start : start + 128].T


def lay_out(core, arrays, quarter):
    columns = arrays[0].shape[0]
    outs = [((2, 3, 2 * quarter, columns), F32), ((2, 2 * quarter, columns), F32)]
    return call(lay_out_kernel, outs, arrays, [core])


def take(array, index, axis=0):
    return lax.dynamic_index_in_dim(array, index, axis, keepdims=False)


def tie(values, *others):
    return lax.optimization_barrier((values, others))[0]


def make_shards(mesh):
    dp_size = mesh.shape["dp"]
    bits = dp_size.bit_length() - 1

    def shards(
        hidden_in, memory, in_proj, in_bias, out_proj, ffn_up, ffn_up_bias, ffn_down, out_bias,
        norm_gain, norm_bias, out_grad, target_len, source_len, assignment,
    ):
        dp = lax.axis_index("dp")
        side = lax.axis_index("tensor")
        core = dp & 1
        core_one = core.reshape(1)
        bit = [(dp >> i) & 1 for i in range(bits)]
        model = norm_gain.shape[1]

        def over(array, i):
            return lax.ppermute(array, "dp", [(d, d ^ (1 << i)) for d in range(dp_size)])

        def across(array):
            return lax.ppermute(array, "tensor", [(0, 1), (1, 0)])

        def slot_swap(array):
            pairs = []
            for j in range(dp_size // 2):
                pairs += [(4 * j + 1, 4 * j + 2), (4 * j + 2, 4 * j + 1)]
            return jnp.where(core == side, array, lax.ppermute(array, ("dp", "tensor"), pairs))

        def whole_row(half):
            other = over(half, 0)
            return jnp.concatenate(
                [jnp.where(core == 0, half, other), jnp.where(core == 0, other, half)], axis=0
            )

        def half_of(array, index):
            return take(array.reshape(2, array.shape[0] // 2, -1), index)

        own_row = jnp.broadcast_to(assignment.reshape(1, 1).astype(F32), (8, 128))
        held = jnp.where(core == side, own_row, over(own_row, 0))[0, 0].astype(jnp.int32)
        row_ids = lax.iota(jnp.int32, target_len.shape[0])
        target_length = jnp.sum(jnp.where(row_ids == held, target_len, 0)).reshape(1)
        source_length = jnp.sum(jnp.where(row_ids == held, source_len, 0)).reshape(1)

        place = bit[1] + 2 * bit[2]
        where = jnp.stack([core, place])
        heads_q = in_proj.shape[2] // 2
        heads_p = heads_q // 4
        pairs = heads_q // 128
        ffn_q = ffn_up.shape[0] // 2
        ffn_p = ffn_q // 4

        def spot(quarter, size):
            return lambda c, p: c * quarter + p * size

        def pieces(sources, picks, quarter, size):
            moves = [
                (source, (lead, spot(quarter, size)), size, 0, ((kind,), 0))
                for kind, (source, lead) in enumerate(picks)
            ]
            return copy_rows(where, sources, [(len(picks), size, model)], moves, 60)[0]

        def hand_on(far):
            return far, over(far, 1), over(far, 2)

        def hand_last(got):
            cut = got[0].shape[0] // 2
            return got + (over(got[1][:cut], 2), over(got[2][cut:], 1))

        def there_moves(got, kind, out, size, dest):
            cut = got[0].shape[0] // 2
            moves = []
            for number in range(4):
                if number < 3:
                    source, lead = number, (kind,)
                elif kind < cut:
                    source, lead = 3, (kind,)
                else:
                    source, lead = 4, (kind - cut,)
                moves.append(
                    (source, (lead, 0), size, out, ((), lambda c, p, n=number: dest(p ^ n)))
                )
            return moves

        def pair_row(kinds, kind):
            return lambda head: ((head // 2) * kinds + kind) * 128 + (head % 2) * 64

        def near_pairs(layer, kinds, out):
            return [
                (0, ((layer, kind), lambda c, p, r=pair: c * heads_q + r * 128), 128, out,
                 ((), (pair * len(kinds) + number) * 128))
                for pair in range(pairs)
                for number, kind in enumerate(kinds)
            ]

        own_c = lambda c, p: c * heads_q
        near_c = lambda c, p: c * ffn_q

        first_piece = pieces(
            [in_proj, out_proj], [(0, (0, 0)), (0, (0, 1)), (0, (0, 2)), (1, (0,))], heads_q, heads_p
        )
        self_far = across(first_piece)
        in_late, out_late, up_late, down_late = tie((in_proj, out_proj, ffn_up, ffn_down), first_piece)
        second_piece = pieces(
            [in_late, out_late], [(0, (1, 0)), (0, (1, 1)), (0, (1, 2)), (1, (1,))], heads_q, heads_p
        )
        third_piece = pieces(
            list(tie((up_late, down_late), second_piece)), [(0, ()), (1, ())], ffn_q, ffn_p
        )
        wide = (3 * heads_q, model)
        slim = (heads_q, model)
        near_self, near_out_one = copy_rows(
            where,
            list(tie((in_late, out_late), third_piece)),
            [wide, slim],
            near_pairs(0, [0, 1, 2], 0) + [(1, ((0,), own_c), heads_q, 1, ((), 0))],
            60,
        )
        near_query, near_memory, near_out_two = copy_rows(
            where,
            list(tie((in_late, out_late), near_self)),
            [slim, (2 * heads_q, model), slim],
            [(0, ((1, 0), own_c), heads_q, 0, ((), 0))]
            + near_pairs(1, [1, 2], 1)
            + [(1, ((1,), own_c), heads_q, 2, ((), 0))],
            60,
        )
        def quarter(array, axis):
            size = array.shape[axis] // 2
            return lax.dynamic_slice_in_dim(array, core * size, size, axis)

        self_far, hidden_half = tie((self_far, slot_swap(tie(hidden_in, first_piece))), near_memory)
        self_got = hand_on(self_far)
        memory_half = slot_swap(tie(memory, hidden_half))
        cross_far = across(tie(second_piece, hidden_half))
        hidden_row = whole_row(hidden_half)
        self_got = hand_last(self_got)

        bias_near = jnp.concatenate([quarter(in_bias, 2).reshape(-1), quarter(ffn_up_bias, 0)])
        bias_far = across(bias_near)
        head_part = in_bias.shape[2] // 2
        bias_sides = [b[: 4 * head_part].reshape(2, 2, pairs, 128) for b in (bias_near, bias_far)]
        up_bias = [b[4 * head_part :].reshape(1, -1) for b in (bias_near, bias_far)]
        zero = jnp.zeros((pairs, 128), F32)
        self_bias = [jnp.stack([b[0, 0], zero, b[0, 1]], axis=1).reshape(1, -1) for b in bias_sides]
        query_bias = [b[1, 0].reshape(1, -1) for b in bias_sides]
        memory_bias = [jnp.stack([zero, b[1, 1]], axis=1).reshape(1, -1) for b in bias_sides]

        gains = [norm_gain[i : i + 1] for i in range(3)]
        shifts = [norm_bias[i : i + 1] for i in range(3)]

        def both_sides(lefts, rights, rows=None):
            if rows is not None:
                lefts = [lax.dynamic_slice_in_dim(a, *rows) for a in lefts]
            return (mm(lefts[0], rights[0]) + mm(lefts[1], rights[1])).astype(BF)

        def in_pieces(lefts, rights, start=0, count=2, size=512):
            return [both_sides(lefts, rights, (start + size * i, size)) for i in range(count)]

        def exchange(pieces):
            return [over(piece, 0) for piece in pieces]

        near_up, near_down = copy_rows(
            where,
            list(tie((up_late, down_late), hidden_row)),
            [(ffn_q, model)] * 2,
            [(i, ((), near_c), ffn_q, i, ((), 0)) for i in range(2)],
        )
        (rows_one,) = norm(gains[0], shifts[0], hidden_row)

        def self_side(weight, bias):
            joint = product([(rows_one, weight)], NT, bias)
            return ([joint], *attend([joint], target_length, True))

        one = [self_side(near_self, self_bias[0])]
        memory_half = tie(memory_half, one[0][1])
        memory_row = whole_row(memory_half)
        far_self, far_out_one = copy_rows(
            where,
            list(tie(self_got, one[0][1])),
            [wide, slim],
            [m for k in range(3) for m in there_moves(self_got, k, 0, heads_p, pair_row(3, k))]
            + there_moves(self_got, 3, 1, heads_p, lambda head: head * heads_p),
        )
        w_self = [near_self, far_self]
        cross_far = tie(cross_far, one[0][1])
        cross_got = hand_on(cross_far)
        ffn_far = across(tie(third_piece, cross_far))
        one.append(self_side(tie(far_self, cross_far), self_bias[1]))
        part = in_pieces(tie([s[1] for s in one], cross_got), [near_out_one, far_out_one])
        stream_one, rows_two = norm(
            gains[1], shifts[1], hidden_row, part, exchange(part), out_bias[0:1]
        )

        def cross_side(weight, bias, kv_weight, kv_bias):
            kv = product([(memory_row, kv_weight)], NT, kv_bias)
            query = product([(rows_two, weight)], NT, bias)
            return ([query, kv], *attend([query, kv], source_length, False))

        cross_got = hand_last(cross_got)
        two = [cross_side(near_query, query_bias[0], near_memory, memory_bias[0])]
        far_query, far_memory, far_out_two = copy_rows(
            where,
            list(tie(cross_got, two[0][1])),
            [slim, (2 * heads_q, model), slim],
            there_moves(cross_got, 0, 0, heads_p, lambda head: head * heads_p)
            + [m for k in range(2) for m in there_moves(cross_got, k + 1, 1, heads_p, pair_row(2, k))]
            + there_moves(cross_got, 3, 2, heads_p, lambda head: head * heads_p),
        )
        ffn_far = tie(ffn_far, two[0][1])
        ffn_got = hand_on(ffn_far)
        grad_half = slot_swap(tie(out_grad, ffn_far))
        two.append(cross_side(far_query, query_bias[1], far_memory, memory_bias[1]))
        grad_row = whole_row(tie(grad_half, two[1][1]))
        w_query = [near_query, far_query]
        w_memory = [near_memory, far_memory]
        w_out = [[near_out_one, near_out_two], [far_out_one, far_out_two]]
        part = in_pieces([s[1] for s in two], [near_out_two, far_out_two], 0, 4, 256)
        stream_two, rows_three = norm(
            gains[2], shifts[2], stream_one, part, exchange(part), out_bias[1:2]
        )

        sides = [ffn(rows_three, grad_row, near_up, near_down, up_bias[0])]
        ffn_got = hand_last(tie(ffn_got, rows_three))
        near_grads = [
            mm(grad_row, sides[0][0], TN).astype(BF), mm(rows_three, sides[0][1], TN).astype(BF)
        ]
        far_up, far_down = copy_rows(
            where,
            list(tie(ffn_got, near_grads)),
            [(ffn_q, model)] * 2,
            [m for k in range(2) for m in there_moves(ffn_got, k, k, ffn_p, lambda n: n * ffn_p)],
        )
        sides.append(ffn(rows_three, grad_row, far_up, far_down, up_bias[1]))
        w_up = [near_up, far_up]
        w_down = [near_down, far_down]
        active = [s[0] for s in sides]
        grad_pre = [s[1] for s in sides]

        unit = model // dp_size

        class Sum:
            def __init__(self, parts, left):
                self.parts, self.left, self.sent = parts, left, None

            def step(self, i, send_type=BF):
                low = unit << sum(1 for j in self.left if j < i)
                send, keep = split_step(self.parts, bit[i], low, send_type)
                self.left = [j for j in self.left if j != i]
                self.sent = send
                self.parts = [[keep, over(send, i)]]
                return self

            def after(self, *others):
                items = [item for part in self.parts for item in part]
                arrays = tie([i[0] if isinstance(i, tuple) else i for i in items], *others)
                whole = iter(
                    (a, *i[1:]) if isinstance(i, tuple) else a for a, i in zip(arrays, items)
                )
                self.parts = [[next(whole) for _ in part] for part in self.parts]
                return self

        def meet(totals, *arrays):
            lists = [[i[0] if isinstance(i, tuple) else i for p in t.parts for i in p] for t in totals]
            lists, arrays = lax.optimization_barrier((lists, arrays))
            for total, values in zip(totals, lists):
                values = iter(values)
                total.parts = [
                    [(next(values), *i[1:]) if isinstance(i, tuple) else next(values) for i in p]
                    for p in total.parts
                ]
            return arrays

        every = list(range(bits))

        def turn(total):
            keep, arrived = total.parts[0]
            half = keep.shape[1] // 2
            send = add_columns(keep, arrived, half, half)
            total.parts = [[(keep, 0, half), (arrived, 0, half), across(send)]]
            total.sent = send
            return total

        def joined(*totals):
            return Sum([part for total in totals for part in total.parts], totals[0].left)

        far_grads = [
            mm(grad_row, active[1], TN).astype(BF), mm(rows_three, grad_pre[1], TN).astype(BF)
        ]
        cut = near_grads[0].shape[1] // 4
        up_there = far_grads[1][:, : 3 * cut]
        by_y = Sum([[(g[0], 0, 3 * cut)] for g in (near_grads, far_grads)], every).step(1)
        by_z = Sum([[(g, 3, cut)] for g in (*near_grads, *far_grads)], every).step(2)
        part = in_pieces(tie(grad_pre, up_there, by_y.sent, by_z.sent), w_up)
        by_x = Sum([[(near_grads[1], 0, 3 * cut), across(up_there)]], every)
        part_far = exchange(part)
        half_rows = model // 2
        here_rows = (core * half_rows, half_rows)
        there_rows = ((1 - core) * half_rows, half_rows)
        hidden_send = both_sides(active, w_down, there_rows)
        hidden_own = both_sides(active, w_down, here_rows)
        grad_two, down_two, sums_three = norm_back(
            core_one, gains[2], part, part_far, stream_two, grad_row, True
        )

        def back_side(down, weight, kept, length, causal):
            arrays, mixed, sums = kept
            grad_mixed = mm(down, weight, NT).astype(BF)
            return attend_back(arrays, grad_mixed, mixed, sums, length, causal)

        two_back = [None, None]
        two_back[1] = back_side(
            tie(down_two, hidden_send), w_out[1][1], two[1], source_length, False
        )
        hidden_far = over(hidden_send, 0)
        two_back[1], hidden_far = meet([by_x, by_y, by_z], two_back[1], hidden_far)
        by_x.step(1)
        turn(by_y)
        sent = (by_x.sent, by_y.sent)
        two_back[0] = back_side(tie(down_two, sent), w_out[0][1], two[0], source_length, False)
        hidden_out = half_of(stream_two, core) + hidden_own.astype(F32)
        hidden_out = (hidden_out + hidden_far.astype(F32) + out_bias[2]).astype(BF)
        two_back[0], = meet([by_x, by_y], two_back[0])
        part = in_pieces([s[0] for s in two_back], w_query)
        part_far = exchange(part)
        first_sum = joined(by_x, by_y).step(2)
        by_z.step(1)
        kv_near, kv_there = (mm(memory_row, two_back[i][1], TN).astype(BF) for i in range(2))
        q_parts = [
            [mm(mat, array, TN).astype(BF) for mat, array in ((down_two, two[i][1]), (rows_two, two_back[i][0]))]
            for i in range(2)
        ]
        memory_send = both_sides([s[1] for s in two_back], w_memory, there_rows)
        memory_own = both_sides([s[1] for s in two_back], w_memory, here_rows)
        grad_one, down_one, sums_two = norm_back(
            core_one, gains[1], tie(part, first_sum.sent, by_z.sent), part_far, stream_one, grad_two, True
        )

        down_one, = meet([by_z], down_one)
        turn(by_z)
        for i in range(2):
            q_parts[i].append(mm(tie(down_one, by_z.sent), one[i][1], TN).astype(BF))
        q_sum = Sum([[array] for side_parts in q_parts for array in side_parts], every).step(1)
        sent = (by_z.sent, kv_there, q_sum.sent)
        one_back = [None, None]
        one_back[1] = back_side(tie(down_one, sent), w_out[1][0], one[1], target_length, True)
        kv_there = across(kv_there)
        self_there = mm(rows_one, one_back[1][0], TN).astype(BF)
        one_back[0] = back_side(
            tie(down_one, self_there), w_out[0][0], one[0], target_length, True
        )
        self_there = across(self_there)

        def last_steps(total, first):
            for i in range(first, bits):
                total.step(i)
            return total

        def by_core(total):
            mine, other = total.parts[0]
            return jnp.stack(
                [jnp.where(core == 0, mine, other), jnp.where(core == 0, other, mine)]
            )

        def laid_out(total, low, groups, kinds, width):
            part = total[:, :, low : low + groups * kinds * width]
            part = part.reshape(2, part.shape[1], groups, kinds, width)
            return jnp.transpose(part, (3, 0, 2, 4, 1)).reshape(kinds, 2 * groups * width, -1)

        def spread(near, far):
            width = near.shape[-1]
            out = jnp.zeros(near.shape[:-1] + (4, width), F32)
            axis = out.ndim - 2
            for part, half in ((near, side), (far, 1 - side)):
                out = lax.dynamic_update_slice_in_dim(
                    out, jnp.expand_dims(part, axis), half * 2 + core, axis
                )
            return out.reshape(near.shape[:-1] + (4 * width,))

        def bias_sums(columns):
            return jnp.swapaxes(columns[0].reshape(pairs, 2, 128), 0, 1).reshape(2, -1)

        here_back, kv_there = meet([first_sum, by_z], one_back[0][0], kv_there)
        first_sum = last_steps(joined(first_sum, by_z), 3)
        here_back, = meet([q_sum], tie(here_back, first_sum.sent))
        turn(q_sum)
        kv_sum = Sum([[kv_near, kv_there]], every).step(1)
        here_back = tie(here_back, q_sum.sent, kv_sum.sent)
        last_back = [here_back, one_back[1][0]]
        part_far = exchange(in_pieces(last_back, w_self, (1 - core) * half_rows, 1))
        self_here = mm(rows_one, last_back[0], TN).astype(BF)
        part = in_pieces(tie(last_back, self_here), w_self, core * half_rows, 1)
        _, hidden_low, sums_one = norm_back(
            core_one, gains[0], part, part_far, hidden_half, grad_one, False
        )

        in_bias_part = spread(
            *(
                jnp.stack([bias_sums(one_back[i][-1]), bias_sums(two_back[i][-1])])
                for i in range(2)
            )
        )
        up_bias_part = spread(sides[0][2][0], sides[1][2][0])
        dy_sum = jnp.sum(grad_half.astype(F32), axis=0)
        model_part = jnp.stack(
            [
                sums_two[0],
                sums_three[0],
                dy_sum,
                sums_one[1],
                sums_two[1],
                sums_three[1],
                sums_one[2],
                sums_two[2],
                sums_three[2],
            ]
        )
        sums = jnp.concatenate(
            [in_bias_part.reshape(-1, model), up_bias_part.reshape(-1, model), model_part]
        )
        sums, self_there, hidden_low = meet([kv_sum, q_sum, first_sum], sums, self_there, hidden_low)

        self_sum = Sum([[self_here, self_there]], every).step(1)
        cross_sum = joined(kv_sum, q_sum).step(2)
        hidden_far = slot_swap(hidden_low)
        first_sum.step(0, F32)
        memory_far = over(memory_send, 0)
        sums = sums + over(sums, 0)
        sums = sums + across(sums)
        far = over(sums, 1)
        sums, far, hidden_far, memory_far = meet(
            [self_sum, cross_sum, first_sum], sums, far, hidden_far, memory_far
        )

        self_sum.step(2)
        last_steps(cross_sum, 3)
        moved = (memory_own.astype(F32) + memory_far.astype(F32)).astype(BF)
        moved = slot_swap(tie(jnp.stack([moved, hidden_out]), self_sum.sent, cross_sum.sent))
        sums = sums + far
        far = over(sums, 2)
        sums, far, moved, hidden_far = meet([self_sum, cross_sum], sums, far, moved, hidden_far)

        last_steps(self_sum, 3)
        cross_sum.step(0, F32)
        hidden_grad, memory_grad, hidden_out = tie(
            (hidden_far.astype(F32), moved[0].astype(F32), moved[1]), self_sum.sent
        )
        sums = sums + far
        far = over(sums, 3)
        total = by_core(first_sum)
        near_cols = active[0].shape[1]
        cut = near_cols // 4
        up_total = jnp.concatenate([total[:, :, : 3 * cut], total[:, :, 7 * cut :]], axis=2)
        up_share = laid_out(up_total, 0, 1, 1, near_cols)[0]
        down_share = laid_out(total, 3 * cut, 1, 1, near_cols)[0]
        sums, far, *_ = meet(
            [self_sum, cross_sum], sums, far, hidden_grad, memory_grad, hidden_out, up_share, down_share
        )

        self_sum.step(0, F32)
        sums = sums + far
        for i in range(4, bits):
            sums = sums + over(sums, i)
        in_proj_grad, out_proj_grad = lay_out(
            core_one, [*self_sum.parts[0], *cross_sum.parts[0]], heads_q
        )
        in_bias_grad = sums[:4].reshape(2, 2, model)
        up_rows = up_bias_part.size // model
        ffn_up_bias_grad = sums[4 : 4 + up_rows].reshape(-1)
        out_bias_grad = sums[4 + up_rows : 7 + up_rows]
        norm_gain_grad = sums[7 + up_rows : 10 + up_rows]
        norm_bias_grad = sums[10 + up_rows : 13 + up_rows]
        return (
            hidden_out,
            hidden_grad,
            memory_grad,
            in_proj_grad,
            out_proj_grad,
            up_share,
            down_share,
            in_bias_grad,
            ffn_up_bias_grad,
            out_bias_grad,
            norm_gain_grad,
            norm_bias_grad,
        )

    return shards


def solution(mesh):
    return jax.shard_map(
        make_shards(mesh),
        mesh=mesh,
        in_specs=(
            P(("dp", "tensor"), None),
            P(("dp", "tensor"), None),
            P(None, None, "tensor", None),
            P(None, None, "tensor"),
            P(None, "tensor", None),
            P("tensor", None),
            P("tensor"),
            P("tensor", None),
            P(),
            P(),
            P(),
            P(("dp", "tensor"), None),
            P(),
            P(),
            P("dp"),
        ),
        out_specs=(
            P(("dp", "tensor"), None),
            P(("dp", "tensor"), None),
            P(("dp", "tensor"), None),
            P(None, None, "tensor", "dp"),
            P(None, "tensor", "dp"),
            P("tensor", "dp"),
            P("tensor", "dp"),
            P(),
            P(),
            P(),
            P(),
            P(),
        ),
        check_vma=False,
    )
```

```python
import functools

import jax
import jax.numpy as jnp
from jax import lax
from jax.experimental import pallas as pl
from jax.experimental.pallas import tpu as pltpu
from jax.sharding import PartitionSpec as P

HEAD_DIM = 64
F32 = jnp.float32
BF = jnp.bfloat16
NT = (((1,), (1,)), ((), ()))
TN = (((0,), (0,)), ((), ()))
NN = (((1,), (0,)), ((), ()))

epsilon = 1e-05
masked_score = -1e30
root_half = 0.7071067811865476
normal_peak = 0.3989422804014327
score_scale = HEAD_DIM ** (-0.5)


def mm(left, right, dims=NN):
    return lax.dot_general(left, right, dims, preferred_element_type=F32)


def three_parts(values):
    top = values.astype(BF).astype(F32)
    rest = values - top
    middle = rest.astype(BF).astype(F32)
    return top, middle, rest - middle


def attend_kernel(causal, step, joint, len_ref, *refs):
    for pair in range(refs[-1].shape[1] // 128):
        attend_pair(causal, step, joint, pair, len_ref, *refs)


def attend_pair(causal, step, joint, pair, len_ref, *refs):
    if joint:
        a_ref, o_ref, sum_ref = refs
        q, k, v = (a_ref[:, pair * 384 + i * 128 : pair * 384 + (i + 1) * 128] for i in range(3))
    else:
        q_ref, kv_ref, o_ref, sum_ref = refs
        q = q_ref[:, pair * 128 : (pair + 1) * 128]
        k, v = (kv_ref[:, pair * 256 + i * 128 : pair * 256 + (i + 1) * 128] for i in range(2))
    mine = slice(pair * 128, (pair + 1) * 128)
    length = len_ref[0]
    rows, keys = q.shape[0], k.shape[0]
    lane = lax.broadcasted_iota(jnp.int32, (1, 128), 1)
    key_pos = lax.broadcasted_iota(jnp.int32, (keys, 1), 0)
    bias = jnp.where(key_pos < length, 0.0, masked_score)
    q = q.astype(F32) * score_scale
    k = k.astype(F32)
    v = v.astype(F32)
    sides = []
    for head in range(2):
        own = (lane < 64) if head == 0 else (lane >= 64)
        first = lane == (64 if head == 0 else 0)
        q_wide = jnp.where(own, q, jnp.where(first, 1.0, 0.0)).astype(BF)
        k_wide = jnp.where(own, k, jnp.where(first, bias, 0.0)).astype(BF)
        v_wide = jnp.where(own, v, 1.0).astype(BF)
        sides.append((q_wide, k_wide, v_wide))
    tasks = [(block, head) for block in range(rows // step) for head in range(2)]

    def scores_of(block, head):
        reach = (block + 1) * step if causal else keys
        q_wide, k_wide, _ = sides[head]
        scores = mm(q_wide[block * step : (block + 1) * step], k_wide[:reach], NT)
        if causal:
            below = lax.broadcasted_iota(jnp.int32, (step, step), 1) <= lax.broadcasted_iota(
                jnp.int32, (step, step), 0
            )
            edge = jnp.where(below, scores[:, reach - step :], masked_score)
            if block == 0:
                scores = edge
            else:
                scores = jnp.concatenate([scores[:, : reach - step], edge], axis=1)
        return scores

    ahead = scores_of(*tasks[0])
    parts = []
    for number, (block, head) in enumerate(tasks):
        scores = ahead
        if number + 1 < len(tasks):
            ahead = scores_of(*tasks[number + 1])
        here = slice(block * step, (block + 1) * step)
        reach = scores.shape[1]
        top = jnp.max(scores, axis=1, keepdims=True)
        weights = jnp.exp(scores - top).astype(BF)
        mixed = mm(weights, sides[head][2][:reach])
        total = mixed[:, 64:65] if head == 0 else mixed[:, 0:1]
        parts.append((mixed / total, top + jnp.log(total)))
        if head == 1:
            o_ref[here, mine] = jnp.where(lane < 64, parts[0][0], parts[1][0]).astype(BF)
            sum_ref[here, mine] = jnp.where(lane < 64, parts[0][1], parts[1][1])
            parts = []


def attend_back_kernel(causal, step, joint, len_ref, *refs):
    for pair in range(refs[-2].shape[1] // 256):
        attend_back_pair(causal, step, joint, pair, len_ref, *refs)


def attend_back_pair(causal, step, joint, pair, len_ref, *refs):
    if joint:
        a_ref, g_ref, o_ref, sum_ref, da_ref, col_ref, acc_ref = refs
        q, k, v = (a_ref[:, pair * 384 + i * 128 : pair * 384 + (i + 1) * 128] for i in range(3))
        dq_ref, dk_ref, dv_ref = da_ref, da_ref, da_ref
        starts = [pair * 384 + i * 128 for i in range(3)]
    else:
        q_ref, kv_ref, g_ref, o_ref, sum_ref, dq_ref, dkv_ref, col_ref, acc_ref = refs
        q = q_ref[:, pair * 128 : (pair + 1) * 128]
        k, v = (kv_ref[:, pair * 256 + i * 128 : pair * 256 + (i + 1) * 128] for i in range(2))
        dk_ref, dv_ref = dkv_ref, dkv_ref
        starts = (pair * 128, pair * 256, pair * 256 + 128)
    mine = slice(pair * 128, (pair + 1) * 128)
    length = len_ref[0]
    rows, keys = q.shape[0], k.shape[0]
    lane = lax.broadcasted_iota(jnp.int32, (1, 128), 1)
    key_pos = lax.broadcasted_iota(jnp.int32, (keys, 1), 0)
    bias = jnp.where(key_pos < length, 0.0, masked_score)
    q = q.astype(F32) * score_scale
    k = k.astype(F32)
    v = v.astype(F32)
    g = g_ref[:, mine].astype(F32)
    overlap = g * o_ref[:, mine].astype(F32)
    log_sums = sum_ref[:, mine]
    sides = []
    for head in range(2):
        own = (lane < 64) if head == 0 else (lane >= 64)
        base = 64 if head == 0 else 0
        at = [lane == base + i for i in range(4)]
        minus = jnp.where(at[1] | at[2] | at[3], -1.0, 0.0)
        delta = jnp.sum(jnp.where(own, overlap, 0.0), axis=1, keepdims=True)
        log_sum = log_sums[:, 0:1] if head == 0 else log_sums[:, 64:65]
        s0, s1, s2 = three_parts(log_sum)
        d0, d1, d2 = three_parts(delta)
        extra_q = jnp.where(
            at[0], 1.0, jnp.where(at[1], s0, jnp.where(at[2], s1, jnp.where(at[3], s2, 0.0)))
        )
        extra_g = jnp.where(at[1], d0, jnp.where(at[2], d1, jnp.where(at[3], d2, 0.0)))
        q_wide = jnp.where(own, q, extra_q).astype(BF)
        k_wide = jnp.where(own, k, jnp.where(at[0], bias, minus)).astype(BF)
        g_wide = jnp.where(own, g, extra_g).astype(BF)
        v_wide = jnp.where(own, v, minus).astype(BF)
        sides.append((q_wide, k_wide, g_wide, v_wide))
    tasks = [(block, head) for block in range(keys // step) for head in range(2)]

    def products_of(block, head):
        here = slice(block * step, (block + 1) * step)
        low = block * step if causal else 0
        q_wide, k_wide, g_wide, v_wide = sides[head]
        scores = mm(k_wide[here], q_wide[low:], NT)
        if causal:
            below = lax.broadcasted_iota(jnp.int32, (step, step), 0) <= lax.broadcasted_iota(
                jnp.int32, (step, step), 1
            )
            edge = jnp.where(below, scores[:, :step], masked_score)
            if low + step == rows:
                scores = edge
            else:
                scores = jnp.concatenate([edge, scores[:, step:]], axis=1)
        return scores, mm(v_wide[here], g_wide[low:], NT)

    ahead = products_of(*tasks[0])
    dv_sum = jnp.zeros((1, 128), F32)
    dks = []
    dvs = []
    for number, (block, head) in enumerate(tasks):
        scores, change = ahead
        if number + 1 < len(tasks):
            ahead = products_of(*tasks[number + 1])
        here = slice(block * step, (block + 1) * step)
        low = block * step if causal else 0
        q_wide, k_wide, g_wide, v_wide = sides[head]
        probs = jnp.exp(scores)
        grads = (probs * change).astype(BF)
        dvs.append(mm(probs.astype(BF), g_wide[low:]))
        dks.append(mm(grads, q_wide[low:]))
        dq = mm(k_wide[here], grads, TN)
        if block == 0:
            acc_ref[head] = dq
        else:
            acc_ref[head, :, low:] += dq
        if head == 1:
            dv = jnp.where(lane < 64, dvs[0], dvs[1]).astype(BF)
            dv_sum = dv_sum + jnp.sum(dv.astype(F32), axis=0, keepdims=True)
            dv_ref[here, starts[2] : starts[2] + 128] = dv
            dk_ref[here, starts[1] : starts[1] + 128] = jnp.where(lane < 64, dks[0], dks[1]).astype(BF)
            dks = []
            dvs = []
    side_row = lax.broadcasted_iota(jnp.int32, (128, 1), 0)
    dq = (jnp.where(side_row < 64, acc_ref[0], acc_ref[1]) * score_scale).T.astype(BF)
    dq_ref[:, starts[0] : starts[0] + 128] = dq
    dq_sum = jnp.sum(dq.astype(F32), axis=0, keepdims=True)
    both = jnp.concatenate([dq_sum, dv_sum], axis=1)
    col_ref[:, pair * 256 : (pair + 1) * 256] = jnp.broadcast_to(both, (8, 256))


CHEAP = pl.CostEstimate(flops=1, bytes_accessed=1, transcendentals=0)


def call(kernel, outs, operands, scalars=(), scratch=()):
    vmem = pl.BlockSpec(memory_space=pltpu.VMEM)
    return pl.pallas_call(
        kernel,
        in_specs=[pl.BlockSpec(memory_space=pltpu.SMEM)] * len(scalars) + [vmem] * len(operands),
        out_specs=[vmem] * len(outs),
        out_shape=[jax.ShapeDtypeStruct(*out) for out in outs],
        scratch_shapes=list(scratch),
        compiler_params=pltpu.CompilerParams(vmem_limit_bytes=24 << 20),
        cost_estimate=CHEAP,
    )(*scalars, *operands)


def attend(arrays, length, causal):
    joint = len(arrays) == 1
    rows = arrays[0].shape[0]
    width = arrays[0].shape[1] // (3 if joint else 1)
    return call(
        functools.partial(attend_kernel, causal, min(512, rows), joint),
        [((rows, width), BF), ((rows, width), F32)],
        arrays,
        [length],
    )


def attend_back(arrays, grad, out, sums, length, causal):
    joint = len(arrays) == 1
    rows, width = out.shape
    return call(
        functools.partial(attend_back_kernel, causal, min(256 if causal else 512, rows), joint),
        [(a.shape, BF) for a in arrays] + [((8, 2 * width), F32)],
        [*arrays, grad, out, sums],
        [length],
        [pltpu.VMEM((2, 128, rows), F32)],
    )


def unit_of(values):
    centred = values - jnp.mean(values, axis=-1, keepdims=True)
    inverse = lax.rsqrt(jnp.mean(centred * centred, axis=-1, keepdims=True) + epsilon)
    return centred * inverse, inverse


def row_blocks(rows, block=256):
    block = min(block, rows)
    return [slice(start, start + block) for start in range(0, rows, block)]


def piece_sum(own_refs, far_refs, here):
    first = 0
    for own_ref, far_ref in zip(own_refs, far_refs):
        if here.start < first + own_ref.shape[0]:
            break
        first += own_ref.shape[0]
    part = slice(here.start - first, here.stop - first)
    return own_ref[part, :].astype(F32) + far_ref[part, :].astype(F32)


def norm_kernel(pieces, *refs):
    gain_ref, shift_ref, stream_ref = refs[:3]
    out_ref = refs[-1]
    for here in row_blocks(stream_ref.shape[0], 128):
        stream = stream_ref[here, :].astype(F32)
        if pieces:
            stream = stream + piece_sum(refs[3 : 3 + pieces], refs[3 + pieces : 3 + 2 * pieces], here)
            stream = stream + refs[3 + 2 * pieces][...]
            refs[-2][here, :] = stream
        unit, _ = unit_of(stream)
        out_ref[here, :] = (unit * gain_ref[...] + shift_ref[...]).astype(BF)


def norm(gain, shift, stream, own=(), far=(), bias=None):
    outs = ([(stream.shape, F32)] if own else []) + [(stream.shape, BF)]
    operands = [gain, shift, stream, *own, *far] + ([] if bias is None else [bias])
    return call(functools.partial(norm_kernel, len(own)), outs, operands)


def norm_back_kernel(pieces, whole_slot, core_ref, gain_ref, *refs):
    own_refs, far_refs = refs[:pieces], refs[pieces : 2 * pieces]
    stream_ref, down_ref, full_ref, low_ref, sum_ref = refs[2 * pieces :]
    rows = stream_ref.shape[0]
    blocks = row_blocks(rows)
    sum_ref[...] = jnp.zeros_like(sum_ref)
    for number, here in enumerate(blocks):
        grad = piece_sum(own_refs, far_refs, here)
        unit, inverse = unit_of(stream_ref[here, :].astype(F32))
        scaled = grad * gain_ref[...]
        if whole_slot:
            down = down_ref[here, :]
        else:
            size = here.stop - here.start
            down = down_ref[pl.ds(pl.multiple_of(core_ref[0] * rows + here.start, size), size), :]
        total = down.astype(F32) + inverse * (
            scaled
            - jnp.mean(scaled, axis=-1, keepdims=True)
            - unit * jnp.mean(scaled * unit, axis=-1, keepdims=True)
        )
        full_ref[here, :] = total
        low_ref[here, :] = total.astype(BF)

        def add(total=total, grad=grad, unit=unit):
            sum_ref[0:1, :] += jnp.sum(total, axis=0, keepdims=True)
            sum_ref[1:2, :] += jnp.sum(grad * unit, axis=0, keepdims=True)
            sum_ref[2:3, :] += jnp.sum(grad, axis=0, keepdims=True)

        if whole_slot:
            pl.when((2 * number) // len(blocks) == core_ref[0])(add)
        else:
            add()


def norm_back(core, gain, own, far, stream, down, whole_slot):
    return call(
        functools.partial(norm_back_kernel, len(own), whole_slot),
        [(stream.shape, F32), (stream.shape, BF), ((8, stream.shape[1]), F32)],
        [gain, *own, *far, stream, down],
        [core],
    )


def ffn_kernel(a_ref, g_ref, up_ref, down_ref, bias_ref, active_ref, grad_ref, sum_ref):
    hidden = up_ref.shape[0]
    block = min(512, hidden)

    def block_of(number, carry):
        units = pl.ds(pl.multiple_of(number * block, block), block)
        total = jnp.zeros((1, block), F32)
        for here in row_blocks(a_ref.shape[0], 512):
            values = mm(a_ref[here, :], up_ref[units, :], NT) + bias_ref[:, units]
            below = 0.5 * (1.0 + lax.erf(values * root_half))
            slope = below + values * jnp.exp(-0.5 * values * values) * normal_peak
            active_ref[here, units] = (values * below).astype(BF)
            grad = mm(g_ref[here, :], down_ref[units, :], NT).astype(BF).astype(F32)
            grad = (grad * slope).astype(BF)
            grad_ref[here, units] = grad
            total = total + jnp.sum(grad.astype(F32), axis=0, keepdims=True)
        sum_ref[:, units] = jnp.broadcast_to(total, (8, block))
        return carry

    lax.fori_loop(0, hidden // block, block_of, 0, unroll=True)


def ffn(rows_mat, grad_mat, up, down, bias):
    rows, hidden = rows_mat.shape[0], up.shape[0]
    return call(
        ffn_kernel,
        [((rows, hidden), BF), ((rows, hidden), BF), ((8, hidden), F32)],
        [rows_mat, grad_mat, up, down, bias],
    )


def product_kernel(count, dims, biased, first_ref, *refs):
    out_ref = refs[-1]
    rows, cols = out_ref.shape
    block = min(256, rows if dims == TN else cols)
    for start in range(0, rows if dims == TN else cols, block):
        here = slice(start, start + block)
        total = None
        for left_ref, right_ref in zip(refs[: 2 * count : 2], refs[1 : 2 * count : 2]):
            if dims == TN:
                left, right = left_ref[:, here], right_ref[...]
            else:
                left = left_ref[pl.ds(pl.multiple_of(first_ref[0], 128), rows), :]
                right = right_ref[here, :] if dims == NT else right_ref[:, here]
            term = mm(left, right, dims)
            total = term if total is None else total + term
        if biased:
            total = total + refs[2 * count][:, here]
        if dims == TN:
            out_ref[here, :] = total.astype(BF)
        else:
            out_ref[:, here] = total.astype(BF)


def product(terms, dims=NN, bias=None, span=None):
    left, right = terms[0]
    if span is None:
        span = (0, left.shape[1 if dims == TN else 0])
    cols = right.shape[0 if dims == NT else 1]
    operands = [array for term in terms for array in term] + ([] if bias is None else [bias])
    return call(
        functools.partial(product_kernel, len(terms), dims, bias is not None),
        [((span[1], cols), BF)],
        operands,
        [jnp.asarray(span[0], jnp.int32).reshape(1)],
    )[0]


def split_kernel(parts, low, bit_ref, *refs):
    send_ref, keep_ref = refs[-2:]
    first = bit_ref[0] == 0
    offset = 0
    at = 0
    for part in parts:
        width = part[0][1]
        here = slice(offset, offset + width)
        for block in range(keep_ref.shape[0] // low):
            rows = slice(2 * low * block, 2 * low * (block + 1))
            total = None
            for ref, (start, _) in zip(refs[at : at + len(part)], part):
                values = ref[rows, start : start + width].astype(F32)
                total = values if total is None else total + values
            upper, under = total[:low], total[low:]
            out = slice(low * block, low * (block + 1))
            keep_ref[out, here] = jnp.where(first, upper, under).astype(keep_ref.dtype)
            send_ref[out, here] = jnp.where(first, under, upper).astype(send_ref.dtype)
        at += len(part)
        offset += width


def split_step(parts, bit, low, send_type=BF):
    operands = []
    layout = []
    for part in parts:
        spans = []
        for item in part:
            array, block, width = item if isinstance(item, tuple) else (item, 0, item.shape[1])
            operands.append(array)
            spans.append((block * width, width))
        layout.append(spans)
    rows = operands[0].shape[0] // 2
    wide = sum(spans[0][1] for spans in layout)
    return call(
        functools.partial(split_kernel, layout, low),
        [((rows, wide), send_type), ((rows, wide), F32)],
        operands,
        [bit.reshape(1)],
    )


def copy_kernel(count, moves, scalar_ref, *refs):
    semaphore = refs[-1]
    copies = []
    for number, (source, start, rows, out, out_start) in enumerate(moves):
        ends = []
        for ref, (lead, row) in ((refs[source], start), (refs[count + out], out_start)):
            if callable(row):
                row = pl.multiple_of(row(scalar_ref[0], scalar_ref[1]), 64)
            ends.append(ref.at[(*lead, pl.ds(row, rows))])
        copies.append(pltpu.make_async_copy(*ends, semaphore.at[number]))
    for copy in copies:
        copy.start()
    for copy in copies:
        copy.wait()


def copy_rows(scalars, sources, shapes, moves, grant=24):
    return pl.pallas_call(
        functools.partial(copy_kernel, len(sources), moves),
        in_specs=[pl.BlockSpec(memory_space=pltpu.SMEM)]
        + [pl.BlockSpec(memory_space=pltpu.HBM)] * len(sources),
        out_specs=[pl.BlockSpec(memory_space=pltpu.VMEM)] * len(shapes),
        out_shape=[jax.ShapeDtypeStruct(shape, BF) for shape in shapes],
        scratch_shapes=[pltpu.SemaphoreType.DMA((len(moves),))],
        compiler_params=pltpu.CompilerParams(vmem_limit_bytes=grant << 20),
        cost_estimate=pl.CostEstimate(flops=1, bytes_accessed=1, transcendentals=0),
    )(scalars, *sources)


def add_kernel(start, one_ref, two_ref, out_ref):
    here = slice(start, start + out_ref.shape[1])
    out_ref[...] = (one_ref[:, here].astype(F32) + two_ref[:, here].astype(F32)).astype(BF)


def add_columns(one, two, start, width):
    out = ((one.shape[0], width), BF)
    return call(functools.partial(add_kernel, start), [out], [one, two])[0]


def lay_out_kernel(core_ref, self_ref, self_far_ref, cross_ref, cross_far_ref, in_ref, out_ref):
    pairs = self_ref.shape[1] // 384
    quarter = pairs * 128
    for part in range(2):
        mine = core_ref[0] == part
        total = jnp.where(mine, self_ref[...], self_far_ref[...])
        for pair in range(pairs):
            rows = slice(part * quarter + pair * 128, part * quarter + (pair + 1) * 128)
            for kind in range(3):
                start = (pair * 3 + kind) * 128
                in_ref[0, kind, rows, :] = total[:, start : start + 128].T
        total = jnp.where(mine, cross_ref[...], cross_far_ref[...])
        for pair in range(pairs):
            rows = slice(part * quarter + pair * 128, part * quarter + (pair + 1) * 128)
            for kind in range(2):
                start = (pair * 2 + kind) * 128
                in_ref[1, kind + 1, rows, :] = total[:, start : start + 128].T
            start = 2 * quarter + pair * 128
            out_ref[1, rows, :] = total[:, start : start + 128].T
            start += quarter
            in_ref[1, 0, rows, :] = total[:, start : start + 128].T
            start += quarter
            out_ref[0, rows, :] = total[:, start : start + 128].T


def lay_out(core, arrays, quarter):
    columns = arrays[0].shape[0]
    outs = [((2, 3, 2 * quarter, columns), F32), ((2, 2 * quarter, columns), F32)]
    return call(lay_out_kernel, outs, arrays, [core])


def take(array, index, axis=0):
    return lax.dynamic_index_in_dim(array, index, axis, keepdims=False)


def tie(values, *others):
    return lax.optimization_barrier((values, others))[0]


def make_shards(mesh):
    dp_size = mesh.shape["dp"]
    bits = dp_size.bit_length() - 1

    def shards(
        hidden_in, memory, in_proj, in_bias, out_proj, ffn_up, ffn_up_bias, ffn_down, out_bias,
        norm_gain, norm_bias, out_grad, target_len, source_len, assignment,
    ):
        dp = lax.axis_index("dp")
        side = lax.axis_index("tensor")
        core = dp & 1
        core_one = core.reshape(1)
        bit = [(dp >> i) & 1 for i in range(bits)]
        model = norm_gain.shape[1]

        def over(array, i):
            return lax.ppermute(array, "dp", [(d, d ^ (1 << i)) for d in range(dp_size)])

        def across(array):
            return lax.ppermute(array, "tensor", [(0, 1), (1, 0)])

        def slot_swap(array):
            pairs = []
            for j in range(dp_size // 2):
                pairs += [(4 * j + 1, 4 * j + 2), (4 * j + 2, 4 * j + 1)]
            return jnp.where(core == side, array, lax.ppermute(array, ("dp", "tensor"), pairs))

        def whole_row(half):
            other = over(half, 0)
            return jnp.concatenate(
                [jnp.where(core == 0, half, other), jnp.where(core == 0, other, half)], axis=0
            )

        def half_of(array, index):
            return take(array.reshape(2, array.shape[0] // 2, -1), index)

        own_row = jnp.broadcast_to(assignment.reshape(1, 1).astype(F32), (8, 128))
        held = jnp.where(core == side, own_row, over(own_row, 0))[0, 0].astype(jnp.int32)
        row_ids = lax.iota(jnp.int32, target_len.shape[0])
        target_length = jnp.sum(jnp.where(row_ids == held, target_len, 0)).reshape(1)
        source_length = jnp.sum(jnp.where(row_ids == held, source_len, 0)).reshape(1)

        place = bit[1] + 2 * bit[2]
        where = jnp.stack([core, place])
        heads_q = in_proj.shape[2] // 2
        heads_p = heads_q // 4
        pairs = heads_q // 128
        ffn_q = ffn_up.shape[0] // 2
        ffn_p = ffn_q // 4

        def spot(quarter, size):
            return lambda c, p: c * quarter + p * size

        def pieces(sources, picks, quarter, size):
            moves = [
                (source, (lead, spot(quarter, size)), size, 0, ((kind,), 0))
                for kind, (source, lead) in enumerate(picks)
            ]
            return copy_rows(where, sources, [(len(picks), size, model)], moves, 60)[0]

        def hand_on(far):
            return far, over(far, 1), over(far, 2)

        def hand_last(got, hops):
            if len(hops) == 1:
                return got + (over(got[1 if hops[0] == 2 else 2], hops[0]),)
            cut = got[0].shape[0] // 2
            return got + (over(got[1][:cut], 2), over(got[2][cut:], 1))

        def there_moves(got, kind, out, size, dest):
            cut = got[0].shape[0] // 2
            moves = []
            for number in range(4):
                if number < 3 or len(got) == 4:
                    source, lead = number, (kind,)
                elif kind < cut:
                    source, lead = 3, (kind,)
                else:
                    source, lead = 4, (kind - cut,)
                moves.append(
                    (source, (lead, 0), size, out, ((), lambda c, p, n=number: dest(p ^ n)))
                )
            return moves

        def pair_row(kinds, kind):
            return lambda head: ((head // 2) * kinds + kind) * 128 + (head % 2) * 64

        def near_pairs(layer, kinds, out):
            return [
                (0, ((layer, kind), lambda c, p, r=pair: c * heads_q + r * 128), 128, out,
                 ((), (pair * len(kinds) + number) * 128))
                for pair in range(pairs)
                for number, kind in enumerate(kinds)
            ]

        own_c = lambda c, p: c * heads_q
        near_c = lambda c, p: c * ffn_q

        first_piece = pieces(
            [in_proj, out_proj], [(0, (0, 0)), (0, (0, 1)), (0, (0, 2)), (1, (0,))], heads_q, heads_p
        )
        self_far = across(first_piece)
        in_late, out_late, up_late, down_late = tie((in_proj, out_proj, ffn_up, ffn_down), first_piece)
        second_piece = pieces(
            [in_late, out_late], [(0, (1, 0)), (0, (1, 1)), (0, (1, 2)), (1, (1,))], heads_q, heads_p
        )
        third_piece = pieces(
            list(tie((up_late, down_late), second_piece)), [(0, ()), (1, ())], ffn_q, ffn_p
        )
        wide = (3 * heads_q, model)
        slim = (heads_q, model)
        near_self, near_out_one = copy_rows(
            where,
            list(tie((in_late, out_late), third_piece)),
            [wide, slim],
            near_pairs(0, [0, 1, 2], 0) + [(1, ((0,), own_c), heads_q, 1, ((), 0))],
            60,
        )
        near_query, near_memory, near_out_two = copy_rows(
            where,
            list(tie((in_late, out_late), near_self)),
            [slim, (2 * heads_q, model), slim],
            [(0, ((1, 0), own_c), heads_q, 0, ((), 0))]
            + near_pairs(1, [1, 2], 1)
            + [(1, ((1,), own_c), heads_q, 2, ((), 0))],
            60,
        )
        def quarter(array, axis):
            size = array.shape[axis] // 2
            return lax.dynamic_slice_in_dim(array, core * size, size, axis)

        near_up, near_down = copy_rows(
            where,
            list(tie((up_late, down_late), near_query)),
            [(ffn_q, model)] * 2,
            [(i, ((), near_c), ffn_q, i, ((), 0)) for i in range(2)],
            60,
        )
        self_far, hidden_half = tie((self_far, slot_swap(tie(hidden_in, first_piece))), near_up)
        self_got = hand_on(self_far)
        memory_half = slot_swap(tie(memory, hidden_half))
        cross_far = across(tie(second_piece, hidden_half))
        hidden_row = whole_row(hidden_half)

        bias_near = jnp.concatenate([quarter(in_bias, 2).reshape(-1), quarter(ffn_up_bias, 0)])
        bias_far = across(bias_near)
        head_part = in_bias.shape[2] // 2
        bias_sides = [b[: 4 * head_part].reshape(2, 2, pairs, 128) for b in (bias_near, bias_far)]
        up_bias = [b[4 * head_part :].reshape(1, -1) for b in (bias_near, bias_far)]
        zero = jnp.zeros((pairs, 128), F32)
        self_bias = [jnp.stack([b[0, 0], zero, b[0, 1]], axis=1).reshape(1, -1) for b in bias_sides]
        query_bias = [b[1, 0].reshape(1, -1) for b in bias_sides]
        memory_bias = [jnp.stack([zero, b[1, 1]], axis=1).reshape(1, -1) for b in bias_sides]

        gains = [norm_gain[i : i + 1] for i in range(3)]
        shifts = [norm_bias[i : i + 1] for i in range(3)]

        def both_sides(lefts, rights, rows=None):
            if rows is not None:
                lefts = [lax.dynamic_slice_in_dim(a, *rows) for a in lefts]
            return (mm(lefts[0], rights[0]) + mm(lefts[1], rights[1])).astype(BF)

        def in_pieces(lefts, rights, shares=(4, 4)):
            terms = list(zip(lefts, rights))
            eighth = lefts[0].shape[0] // 8
            spans = [(eighth * sum(shares[:i]), eighth * share) for i, share in enumerate(shares)]
            return [product(terms, span=span) for span in spans]

        def exchange(pieces):
            return [over(piece, 0) for piece in pieces]

        (rows_one,) = norm(gains[0], shifts[0], hidden_row)

        joint = product([(rows_one, near_self)], NT, self_bias[0])
        self_got = hand_last(tie(self_got, joint), [1])
        one = [([joint], *attend([joint], target_length, True))]
        memory_half, cross_far = tie((memory_half, cross_far), one[0][1])
        memory_row = whole_row(memory_half)
        far_self, far_out_one = copy_rows(
            where,
            list(tie(self_got, one[0][1])),
            [wide, slim],
            [m for k in range(3) for m in there_moves(self_got, k, 0, heads_p, pair_row(3, k))]
            + there_moves(self_got, 3, 1, heads_p, lambda head: head * heads_p),
        )
        w_self = [near_self, far_self]
        cross_got = hand_on(cross_far)
        ffn_far = across(tie(third_piece, cross_far))
        joint = product([(rows_one, tie(far_self, cross_far, memory_half))], NT, self_bias[1])
        one.append(([joint], *attend([joint], target_length, True)))
        part = in_pieces(tie([s[1] for s in one], cross_got), [near_out_one, far_out_one], (3, 3, 2))
        stream_one, rows_two = norm(
            gains[1], shifts[1], hidden_row, part, exchange(part), out_bias[0:1]
        )

        def cross_side(weight, bias, kv_weight, kv_bias):
            kv = product([(memory_row, kv_weight)], NT, kv_bias)
            query = product([(rows_two, weight)], NT, bias)
            return ([query, kv], *attend([query, kv], source_length, False))

        rows_two, ffn_far = tie((rows_two, ffn_far), ffn_far, rows_two)
        cross_got = hand_last(tie(cross_got, rows_two), [2])
        ffn_got = hand_on(ffn_far)
        grad_half = slot_swap(tie(out_grad, ffn_far))
        two = [cross_side(near_query, query_bias[0], near_memory, memory_bias[0])]
        far_query, far_memory, far_out_two = copy_rows(
            where,
            list(tie(cross_got, two[0][1])),
            [slim, (2 * heads_q, model), slim],
            there_moves(cross_got, 0, 0, heads_p, lambda head: head * heads_p)
            + [m for k in range(2) for m in there_moves(cross_got, k + 1, 1, heads_p, pair_row(2, k))]
            + there_moves(cross_got, 3, 2, heads_p, lambda head: head * heads_p),
        )
        far_query, grad_half = tie((far_query, grad_half), grad_half, two[0][1])
        two.append(cross_side(far_query, query_bias[1], far_memory, memory_bias[1]))
        grad_row = whole_row(grad_half)
        w_query = [near_query, far_query]
        w_memory = [near_memory, far_memory]
        w_out = [[near_out_one, near_out_two], [far_out_one, far_out_two]]
        part = in_pieces(tie([s[1] for s in two], grad_row), [near_out_two, far_out_two], (3, 3, 2))
        stream_two, rows_three = norm(
            gains[2], shifts[2], stream_one, part, exchange(part), out_bias[1:2]
        )

        sides = [ffn(rows_three, grad_row, near_up, near_down, up_bias[0])]
        ffn_got = hand_last(tie(ffn_got, rows_three), [1, 2])
        near_grads = [
            mm(grad_row, sides[0][0], TN).astype(BF), mm(rows_three, sides[0][1], TN).astype(BF)
        ]
        far_up, far_down = copy_rows(
            where,
            list(tie(ffn_got, near_grads)),
            [(ffn_q, model)] * 2,
            [m for k in range(2) for m in there_moves(ffn_got, k, k, ffn_p, lambda n: n * ffn_p)],
        )
        sides.append(ffn(rows_three, grad_row, far_up, far_down, up_bias[1]))
        w_up = [near_up, far_up]
        w_down = [near_down, far_down]
        active = [s[0] for s in sides]
        grad_pre = [s[1] for s in sides]

        unit = model // dp_size

        class Sum:
            def __init__(self, parts, left):
                self.parts, self.left, self.sent = parts, left, None

            def step(self, i, send_type=BF):
                low = unit << sum(1 for j in self.left if j < i)
                send, keep = split_step(self.parts, bit[i], low, send_type)
                self.left = [j for j in self.left if j != i]
                self.sent = send
                self.parts = [[keep, over(send, i)]]
                return self

            def after(self, *others):
                items = [item for part in self.parts for item in part]
                arrays = tie([i[0] if isinstance(i, tuple) else i for i in items], *others)
                whole = iter(
                    (a, *i[1:]) if isinstance(i, tuple) else a for a, i in zip(arrays, items)
                )
                self.parts = [[next(whole) for _ in part] for part in self.parts]
                return self

        def meet(totals, *arrays):
            lists = [[i[0] if isinstance(i, tuple) else i for p in t.parts for i in p] for t in totals]
            lists, arrays = lax.optimization_barrier((lists, arrays))
            for total, values in zip(totals, lists):
                values = iter(values)
                total.parts = [
                    [(next(values), *i[1:]) if isinstance(i, tuple) else next(values) for i in p]
                    for p in total.parts
                ]
            return arrays

        every = list(range(bits))

        def turn(total):
            keep, arrived = total.parts[0]
            half = keep.shape[1] // 2
            send = add_columns(keep, arrived, half, half)
            total.parts = [[(keep, 0, half), (arrived, 0, half), across(send)]]
            total.sent = send
            return total

        def joined(*totals):
            return Sum([part for total in totals for part in total.parts], totals[0].left)

        far_grads = [
            mm(grad_row, active[1], TN).astype(BF), mm(rows_three, grad_pre[1], TN).astype(BF)
        ]
        cut = near_grads[0].shape[1] // 4
        up_there = far_grads[1][:, : 3 * cut]
        by_y = Sum([[(g[0], 0, 3 * cut)] for g in (near_grads, far_grads)], every).step(1)
        by_z = Sum([[(g, 3, cut)] for g in (*near_grads, *far_grads)], every).step(2)
        part = in_pieces(tie(grad_pre, up_there, by_y.sent, by_z.sent), w_up)
        by_x = Sum([[(near_grads[1], 0, 3 * cut), across(up_there)]], every)
        part_far = exchange(part)
        half_rows = model // 2
        here_rows = (core * half_rows, half_rows)
        there_rows = ((1 - core) * half_rows, half_rows)
        grad_two, down_two, sums_three = norm_back(
            core_one, gains[2], part, part_far, stream_two, grad_row, True
        )

        def back_side(down, weight, kept, length, causal):
            arrays, mixed, sums = kept
            grad_mixed = mm(down, weight, NT).astype(BF)
            return attend_back(arrays, grad_mixed, mixed, sums, length, causal)

        two_back = [None, None]
        two_back[1] = back_side(down_two, w_out[1][1], two[1], source_length, False)
        two_back[1], = meet([by_x, by_y, by_z], two_back[1])
        by_x.step(1)
        turn(by_y)
        sent = (by_x.sent, by_y.sent)
        two_back[0] = back_side(tie(down_two, sent), w_out[0][1], two[0], source_length, False)
        two_back[0], = meet([by_x, by_y], two_back[0])
        part = in_pieces([s[0] for s in two_back], w_query)
        part_far = exchange(part)
        first_sum = joined(by_x, by_y).step(2)
        by_z.step(1)
        kv_near, kv_there = (mm(memory_row, two_back[i][1], TN).astype(BF) for i in range(2))
        q_parts = [
            [mm(mat, array, TN).astype(BF) for mat, array in ((down_two, two[i][1]), (rows_two, two_back[i][0]))]
            for i in range(2)
        ]
        hidden_part = both_sides(tie(active, two_back[0][0]), w_down)
        hidden_send = half_of(hidden_part, 1 - core)
        hidden_own = half_of(hidden_part, core)
        memory_part = both_sides([s[1] for s in two_back], w_memory)
        memory_send = half_of(memory_part, 1 - core)
        memory_own = half_of(memory_part, core)
        grad_one, down_one, sums_two = norm_back(
            core_one, gains[1], tie(part, first_sum.sent, by_z.sent, hidden_part), part_far, stream_one, grad_two, True
        )

        down_one, = meet([by_z], down_one)
        turn(by_z)
        for i in range(2):
            q_parts[i].append(mm(tie(down_one, by_z.sent), one[i][1], TN).astype(BF))
        q_sum = Sum([[array] for side_parts in q_parts for array in side_parts], every).step(1)
        sent = (by_z.sent, kv_there, q_sum.sent)
        one_back = [None, None]
        one_back[1] = back_side(tie(down_one, sent), w_out[1][0], one[1], target_length, True)
        kv_there = across(kv_there)
        self_there = mm(rows_one, one_back[1][0], TN).astype(BF)
        one_back[0] = back_side(
            tie(down_one, self_there), w_out[0][0], one[0], target_length, True
        )
        self_there = across(self_there)

        def last_steps(total, first):
            for i in range(first, bits):
                total.step(i)
            return total

        def by_core(total):
            mine, other = total.parts[0]
            return jnp.stack(
                [jnp.where(core == 0, mine, other), jnp.where(core == 0, other, mine)]
            )

        def laid_out(total, low, groups, kinds, width):
            part = total[:, :, low : low + groups * kinds * width]
            part = part.reshape(2, part.shape[1], groups, kinds, width)
            return jnp.transpose(part, (3, 0, 2, 4, 1)).reshape(kinds, 2 * groups * width, -1)

        def spread(near, far):
            width = near.shape[-1]
            out = jnp.zeros(near.shape[:-1] + (4, width), F32)
            axis = out.ndim - 2
            for part, half in ((near, side), (far, 1 - side)):
                out = lax.dynamic_update_slice_in_dim(
                    out, jnp.expand_dims(part, axis), half * 2 + core, axis
                )
            return out.reshape(near.shape[:-1] + (4 * width,))

        def bias_sums(columns):
            return jnp.swapaxes(columns[0].reshape(pairs, 2, 128), 0, 1).reshape(2, -1)

        here_back, kv_there = meet([first_sum, by_z], one_back[0][0], kv_there)
        first_sum = last_steps(joined(first_sum, by_z), 3)
        here_back, = meet([q_sum], tie(here_back, first_sum.sent))
        turn(q_sum)
        kv_sum = Sum([[kv_near, kv_there]], every).step(1)
        here_back = tie(here_back, q_sum.sent, kv_sum.sent)
        last_back = [here_back, one_back[1][0]]
        part_far = exchange([both_sides(last_back, w_self, there_rows)])
        self_here = mm(rows_one, last_back[0], TN).astype(BF)
        part = [both_sides(tie(last_back, self_here), w_self, here_rows)]
        _, hidden_low, sums_one = norm_back(
            core_one, gains[0], part, part_far, hidden_half, grad_one, False
        )

        in_bias_part = spread(
            *(
                jnp.stack([bias_sums(one_back[i][-1]), bias_sums(two_back[i][-1])])
                for i in range(2)
            )
        )
        up_bias_part = spread(sides[0][2][0], sides[1][2][0])
        dy_sum = jnp.sum(grad_half.astype(F32), axis=0)
        model_part = jnp.stack(
            [
                sums_two[0],
                sums_three[0],
                dy_sum,
                sums_one[1],
                sums_two[1],
                sums_three[1],
                sums_one[2],
                sums_two[2],
                sums_three[2],
            ]
        )
        sums = jnp.concatenate(
            [in_bias_part.reshape(-1, model), up_bias_part.reshape(-1, model), model_part]
        )
        sums, self_there, hidden_low = meet(
            [kv_sum, q_sum, first_sum], sums, self_there, hidden_low
        )

        self_sum = Sum([[self_here, self_there]], every).step(1)
        cross_sum = joined(kv_sum, q_sum).step(2)
        hidden_far = slot_swap(hidden_low)
        first_sum.step(0, F32)
        memory_far, out_far = over(tie(jnp.stack([memory_send, hidden_send]), hidden_low), 0)
        sums = sums + over(sums, 0)
        sums = sums + across(sums)
        far = over(sums, 1)
        sums, far, hidden_far, memory_far, out_far = meet(
            [self_sum, cross_sum, first_sum], sums, far, hidden_far, memory_far, out_far
        )
        hidden_out = half_of(stream_two, core) + hidden_own.astype(F32)
        hidden_out = (hidden_out + out_far.astype(F32) + out_bias[2]).astype(BF)

        self_sum.step(2)
        last_steps(cross_sum, 3)
        moved = (memory_own.astype(F32) + memory_far.astype(F32)).astype(BF)
        moved = slot_swap(tie(jnp.stack([moved, hidden_out]), self_sum.sent, cross_sum.sent))
        sums = sums + far
        far = over(sums, 2)
        sums, far, moved, hidden_far = meet([self_sum, cross_sum], sums, far, moved, hidden_far)

        last_steps(self_sum, 3)
        cross_sum.after(self_sum.sent).step(0, F32)
        hidden_grad, memory_grad, hidden_out = tie(
            (hidden_far.astype(F32), moved[0].astype(F32), moved[1]), self_sum.sent
        )
        sums = sums + far
        far = over(sums, 3)
        total = by_core(first_sum)
        near_cols = active[0].shape[1]
        cut = near_cols // 4
        up_total = jnp.concatenate([total[:, :, : 3 * cut], total[:, :, 7 * cut :]], axis=2)
        up_share = laid_out(up_total, 0, 1, 1, near_cols)[0]
        down_share = laid_out(total, 3 * cut, 1, 1, near_cols)[0]
        sums, far, *_ = meet(
            [self_sum, cross_sum], sums, far, hidden_grad, memory_grad, hidden_out, up_share, down_share
        )

        self_sum.step(0, F32)
        sums = sums + far
        for i in range(4, bits):
            sums = sums + over(sums, i)
        in_proj_grad, out_proj_grad = lay_out(
            core_one, [*self_sum.parts[0], *cross_sum.parts[0]], heads_q
        )
        in_bias_grad = sums[:4].reshape(2, 2, model)
        up_rows = up_bias_part.size // model
        ffn_up_bias_grad = sums[4 : 4 + up_rows].reshape(-1)
        out_bias_grad = sums[4 + up_rows : 7 + up_rows]
        norm_gain_grad = sums[7 + up_rows : 10 + up_rows]
        norm_bias_grad = sums[10 + up_rows : 13 + up_rows]
        return (
            hidden_out,
            hidden_grad,
            memory_grad,
            in_proj_grad,
            out_proj_grad,
            up_share,
            down_share,
            in_bias_grad,
            ffn_up_bias_grad,
            out_bias_grad,
            norm_gain_grad,
            norm_bias_grad,
        )

    return shards


def solution(mesh):
    return jax.shard_map(
        make_shards(mesh),
        mesh=mesh,
        in_specs=(
            P(("dp", "tensor"), None),
            P(("dp", "tensor"), None),
            P(None, None, "tensor", None),
            P(None, None, "tensor"),
            P(None, "tensor", None),
            P("tensor", None),
            P("tensor"),
            P("tensor", None),
            P(),
            P(),
            P(),
            P(("dp", "tensor"), None),
            P(),
            P(),
            P("dp"),
        ),
        out_specs=(
            P(("dp", "tensor"), None),
            P(("dp", "tensor"), None),
            P(("dp", "tensor"), None),
            P(None, None, "tensor", "dp"),
            P(None, "tensor", "dp"),
            P("tensor", "dp"),
            P("tensor", "dp"),
            P(),
            P(),
            P(),
            P(),
            P(),
        ),
        check_vma=False,
    )
```

```python
import functools

import jax
import jax.numpy as jnp
from jax import lax
from jax.experimental import pallas as pl
from jax.experimental.pallas import tpu as pltpu
from jax.sharding import PartitionSpec as P

HEAD_DIM = 64
F32 = jnp.float32
BF = jnp.bfloat16
NT = (((1,), (1,)), ((), ()))
TN = (((0,), (0,)), ((), ()))
NN = (((1,), (0,)), ((), ()))

epsilon = 1e-05
masked_score = -1e30
root_half = 0.7071067811865476
normal_peak = 0.3989422804014327
score_scale = HEAD_DIM ** (-0.5)


def mm(left, right, dims=NN):
    return lax.dot_general(left, right, dims, preferred_element_type=F32)


def three_parts(values):
    top = values.astype(BF).astype(F32)
    rest = values - top
    middle = rest.astype(BF).astype(F32)
    return top, middle, rest - middle


def attend_kernel(causal, step, joint, len_ref, *refs):
    for pair in range(refs[-1].shape[1] // 128):
        attend_pair(causal, step, joint, pair, len_ref, *refs)


def attend_pair(causal, step, joint, pair, len_ref, *refs):
    if joint:
        a_ref, o_ref, sum_ref = refs
        q, k, v = (a_ref[:, pair * 384 + i * 128 : pair * 384 + (i + 1) * 128] for i in range(3))
    else:
        q_ref, kv_ref, o_ref, sum_ref = refs
        q = q_ref[:, pair * 128 : (pair + 1) * 128]
        k, v = (kv_ref[:, pair * 256 + i * 128 : pair * 256 + (i + 1) * 128] for i in range(2))
    mine = slice(pair * 128, (pair + 1) * 128)
    length = len_ref[0]
    rows, keys = q.shape[0], k.shape[0]
    lane = lax.broadcasted_iota(jnp.int32, (1, 128), 1)
    key_pos = lax.broadcasted_iota(jnp.int32, (keys, 1), 0)
    bias = jnp.where(key_pos < length, 0.0, masked_score)
    q = q.astype(F32) * score_scale
    k = k.astype(F32)
    v = v.astype(F32)
    sides = []
    for head in range(2):
        own = (lane < 64) if head == 0 else (lane >= 64)
        first = lane == (64 if head == 0 else 0)
        q_wide = jnp.where(own, q, jnp.where(first, 1.0, 0.0)).astype(BF)
        k_wide = jnp.where(own, k, jnp.where(first, bias, 0.0)).astype(BF)
        v_wide = jnp.where(own, v, 1.0).astype(BF)
        sides.append((q_wide, k_wide, v_wide))
    tasks = [(block, head) for block in range(rows // step) for head in range(2)]

    def scores_of(block, head):
        reach = (block + 1) * step if causal else keys
        q_wide, k_wide, _ = sides[head]
        scores = mm(q_wide[block * step : (block + 1) * step], k_wide[:reach], NT)
        if causal:
            below = lax.broadcasted_iota(jnp.int32, (step, step), 1) <= lax.broadcasted_iota(
                jnp.int32, (step, step), 0
            )
            edge = jnp.where(below, scores[:, reach - step :], masked_score)
            if block == 0:
                scores = edge
            else:
                scores = jnp.concatenate([scores[:, : reach - step], edge], axis=1)
        return scores

    ahead = scores_of(*tasks[0])
    parts = []
    for number, (block, head) in enumerate(tasks):
        scores = ahead
        if number + 1 < len(tasks):
            ahead = scores_of(*tasks[number + 1])
        here = slice(block * step, (block + 1) * step)
        reach = scores.shape[1]
        top = jnp.max(scores, axis=1, keepdims=True)
        weights = jnp.exp(scores - top).astype(BF)
        mixed = mm(weights, sides[head][2][:reach])
        total = mixed[:, 64:65] if head == 0 else mixed[:, 0:1]
        parts.append((mixed / total, top + jnp.log(total)))
        if head == 1:
            o_ref[here, mine] = jnp.where(lane < 64, parts[0][0], parts[1][0]).astype(BF)
            sum_ref[here, mine] = jnp.where(lane < 64, parts[0][1], parts[1][1])
            parts = []


def attend_back_kernel(causal, step, joint, len_ref, *refs):
    for pair in range(refs[-2].shape[1] // 256):
        attend_back_pair(causal, step, joint, pair, len_ref, *refs)


def attend_back_pair(causal, step, joint, pair, len_ref, *refs):
    if joint:
        a_ref, g_ref, o_ref, sum_ref, da_ref, col_ref, acc_ref = refs
        q, k, v = (a_ref[:, pair * 384 + i * 128 : pair * 384 + (i + 1) * 128] for i in range(3))
        dq_ref, dk_ref, dv_ref = da_ref, da_ref, da_ref
        starts = [pair * 384 + i * 128 for i in range(3)]
    else:
        q_ref, kv_ref, g_ref, o_ref, sum_ref, dq_ref, dkv_ref, col_ref, acc_ref = refs
        q = q_ref[:, pair * 128 : (pair + 1) * 128]
        k, v = (kv_ref[:, pair * 256 + i * 128 : pair * 256 + (i + 1) * 128] for i in range(2))
        dk_ref, dv_ref = dkv_ref, dkv_ref
        starts = (pair * 128, pair * 256, pair * 256 + 128)
    mine = slice(pair * 128, (pair + 1) * 128)
    length = len_ref[0]
    rows, keys = q.shape[0], k.shape[0]
    lane = lax.broadcasted_iota(jnp.int32, (1, 128), 1)
    key_pos = lax.broadcasted_iota(jnp.int32, (keys, 1), 0)
    bias = jnp.where(key_pos < length, 0.0, masked_score)
    q = q.astype(F32) * score_scale
    k = k.astype(F32)
    v = v.astype(F32)
    g = g_ref[:, mine].astype(F32)
    overlap = g * o_ref[:, mine].astype(F32)
    log_sums = sum_ref[:, mine]
    sides = []
    for head in range(2):
        own = (lane < 64) if head == 0 else (lane >= 64)
        base = 64 if head == 0 else 0
        at = [lane == base + i for i in range(4)]
        minus = jnp.where(at[1] | at[2] | at[3], -1.0, 0.0)
        delta = jnp.sum(jnp.where(own, overlap, 0.0), axis=1, keepdims=True)
        log_sum = log_sums[:, 0:1] if head == 0 else log_sums[:, 64:65]
        s0, s1, s2 = three_parts(log_sum)
        d0, d1, d2 = three_parts(delta)
        extra_q = jnp.where(
            at[0], 1.0, jnp.where(at[1], s0, jnp.where(at[2], s1, jnp.where(at[3], s2, 0.0)))
        )
        extra_g = jnp.where(at[1], d0, jnp.where(at[2], d1, jnp.where(at[3], d2, 0.0)))
        q_wide = jnp.where(own, q, extra_q).astype(BF)
        k_wide = jnp.where(own, k, jnp.where(at[0], bias, minus)).astype(BF)
        g_wide = jnp.where(own, g, extra_g).astype(BF)
        v_wide = jnp.where(own, v, minus).astype(BF)
        sides.append((q_wide, k_wide, g_wide, v_wide))
    tasks = [(block, head) for block in range(keys // step) for head in range(2)]

    def products_of(block, head):
        here = slice(block * step, (block + 1) * step)
        low = block * step if causal else 0
        q_wide, k_wide, g_wide, v_wide = sides[head]
        scores = mm(k_wide[here], q_wide[low:], NT)
        if causal:
            below = lax.broadcasted_iota(jnp.int32, (step, step), 0) <= lax.broadcasted_iota(
                jnp.int32, (step, step), 1
            )
            edge = jnp.where(below, scores[:, :step], masked_score)
            if low + step == rows:
                scores = edge
            else:
                scores = jnp.concatenate([edge, scores[:, step:]], axis=1)
        return scores, mm(v_wide[here], g_wide[low:], NT)

    ahead = products_of(*tasks[0])
    dv_sum = jnp.zeros((1, 128), F32)
    dks = []
    dvs = []
    for number, (block, head) in enumerate(tasks):
        scores, change = ahead
        if number + 1 < len(tasks):
            ahead = products_of(*tasks[number + 1])
        here = slice(block * step, (block + 1) * step)
        low = block * step if causal else 0
        q_wide, k_wide, g_wide, v_wide = sides[head]
        probs = jnp.exp(scores)
        grads = (probs * change).astype(BF)
        dvs.append(mm(probs.astype(BF), g_wide[low:]))
        dks.append(mm(grads, q_wide[low:]))
        dq = mm(k_wide[here], grads, TN)
        if block == 0:
            acc_ref[head] = dq
        else:
            acc_ref[head, :, low:] += dq
        if head == 1:
            dv = jnp.where(lane < 64, dvs[0], dvs[1]).astype(BF)
            dv_sum = dv_sum + jnp.sum(dv.astype(F32), axis=0, keepdims=True)
            dv_ref[here, starts[2] : starts[2] + 128] = dv
            dk_ref[here, starts[1] : starts[1] + 128] = jnp.where(lane < 64, dks[0], dks[1]).astype(BF)
            dks = []
            dvs = []
    side_row = lax.broadcasted_iota(jnp.int32, (128, 1), 0)
    dq = (jnp.where(side_row < 64, acc_ref[0], acc_ref[1]) * score_scale).T.astype(BF)
    dq_ref[:, starts[0] : starts[0] + 128] = dq
    dq_sum = jnp.sum(dq.astype(F32), axis=0, keepdims=True)
    both = jnp.concatenate([dq_sum, dv_sum], axis=1)
    col_ref[:, pair * 256 : (pair + 1) * 256] = jnp.broadcast_to(both, (8, 256))


CHEAP = pl.CostEstimate(flops=1, bytes_accessed=1, transcendentals=0)


def call(kernel, outs, operands, scalars=(), scratch=()):
    vmem = pl.BlockSpec(memory_space=pltpu.VMEM)
    return pl.pallas_call(
        kernel,
        in_specs=[pl.BlockSpec(memory_space=pltpu.SMEM)] * len(scalars) + [vmem] * len(operands),
        out_specs=[vmem] * len(outs),
        out_shape=[jax.ShapeDtypeStruct(*out) for out in outs],
        scratch_shapes=list(scratch),
        compiler_params=pltpu.CompilerParams(vmem_limit_bytes=24 << 20),
        cost_estimate=CHEAP,
    )(*scalars, *operands)


def attend(arrays, length, causal):
    joint = len(arrays) == 1
    rows = arrays[0].shape[0]
    width = arrays[0].shape[1] // (3 if joint else 1)
    return call(
        functools.partial(attend_kernel, causal, min(512, rows), joint),
        [((rows, width), BF), ((rows, width), F32)],
        arrays,
        [length],
    )


def attend_back(arrays, grad, out, sums, length, causal):
    joint = len(arrays) == 1
    rows, width = out.shape
    return call(
        functools.partial(attend_back_kernel, causal, min(256 if causal else 512, rows), joint),
        [(a.shape, BF) for a in arrays] + [((8, 2 * width), F32)],
        [*arrays, grad, out, sums],
        [length],
        [pltpu.VMEM((2, 128, rows), F32)],
    )


def unit_of(values):
    centred = values - jnp.mean(values, axis=-1, keepdims=True)
    inverse = lax.rsqrt(jnp.mean(centred * centred, axis=-1, keepdims=True) + epsilon)
    return centred * inverse, inverse


def row_blocks(rows, block=256):
    block = min(block, rows)
    return [slice(start, start + block) for start in range(0, rows, block)]


def piece_sum(own_refs, far_refs, here):
    first = 0
    for own_ref, far_ref in zip(own_refs, far_refs):
        if here.start < first + own_ref.shape[0]:
            break
        first += own_ref.shape[0]
    part = slice(here.start - first, here.stop - first)
    return own_ref[part, :].astype(F32) + far_ref[part, :].astype(F32)


def norm_kernel(pieces, *refs):
    gain_ref, shift_ref, stream_ref = refs[:3]
    out_ref = refs[-1]
    for here in row_blocks(stream_ref.shape[0], 128):
        stream = stream_ref[here, :].astype(F32)
        if pieces:
            stream = stream + piece_sum(refs[3 : 3 + pieces], refs[3 + pieces : 3 + 2 * pieces], here)
            stream = stream + refs[3 + 2 * pieces][...]
            refs[-2][here, :] = stream
        unit, _ = unit_of(stream)
        out_ref[here, :] = (unit * gain_ref[...] + shift_ref[...]).astype(BF)


def norm(gain, shift, stream, own=(), far=(), bias=None):
    outs = ([(stream.shape, F32)] if own else []) + [(stream.shape, BF)]
    operands = [gain, shift, stream, *own, *far] + ([] if bias is None else [bias])
    return call(functools.partial(norm_kernel, len(own)), outs, operands)


def norm_back_kernel(pieces, whole_slot, core_ref, gain_ref, *refs):
    own_refs, far_refs = refs[:pieces], refs[pieces : 2 * pieces]
    stream_ref, down_ref, full_ref, low_ref, sum_ref = refs[2 * pieces :]
    rows = stream_ref.shape[0]
    blocks = row_blocks(rows)
    sum_ref[...] = jnp.zeros_like(sum_ref)
    for number, here in enumerate(blocks):
        grad = piece_sum(own_refs, far_refs, here)
        unit, inverse = unit_of(stream_ref[here, :].astype(F32))
        scaled = grad * gain_ref[...]
        if whole_slot:
            down = down_ref[here, :]
        else:
            size = here.stop - here.start
            down = down_ref[pl.ds(pl.multiple_of(core_ref[0] * rows + here.start, size), size), :]
        total = down.astype(F32) + inverse * (
            scaled
            - jnp.mean(scaled, axis=-1, keepdims=True)
            - unit * jnp.mean(scaled * unit, axis=-1, keepdims=True)
        )
        full_ref[here, :] = total
        low_ref[here, :] = total.astype(BF)

        def add(total=total, grad=grad, unit=unit):
            sum_ref[0:1, :] += jnp.sum(total, axis=0, keepdims=True)
            sum_ref[1:2, :] += jnp.sum(grad * unit, axis=0, keepdims=True)
            sum_ref[2:3, :] += jnp.sum(grad, axis=0, keepdims=True)

        if whole_slot:
            pl.when((2 * number) // len(blocks) == core_ref[0])(add)
        else:
            add()


def norm_back(core, gain, own, far, stream, down, whole_slot):
    return call(
        functools.partial(norm_back_kernel, len(own), whole_slot),
        [(stream.shape, F32), (stream.shape, BF), ((8, stream.shape[1]), F32)],
        [gain, *own, *far, stream, down],
        [core],
    )


def ffn_kernel(a_ref, g_ref, up_ref, down_ref, bias_ref, active_ref, grad_ref, sum_ref):
    hidden = up_ref.shape[0]
    block = min(512, hidden)

    def block_of(number, carry):
        units = pl.ds(pl.multiple_of(number * block, block), block)
        total = jnp.zeros((1, block), F32)
        for here in row_blocks(a_ref.shape[0], 512):
            values = mm(a_ref[here, :], up_ref[units, :], NT) + bias_ref[:, units]
            below = 0.5 * (1.0 + lax.erf(values * root_half))
            slope = below + values * jnp.exp(-0.5 * values * values) * normal_peak
            active_ref[here, units] = (values * below).astype(BF)
            grad = mm(g_ref[here, :], down_ref[units, :], NT).astype(BF).astype(F32)
            grad = (grad * slope).astype(BF)
            grad_ref[here, units] = grad
            total = total + jnp.sum(grad.astype(F32), axis=0, keepdims=True)
        sum_ref[:, units] = jnp.broadcast_to(total, (8, block))
        return carry

    lax.fori_loop(0, hidden // block, block_of, 0, unroll=True)


def ffn(rows_mat, grad_mat, up, down, bias):
    rows, hidden = rows_mat.shape[0], up.shape[0]
    return call(
        ffn_kernel,
        [((rows, hidden), BF), ((rows, hidden), BF), ((8, hidden), F32)],
        [rows_mat, grad_mat, up, down, bias],
    )


def product_kernel(count, dims, biased, first_ref, *refs):
    out_ref = refs[-1]
    rows, cols = out_ref.shape
    block = min(256, rows if dims == TN else cols)
    for start in range(0, rows if dims == TN else cols, block):
        here = slice(start, start + block)
        total = None
        for left_ref, right_ref in zip(refs[: 2 * count : 2], refs[1 : 2 * count : 2]):
            if dims == TN:
                left, right = left_ref[:, here], right_ref[...]
            else:
                left = left_ref[pl.ds(pl.multiple_of(first_ref[0], 128), rows), :]
                right = right_ref[here, :] if dims == NT else right_ref[:, here]
            term = mm(left, right, dims)
            total = term if total is None else total + term
        if biased:
            total = total + refs[2 * count][:, here]
        if dims == TN:
            out_ref[here, :] = total.astype(BF)
        else:
            out_ref[:, here] = total.astype(BF)


def product(terms, dims=NN, bias=None, span=None):
    left, right = terms[0]
    if span is None:
        span = (0, left.shape[1 if dims == TN else 0])
    cols = right.shape[0 if dims == NT else 1]
    operands = [array for term in terms for array in term] + ([] if bias is None else [bias])
    return call(
        functools.partial(product_kernel, len(terms), dims, bias is not None),
        [((span[1], cols), BF)],
        operands,
        [jnp.asarray(span[0], jnp.int32).reshape(1)],
    )[0]


def split_kernel(parts, low, bit_ref, *refs):
    send_ref, keep_ref = refs[-2:]
    first = bit_ref[0] == 0
    offset = 0
    at = 0
    for part in parts:
        width = part[0][1]
        here = slice(offset, offset + width)
        for block in range(keep_ref.shape[0] // low):
            rows = slice(2 * low * block, 2 * low * (block + 1))
            total = None
            for ref, (start, _) in zip(refs[at : at + len(part)], part):
                values = ref[rows, start : start + width].astype(F32)
                total = values if total is None else total + values
            upper, under = total[:low], total[low:]
            out = slice(low * block, low * (block + 1))
            keep_ref[out, here] = jnp.where(first, upper, under).astype(keep_ref.dtype)
            send_ref[out, here] = jnp.where(first, under, upper).astype(send_ref.dtype)
        at += len(part)
        offset += width


def split_step(parts, bit, low, send_type=BF):
    operands = []
    layout = []
    for part in parts:
        spans = []
        for item in part:
            array, block, width = item if isinstance(item, tuple) else (item, 0, item.shape[1])
            operands.append(array)
            spans.append((block * width, width))
        layout.append(spans)
    rows = operands[0].shape[0] // 2
    wide = sum(spans[0][1] for spans in layout)
    return call(
        functools.partial(split_kernel, layout, low),
        [((rows, wide), send_type), ((rows, wide), F32)],
        operands,
        [bit.reshape(1)],
    )


def copy_kernel(count, moves, scalar_ref, *refs):
    semaphore = refs[-1]
    copies = []
    for number, (source, start, rows, out, out_start) in enumerate(moves):
        ends = []
        for ref, (lead, row) in ((refs[source], start), (refs[count + out], out_start)):
            if callable(row):
                row = pl.multiple_of(row(scalar_ref[0], scalar_ref[1]), 64)
            ends.append(ref.at[(*lead, pl.ds(row, rows))])
        copies.append(pltpu.make_async_copy(*ends, semaphore.at[number]))
    for copy in copies:
        copy.start()
    for copy in copies:
        copy.wait()


def copy_rows(scalars, sources, shapes, moves, grant=24):
    return pl.pallas_call(
        functools.partial(copy_kernel, len(sources), moves),
        in_specs=[pl.BlockSpec(memory_space=pltpu.SMEM)]
        + [pl.BlockSpec(memory_space=pltpu.HBM)] * len(sources),
        out_specs=[pl.BlockSpec(memory_space=pltpu.VMEM)] * len(shapes),
        out_shape=[jax.ShapeDtypeStruct(shape, BF) for shape in shapes],
        scratch_shapes=[pltpu.SemaphoreType.DMA((len(moves),))],
        compiler_params=pltpu.CompilerParams(vmem_limit_bytes=grant << 20),
        cost_estimate=pl.CostEstimate(flops=1, bytes_accessed=1, transcendentals=0),
    )(scalars, *sources)


def add_kernel(start, one_ref, two_ref, out_ref):
    here = slice(start, start + out_ref.shape[1])
    out_ref[...] = (one_ref[:, here].astype(F32) + two_ref[:, here].astype(F32)).astype(BF)


def add_columns(one, two, start, width):
    out = ((one.shape[0], width), BF)
    return call(functools.partial(add_kernel, start), [out], [one, two])[0]


def lay_out_kernel(core_ref, self_ref, self_far_ref, cross_ref, cross_far_ref, in_ref, out_ref):
    pairs = self_ref.shape[1] // 384
    quarter = pairs * 128
    for part in range(2):
        mine = core_ref[0] == part
        total = jnp.where(mine, self_ref[...], self_far_ref[...])
        for pair in range(pairs):
            rows = slice(part * quarter + pair * 128, part * quarter + (pair + 1) * 128)
            for kind in range(3):
                start = (pair * 3 + kind) * 128
                in_ref[0, kind, rows, :] = total[:, start : start + 128].T
        total = jnp.where(mine, cross_ref[...], cross_far_ref[...])
        for pair in range(pairs):
            rows = slice(part * quarter + pair * 128, part * quarter + (pair + 1) * 128)
            for kind in range(2):
                start = (pair * 2 + kind) * 128
                in_ref[1, kind + 1, rows, :] = total[:, start : start + 128].T
            start = 2 * quarter + pair * 128
            out_ref[1, rows, :] = total[:, start : start + 128].T
            start += quarter
            in_ref[1, 0, rows, :] = total[:, start : start + 128].T
            start += quarter
            out_ref[0, rows, :] = total[:, start : start + 128].T


def lay_out(core, arrays, quarter):
    columns = arrays[0].shape[0]
    outs = [((2, 3, 2 * quarter, columns), F32), ((2, 2 * quarter, columns), F32)]
    return call(lay_out_kernel, outs, arrays, [core])


def take(array, index, axis=0):
    return lax.dynamic_index_in_dim(array, index, axis, keepdims=False)


def tie(values, *others):
    return lax.optimization_barrier((values, others))[0]


def make_shards(mesh):
    dp_size = mesh.shape["dp"]
    bits = dp_size.bit_length() - 1

    def shards(
        hidden_in, memory, in_proj, in_bias, out_proj, ffn_up, ffn_up_bias, ffn_down, out_bias,
        norm_gain, norm_bias, out_grad, target_len, source_len, assignment,
    ):
        dp = lax.axis_index("dp")
        side = lax.axis_index("tensor")
        core = dp & 1
        core_one = core.reshape(1)
        bit = [(dp >> i) & 1 for i in range(bits)]
        model = norm_gain.shape[1]

        def over(array, i):
            return lax.ppermute(array, "dp", [(d, d ^ (1 << i)) for d in range(dp_size)])

        def across(array):
            return lax.ppermute(array, "tensor", [(0, 1), (1, 0)])

        def slot_swap(array):
            pairs = []
            for j in range(dp_size // 2):
                pairs += [(4 * j + 1, 4 * j + 2), (4 * j + 2, 4 * j + 1)]
            return jnp.where(core == side, array, lax.ppermute(array, ("dp", "tensor"), pairs))

        def whole_row(half):
            other = over(half, 0)
            return jnp.concatenate(
                [jnp.where(core == 0, half, other), jnp.where(core == 0, other, half)], axis=0
            )

        def half_of(array, index):
            return take(array.reshape(2, array.shape[0] // 2, -1), index)

        own_row = jnp.broadcast_to(assignment.reshape(1, 1).astype(F32), (8, 128))
        held = jnp.where(core == side, own_row, over(own_row, 0))[0, 0].astype(jnp.int32)
        row_ids = lax.iota(jnp.int32, target_len.shape[0])
        target_length = jnp.sum(jnp.where(row_ids == held, target_len, 0)).reshape(1)
        source_length = jnp.sum(jnp.where(row_ids == held, source_len, 0)).reshape(1)

        place = bit[1] + 2 * bit[2]
        where = jnp.stack([core, place])
        heads_q = in_proj.shape[2] // 2
        heads_p = heads_q // 4
        pairs = heads_q // 128
        ffn_q = ffn_up.shape[0] // 2
        ffn_p = ffn_q // 4

        def spot(quarter, size):
            return lambda c, p: c * quarter + p * size

        def pieces(sources, picks, quarter, size):
            moves = [
                (source, (lead, spot(quarter, size)), size, 0, ((kind,), 0))
                for kind, (source, lead) in enumerate(picks)
            ]
            return copy_rows(where, sources, [(len(picks), size, model)], moves, 60)[0]

        def hand_on(far):
            return far, over(far, 1), over(far, 2)

        def hand_last(got, hops):
            if len(hops) == 1:
                return got + (over(got[1 if hops[0] == 2 else 2], hops[0]),)
            cut = got[0].shape[0] // 2
            return got + (over(got[1][:cut], 2), over(got[2][cut:], 1))

        def there_moves(got, kind, out, size, dest):
            cut = got[0].shape[0] // 2
            moves = []
            for number in range(4):
                if number < 3 or len(got) == 4:
                    source, lead = number, (kind,)
                elif kind < cut:
                    source, lead = 3, (kind,)
                else:
                    source, lead = 4, (kind - cut,)
                moves.append(
                    (source, (lead, 0), size, out, ((), lambda c, p, n=number: dest(p ^ n)))
                )
            return moves

        def pair_row(kinds, kind):
            return lambda head: ((head // 2) * kinds + kind) * 128 + (head % 2) * 64

        def near_pairs(layer, kinds, out):
            return [
                (0, ((layer, kind), lambda c, p, r=pair: c * heads_q + r * 128), 128, out,
                 ((), (pair * len(kinds) + number) * 128))
                for pair in range(pairs)
                for number, kind in enumerate(kinds)
            ]

        own_c = lambda c, p: c * heads_q
        near_c = lambda c, p: c * ffn_q

        first_piece = pieces(
            [in_proj, out_proj], [(0, (0, 0)), (0, (0, 1)), (0, (0, 2)), (1, (0,))], heads_q, heads_p
        )
        self_far = across(first_piece)
        in_late, out_late, up_late, down_late = tie((in_proj, out_proj, ffn_up, ffn_down), first_piece)
        second_piece = pieces(
            [in_late, out_late], [(0, (1, 0)), (0, (1, 1)), (0, (1, 2)), (1, (1,))], heads_q, heads_p
        )
        third_piece = pieces(
            list(tie((up_late, down_late), second_piece)), [(0, ()), (1, ())], ffn_q, ffn_p
        )
        wide = (3 * heads_q, model)
        slim = (heads_q, model)
        near_self, near_out_one = copy_rows(
            where,
            list(tie((in_late, out_late), third_piece)),
            [wide, slim],
            near_pairs(0, [0, 1, 2], 0) + [(1, ((0,), own_c), heads_q, 1, ((), 0))],
            60,
        )
        near_query, near_memory, near_out_two = copy_rows(
            where,
            list(tie((in_late, out_late), near_self)),
            [slim, (2 * heads_q, model), slim],
            [(0, ((1, 0), own_c), heads_q, 0, ((), 0))]
            + near_pairs(1, [1, 2], 1)
            + [(1, ((1,), own_c), heads_q, 2, ((), 0))],
            60,
        )
        def quarter(array, axis):
            size = array.shape[axis] // 2
            return lax.dynamic_slice_in_dim(array, core * size, size, axis)

        near_up, near_down = copy_rows(
            where,
            list(tie((up_late, down_late), near_query)),
            [(ffn_q, model)] * 2,
            [(i, ((), near_c), ffn_q, i, ((), 0)) for i in range(2)],
            60,
        )
        self_far, hidden_half = tie((self_far, slot_swap(tie(hidden_in, first_piece))), near_up)
        self_got = hand_on(self_far)
        memory_half = slot_swap(tie(memory, hidden_half))
        cross_far = across(tie(second_piece, hidden_half))
        hidden_row = whole_row(hidden_half)

        bias_near = jnp.concatenate([quarter(in_bias, 2).reshape(-1), quarter(ffn_up_bias, 0)])
        bias_far = across(bias_near)
        head_part = in_bias.shape[2] // 2
        bias_sides = [b[: 4 * head_part].reshape(2, 2, pairs, 128) for b in (bias_near, bias_far)]
        up_bias = [b[4 * head_part :].reshape(1, -1) for b in (bias_near, bias_far)]
        zero = jnp.zeros((pairs, 128), F32)
        self_bias = [jnp.stack([b[0, 0], zero, b[0, 1]], axis=1).reshape(1, -1) for b in bias_sides]
        query_bias = [b[1, 0].reshape(1, -1) for b in bias_sides]
        memory_bias = [jnp.stack([zero, b[1, 1]], axis=1).reshape(1, -1) for b in bias_sides]

        gains = [norm_gain[i : i + 1] for i in range(3)]
        shifts = [norm_bias[i : i + 1] for i in range(3)]

        def both_sides(lefts, rights, rows=None):
            if rows is not None:
                lefts = [lax.dynamic_slice_in_dim(a, *rows) for a in lefts]
            return (mm(lefts[0], rights[0]) + mm(lefts[1], rights[1])).astype(BF)

        def in_pieces(lefts, rights, shares=(4, 4)):
            terms = list(zip(lefts, rights))
            eighth = lefts[0].shape[0] // 8
            spans = [(eighth * sum(shares[:i]), eighth * share) for i, share in enumerate(shares)]
            return [product(terms, span=span) for span in spans]

        def exchange(pieces):
            return [over(piece, 0) for piece in pieces]

        (rows_one,) = norm(gains[0], shifts[0], hidden_row)

        joint = product([(rows_one, near_self)], NT, self_bias[0])
        self_got = hand_last(tie(self_got, joint), [1])
        one = [([joint], *attend([joint], target_length, True))]
        memory_half, cross_far = tie((memory_half, cross_far), one[0][1])
        memory_row = whole_row(memory_half)
        far_self, far_out_one = copy_rows(
            where,
            list(tie(self_got, one[0][1])),
            [wide, slim],
            [m for k in range(3) for m in there_moves(self_got, k, 0, heads_p, pair_row(3, k))]
            + there_moves(self_got, 3, 1, heads_p, lambda head: head * heads_p),
        )
        w_self = [near_self, far_self]
        cross_got = hand_on(cross_far)
        ffn_far = across(tie(third_piece, cross_far))
        joint = product([(rows_one, tie(far_self, cross_far, memory_half))], NT, self_bias[1])
        one.append(([joint], *attend([joint], target_length, True)))
        part = in_pieces(tie([s[1] for s in one], cross_got), [near_out_one, far_out_one], (3, 3, 2))
        stream_one, rows_two = norm(
            gains[1], shifts[1], hidden_row, part, exchange(part), out_bias[0:1]
        )

        def cross_side(weight, bias, kv_weight, kv_bias):
            kv = product([(memory_row, kv_weight)], NT, kv_bias)
            query = product([(rows_two, weight)], NT, bias)
            return ([query, kv], *attend([query, kv], source_length, False))

        rows_two, ffn_far = tie((rows_two, ffn_far), ffn_far, rows_two)
        cross_got = hand_last(tie(cross_got, rows_two), [2])
        ffn_got = hand_on(ffn_far)
        grad_half = slot_swap(tie(out_grad, ffn_far))
        two = [cross_side(near_query, query_bias[0], near_memory, memory_bias[0])]
        far_query, far_memory, far_out_two = copy_rows(
            where,
            list(tie(cross_got, two[0][1])),
            [slim, (2 * heads_q, model), slim],
            there_moves(cross_got, 0, 0, heads_p, lambda head: head * heads_p)
            + [m for k in range(2) for m in there_moves(cross_got, k + 1, 1, heads_p, pair_row(2, k))]
            + there_moves(cross_got, 3, 2, heads_p, lambda head: head * heads_p),
        )
        far_query, grad_half = tie((far_query, grad_half), grad_half, two[0][1])
        two.append(cross_side(far_query, query_bias[1], far_memory, memory_bias[1]))
        grad_row = whole_row(grad_half)
        w_query = [near_query, far_query]
        w_memory = [near_memory, far_memory]
        w_out = [[near_out_one, near_out_two], [far_out_one, far_out_two]]
        part = in_pieces(tie([s[1] for s in two], grad_row), [near_out_two, far_out_two], (3, 3, 2))
        stream_two, rows_three = norm(
            gains[2], shifts[2], stream_one, part, exchange(part), out_bias[1:2]
        )

        sides = [ffn(rows_three, grad_row, near_up, near_down, up_bias[0])]
        ffn_got = hand_last(tie(ffn_got, rows_three), [1, 2])
        near_grads = [
            mm(grad_row, sides[0][0], TN).astype(BF), mm(rows_three, sides[0][1], TN).astype(BF)
        ]
        far_up, far_down = copy_rows(
            where,
            list(tie(ffn_got, near_grads)),
            [(ffn_q, model)] * 2,
            [m for k in range(2) for m in there_moves(ffn_got, k, k, ffn_p, lambda n: n * ffn_p)],
        )
        sides.append(ffn(rows_three, grad_row, far_up, far_down, up_bias[1]))
        w_up = [near_up, far_up]
        w_down = [near_down, far_down]
        active = [s[0] for s in sides]
        grad_pre = [s[1] for s in sides]

        unit = model // dp_size

        class Sum:
            def __init__(self, parts, left):
                self.parts, self.left, self.sent = parts, left, None

            def step(self, i, send_type=BF):
                low = unit << sum(1 for j in self.left if j < i)
                send, keep = split_step(self.parts, bit[i], low, send_type)
                self.left = [j for j in self.left if j != i]
                self.sent = send
                self.parts = [[keep, over(send, i)]]
                return self

            def after(self, *others):
                items = [item for part in self.parts for item in part]
                arrays = tie([i[0] if isinstance(i, tuple) else i for i in items], *others)
                whole = iter(
                    (a, *i[1:]) if isinstance(i, tuple) else a for a, i in zip(arrays, items)
                )
                self.parts = [[next(whole) for _ in part] for part in self.parts]
                return self

        def meet(totals, *arrays):
            lists = [[i[0] if isinstance(i, tuple) else i for p in t.parts for i in p] for t in totals]
            lists, arrays = lax.optimization_barrier((lists, arrays))
            for total, values in zip(totals, lists):
                values = iter(values)
                total.parts = [
                    [(next(values), *i[1:]) if isinstance(i, tuple) else next(values) for i in p]
                    for p in total.parts
                ]
            return arrays

        every = list(range(bits))

        def turn(total):
            keep, arrived = total.parts[0]
            half = keep.shape[1] // 2
            send = add_columns(keep, arrived, half, half)
            total.parts = [[(keep, 0, half), (arrived, 0, half), across(send)]]
            total.sent = send
            return total

        def joined(*totals):
            return Sum([part for total in totals for part in total.parts], totals[0].left)

        cut = near_grads[0].shape[1] // 4
        up_there, up_last = (
            mm(rows_three, part, TN).astype(BF)
            for part in (grad_pre[1][:, : 3 * cut], grad_pre[1][:, 3 * cut :])
        )
        far_grads = [mm(grad_row, active[1], TN).astype(BF), up_last]
        by_y = Sum([[(g[0], 0, 3 * cut)] for g in (near_grads, far_grads)], every).step(1)
        by_z = Sum([[(g, 3, cut)] for g in (*near_grads, far_grads[0])] + [[up_last]], every).step(2)
        part = in_pieces(tie(grad_pre, up_there, by_y.sent, by_z.sent), w_up)
        by_x = Sum([[(near_grads[1], 0, 3 * cut), across(up_there)]], every)
        part_far = exchange(part)
        half_rows = model // 2
        here_rows = (core * half_rows, half_rows)
        there_rows = ((1 - core) * half_rows, half_rows)
        grad_two, down_two, sums_three = norm_back(
            core_one, gains[2], part, part_far, stream_two, grad_row, True
        )

        def back_side(down, weight, kept, length, causal):
            arrays, mixed, sums = kept
            grad_mixed = mm(down, weight, NT).astype(BF)
            return attend_back(arrays, grad_mixed, mixed, sums, length, causal)

        two_back = [None, None]
        two_back[1] = back_side(down_two, w_out[1][1], two[1], source_length, False)
        two_back[1], = meet([by_x, by_y, by_z], two_back[1])
        by_x.step(1)
        turn(by_y)
        sent = (by_x.sent, by_y.sent)
        two_back[0] = back_side(tie(down_two, sent), w_out[0][1], two[0], source_length, False)
        two_back[0], = meet([by_x, by_y], two_back[0])
        part = in_pieces([s[0] for s in two_back], w_query)
        part_far = exchange(part)
        first_sum = joined(by_x, by_y).step(2)
        by_z.step(1)
        kv_near, kv_there = (mm(memory_row, two_back[i][1], TN).astype(BF) for i in range(2))
        q_parts = [
            [mm(mat, array, TN).astype(BF) for mat, array in ((down_two, two[i][1]), (rows_two, two_back[i][0]))]
            for i in range(2)
        ]
        hidden_part = both_sides(tie(active, two_back[0][0]), w_down)
        hidden_send = half_of(hidden_part, 1 - core)
        hidden_own = half_of(hidden_part, core)
        memory_part = both_sides([s[1] for s in two_back], w_memory)
        memory_send = half_of(memory_part, 1 - core)
        memory_own = half_of(memory_part, core)
        grad_one, down_one, sums_two = norm_back(
            core_one, gains[1], tie(part, first_sum.sent, by_z.sent, hidden_part), part_far, stream_one, grad_two, True
        )

        down_one, = meet([by_z], down_one)
        turn(by_z)
        for i in range(2):
            q_parts[i].append(mm(tie(down_one, by_z.sent), one[i][1], TN).astype(BF))
        q_sum = Sum([[array] for side_parts in q_parts for array in side_parts], every).step(1)
        sent = (by_z.sent, kv_there, q_sum.sent)
        one_back = [None, None]
        one_back[1] = back_side(tie(down_one, sent), w_out[1][0], one[1], target_length, True)
        kv_there = across(kv_there)
        self_there = mm(rows_one, one_back[1][0], TN).astype(BF)
        one_back[0] = back_side(
            tie(down_one, self_there), w_out[0][0], one[0], target_length, True
        )
        self_there = across(self_there)

        def last_steps(total, first):
            for i in range(first, bits):
                total.step(i)
            return total

        def by_core(total):
            mine, other = total.parts[0]
            return jnp.stack(
                [jnp.where(core == 0, mine, other), jnp.where(core == 0, other, mine)]
            )

        def laid_out(total, low, groups, kinds, width):
            part = total[:, :, low : low + groups * kinds * width]
            part = part.reshape(2, part.shape[1], groups, kinds, width)
            return jnp.transpose(part, (3, 0, 2, 4, 1)).reshape(kinds, 2 * groups * width, -1)

        def spread(near, far):
            width = near.shape[-1]
            out = jnp.zeros(near.shape[:-1] + (4, width), F32)
            axis = out.ndim - 2
            for part, half in ((near, side), (far, 1 - side)):
                out = lax.dynamic_update_slice_in_dim(
                    out, jnp.expand_dims(part, axis), half * 2 + core, axis
                )
            return out.reshape(near.shape[:-1] + (4 * width,))

        def bias_sums(columns):
            return jnp.swapaxes(columns[0].reshape(pairs, 2, 128), 0, 1).reshape(2, -1)

        here_back, kv_there = meet([first_sum, by_z], one_back[0][0], kv_there)
        first_sum = last_steps(joined(first_sum, by_z), 3)
        here_back, = meet([q_sum], tie(here_back, first_sum.sent))
        turn(q_sum)
        kv_sum = Sum([[kv_near, kv_there]], every).step(1)
        here_back = tie(here_back, q_sum.sent, kv_sum.sent)
        last_back = [here_back, one_back[1][0]]
        part_far = exchange([both_sides(last_back, w_self, there_rows)])
        self_here = mm(rows_one, last_back[0], TN).astype(BF)
        part = [both_sides(tie(last_back, self_here), w_self, here_rows)]
        _, hidden_low, sums_one = norm_back(
            core_one, gains[0], part, part_far, hidden_half, grad_one, False
        )

        in_bias_part = spread(
            *(
                jnp.stack([bias_sums(one_back[i][-1]), bias_sums(two_back[i][-1])])
                for i in range(2)
            )
        )
        up_bias_part = spread(sides[0][2][0], sides[1][2][0])
        dy_sum = jnp.sum(grad_half.astype(F32), axis=0)
        model_part = jnp.stack(
            [
                sums_two[0],
                sums_three[0],
                dy_sum,
                sums_one[1],
                sums_two[1],
                sums_three[1],
                sums_one[2],
                sums_two[2],
                sums_three[2],
            ]
        )
        sums = jnp.concatenate(
            [in_bias_part.reshape(-1, model), up_bias_part.reshape(-1, model), model_part]
        )
        sums, self_there, hidden_low = meet(
            [kv_sum, q_sum, first_sum], sums, self_there, hidden_low
        )

        self_sum = Sum([[self_here, self_there]], every).step(1)
        cross_sum = joined(kv_sum, q_sum).step(2)
        hidden_far = slot_swap(hidden_low)
        first_sum.step(0, F32)
        memory_far, out_far = over(tie(jnp.stack([memory_send, hidden_send]), hidden_low), 0)
        sums = sums + over(sums, 0)
        sums = sums + across(sums)
        far = over(sums, 1)
        sums, far, hidden_far, memory_far, out_far = meet(
            [self_sum, cross_sum, first_sum], sums, far, hidden_far, memory_far, out_far
        )
        hidden_out = half_of(stream_two, core) + hidden_own.astype(F32)
        hidden_out = (hidden_out + out_far.astype(F32) + out_bias[2]).astype(BF)

        self_sum.step(2)
        last_steps(cross_sum, 3)
        moved = (memory_own.astype(F32) + memory_far.astype(F32)).astype(BF)
        moved = slot_swap(tie(jnp.stack([moved, hidden_out]), self_sum.sent, cross_sum.sent))
        sums = sums + far
        far = over(sums, 2)
        sums, far, moved, hidden_far = meet([self_sum, cross_sum], sums, far, moved, hidden_far)

        last_steps(self_sum, 3)
        cross_sum.after(self_sum.sent).step(0, F32)
        hidden_grad, memory_grad, hidden_out = tie(
            (hidden_far.astype(F32), moved[0].astype(F32), moved[1]), self_sum.sent
        )
        sums = sums + far
        far = over(sums, 3)
        total = by_core(first_sum)
        near_cols = active[0].shape[1]
        cut = near_cols // 4
        up_total = jnp.concatenate([total[:, :, : 3 * cut], total[:, :, 7 * cut :]], axis=2)
        up_share = laid_out(up_total, 0, 1, 1, near_cols)[0]
        down_share = laid_out(total, 3 * cut, 1, 1, near_cols)[0]
        sums, far, *_ = meet(
            [self_sum, cross_sum], sums, far, hidden_grad, memory_grad, hidden_out, up_share, down_share
        )

        self_sum.step(0, F32)
        sums = sums + far
        for i in range(4, bits):
            sums = sums + over(sums, i)
        in_proj_grad, out_proj_grad = lay_out(
            core_one, [*self_sum.parts[0], *cross_sum.parts[0]], heads_q
        )
        in_bias_grad = sums[:4].reshape(2, 2, model)
        up_rows = up_bias_part.size // model
        ffn_up_bias_grad = sums[4 : 4 + up_rows].reshape(-1)
        out_bias_grad = sums[4 + up_rows : 7 + up_rows]
        norm_gain_grad = sums[7 + up_rows : 10 + up_rows]
        norm_bias_grad = sums[10 + up_rows : 13 + up_rows]
        return (
            hidden_out,
            hidden_grad,
            memory_grad,
            in_proj_grad,
            out_proj_grad,
            up_share,
            down_share,
            in_bias_grad,
            ffn_up_bias_grad,
            out_bias_grad,
            norm_gain_grad,
            norm_bias_grad,
        )

    return shards


def solution(mesh):
    return jax.shard_map(
        make_shards(mesh),
        mesh=mesh,
        in_specs=(
            P(("dp", "tensor"), None),
            P(("dp", "tensor"), None),
            P(None, None, "tensor", None),
            P(None, None, "tensor"),
            P(None, "tensor", None),
            P("tensor", None),
            P("tensor"),
            P("tensor", None),
            P(),
            P(),
            P(),
            P(("dp", "tensor"), None),
            P(),
            P(),
            P("dp"),
        ),
        out_specs=(
            P(("dp", "tensor"), None),
            P(("dp", "tensor"), None),
            P(("dp", "tensor"), None),
            P(None, None, "tensor", "dp"),
            P(None, "tensor", "dp"),
            P("tensor", "dp"),
            P("tensor", "dp"),
            P(),
            P(),
            P(),
            P(),
            P(),
        ),
        check_vma=False,
    )
```
